32 devices in a mesh: mem: 8 (over z, core), row: 4 (over y, x).
Axes of the slice: x: 2, y: 2, z: 4, core: 2. Of those that a mesh axis runs over, the one named last changes fastest.
Arguments:
- members: bfloat16 [16, 5, 64, 4096], P('mem', None, 'row'), may hold values from -6 to 6
- enc_first: bfloat16 [64, 5, 3, 3], replicated, may hold values from -0.875 to 0.875
- enc_second: bfloat16 [64, 64, 3, 3], replicated, may hold values from -0.25 to 0.25
- enc_third: bfloat16 [16, 64, 3, 3], replicated, may hold values from -0.25 to 0.25
- mix_weight: bfloat16 [32, 256], replicated, may hold values from -0.375 to 0.375
- dec_first: bfloat16 [32, 32, 4, 4], replicated, may hold values from -0.5 to 0.5
- dec_second: bfloat16 [16, 32, 4, 4], replicated, may hold values from -0.5 to 0.5
Outputs:
- output_field: bfloat16 [16, 64, 4096], P(None, 'row', 'mem')
The draws below stay inside these ranges and needn't reach their ends.
All inputs are finite; a program needn't handle non-finite values.
Results may differ from the reference program's by a relative error of at most 0.029.
Values may be sent and summed in bfloat16 or wider, within the bound.
No kernel may reach another device: no remote copies, remote signals or barrier semaphores. Data moves between devices by JAX's collectives and lax.ppermute only.
A program may use at most 128 MiB of HBM per device.

```python
import jax
import jax.numpy as jnp
from jax import lax

MEMBERS = 16
CH_IN = 5
CH_ENC = 64
CH_BOT = 16
CH_DEC = 32
LEVELS = 16
COLS = 4096
ROWS = 64


def block_levels(key, dims, split, least, largest):
    level = 1.0
    for position, parts in split:
        steps = jax.random.uniform(jax.random.fold_in(jax.random.fold_in(key, 6), position), (parts,), jnp.float32, least / len(split), largest / len(split))
        level = level * jnp.repeat(jnp.exp(steps), dims[position] // parts).reshape((-1,) + (1,) * (len(dims) - 1 - position))
    return level


def noise(key, dims, spread, reach, pieces=(), kind=jnp.bfloat16):
    result = spread * jax.random.normal(key, dims, jnp.float32)
    if pieces:
        result = result * block_levels(key, dims, pieces, -0.22, 0.18)
    return jnp.clip(result, -reach, reach).astype(kind)


def setup_inputs(seed: int = 0) -> dict:
    key_list = jax.random.split(jax.random.key(seed), 8)
    members = noise(key_list[0], (MEMBERS, CH_IN, ROWS, COLS), 1.0, 6.0, ((0, 8), (2, 4)))
    enc_first = noise(key_list[1], (CH_ENC, CH_IN, 3, 3), (CH_IN * 9) ** -0.5, 0.875)
    enc_second = noise(key_list[2], (CH_ENC, CH_ENC, 3, 3), (CH_ENC * 9) ** -0.5, 0.25)
    enc_third = noise(key_list[3], (CH_BOT, CH_ENC, 3, 3), (CH_ENC * 9) ** -0.5, 0.25)
    mix_weight = noise(key_list[4], (CH_DEC, MEMBERS * CH_BOT), (MEMBERS * CH_BOT) ** -0.5, 0.375)
    dec_first = noise(key_list[5], (CH_DEC, CH_DEC, 4, 4), (CH_DEC * 4) ** -0.5, 0.5)
    dec_second = noise(key_list[6], (LEVELS, CH_DEC, 4, 4), (CH_DEC * 4) ** -0.5, 0.5)
    return dict(members=members, enc_first=enc_first, enc_second=enc_second, enc_third=enc_third, mix_weight=mix_weight, dec_first=dec_first, dec_second=dec_second)


def convolve(source, weight, stride, padding, dilation):
    return lax.conv_general_dilated(source, weight, (stride, stride), padding, lhs_dilation=(dilation, dilation), dimension_numbers=("NCHW", "OIHW", "NCHW"), preferred_element_type=jnp.float32)


def reference(members, enc_first, enc_second, enc_third, mix_weight, dec_first, dec_second):
    def encode(member):
        hidden_one = jax.nn.silu(convolve(member[None], enc_first, 2, ((1, 1), (1, 1)), 1)).astype(jnp.bfloat16)
        hidden_two = jax.nn.silu(convolve(hidden_one, enc_second, 1, ((1, 1), (1, 1)), 1)).astype(jnp.bfloat16)
        bottleneck = jax.nn.silu(convolve(hidden_two, enc_third, 2, ((1, 1), (1, 1)), 1)).astype(jnp.bfloat16)
        return bottleneck[0]

    bottles = lax.map(encode, members)
    flattened = bottles.reshape(MEMBERS * CH_BOT, bottles.shape[2], bottles.shape[3])
    mixture = jnp.einsum("oc,chw->ohw", mix_weight.astype(jnp.float32), flattened.astype(jnp.float32), precision=lax.Precision.HIGHEST)
    latent = jax.nn.silu(mixture).astype(jnp.bfloat16)
    upsampled = jax.nn.silu(convolve(latent[None], dec_first, 1, ((2, 2), (2, 2)), 2)).astype(jnp.bfloat16)
    output_field = convolve(upsampled, dec_second, 1, ((2, 2), (2, 2)), 2)
    return output_field[0].astype(jnp.bfloat16)
```

```python
import functools

import jax
import jax.numpy as jnp
import numpy as np
from jax import lax
from jax.experimental import pallas as pl
from jax.experimental.pallas import tpu as pltpu
from jax.sharding import PartitionSpec as P

BF = jnp.bfloat16
F32 = jnp.float32
CH_BOT = 16
TAPS = 3
UP = 5
DOWN = 2


def dot(a, b):
    return lax.dot_general(a, b, (((1,), (0,)), ((), ())), preferred_element_type=F32)


def dot_t(a, b):
    return lax.dot_general(a, b, (((0,), (0,)), ((), ())), preferred_element_type=F32)


def silu_of_half(y):
    return y + y * jnp.tanh(y)


def spread(step, tile):
    one = np.zeros((step * tile, step * tile), np.float32)
    for q in range(step):
        for c in range(tile):
            one[step * c + q, q * tile + c] = 1
    return one


def first_selectors(members, channels, rows):
    own = np.zeros((3, 2, 48, 5 * channels * rows), np.float32)
    per = members * channels * (UP + DOWN)
    per = -(-per // 8) * 8
    total = -(-5 * per // 16) * 16
    halo = np.zeros((members, 4, 2, 48, total), np.float32)
    half = rows // 2
    for pc in range(2):
        for c in range(channels):
            for dr in range(3):
                for dc in range(3):
                    tap = (c * 3 + dr) * 3 + dc
                    ph = 2 * pc + dc
                    for kind, h in enumerate((1, 0, half)):
                        row = 2 * h + dr - 1
                        if 0 <= row < rows:
                            own[kind, pc, tap, (ph * channels + c) * rows + row] = 1
                    for m in range(members):
                        for kind, h in enumerate((-2, -1, 0, half)):
                            row = 2 * h + dr - 1
                            if row < 0:
                                at = (m * channels + c) * UP + row + UP
                            elif row >= rows:
                                at = members * channels * UP + (m * channels + c) * DOWN + row - rows
                            else:
                                continue
                            halo[m, kind, pc, tap, ph * per + at] = 1
    return own, halo, per, total


def shift_right(v):
    return jnp.concatenate([jnp.zeros_like(v[:, :1]), v[:, :-1]], axis=1)


def shift_left(v):
    return jnp.concatenate([v[:, 1:], jnp.zeros_like(v[:, :1])], axis=1)


def encoder_kernel(
    members, channels, rows, per,
    x_ref, down_ref, up_ref, w1_ref, w2_ref, w3_ref, mix_ref, own_ref, halo_ref, p_ref,
    out_ref, y_ref, yh_ref, w1_own, w1_halo, w2_big, w3_big, h1_ref, h2_ref, acc_ref,
):
    row_at = lax.axis_index("row")
    last = lax.axis_size("row") - 1
    half = rows // 2
    wide = x_ref.shape[1]
    tile = p_ref.shape[0] // 4
    tiles = wide // (4 * tile)
    cr = channels * rows
    spreader = p_ref[...]

    for t in range(tiles):
        z = dot(x_ref[:, 4 * tile * t : 4 * tile * (t + 1)], spreader).astype(BF)
        for q in range(4):
            for m in range(members):
                y_ref[m, (q + 1) * cr : (q + 2) * cr, t * tile : (t + 1) * tile] = z[
                    m * cr : (m + 1) * cr, q * tile : (q + 1) * tile
                ]
    for m in range(members):
        y_ref[m, 0:cr, :] = shift_right(y_ref[m, 4 * cr : 5 * cr, :])

    nd, nu = members * channels * UP, members * channels * DOWN
    yh_ref[...] = jnp.zeros_like(yh_ref)
    zd = dot(down_ref[...], spreader)
    zu = dot(up_ref[...], spreader)
    for t in range(tiles):
        for q in range(4):
            lanes = slice(t * tile, (t + 1) * tile)
            yh_ref[(q + 1) * per : (q + 1) * per + nd, lanes] = zd[t * nd : (t + 1) * nd, q * tile : (q + 1) * tile]
            yh_ref[(q + 1) * per + nd : (q + 1) * per + nd + nu, lanes] = zu[t * nu : (t + 1) * nu, q * tile : (q + 1) * tile]
    yh_ref[0:per, :] = shift_right(yh_ref[4 * per : 5 * per, :])
    yh = yh_ref[...].astype(BF)

    w1 = w1_ref[...]
    for kind in range(3):
        for pc in range(2):
            w1_own[kind, pc * 64 : (pc + 1) * 64, :] = (0.5 * dot_t(w1, own_ref[kind, pc])).astype(BF)
    for m in range(members):
        for kind in range(4):
            for pc in range(2):
                w1_halo[m, kind * 128 + pc * 64 : kind * 128 + (pc + 1) * 64, :] = (
                    0.5 * dot_t(w1, halo_ref[m, kind, pc])
                ).astype(BF)
    w2_big[...] = jnp.zeros_like(w2_big)
    for orow in range(2):
        for ocol in range(2):
            for dr in range(3):
                for dc in range(3):
                    w2_big[
                        (orow * 2 + ocol) * 64 : (orow * 2 + ocol + 1) * 64,
                        (orow + dr) * 256 + (ocol + dc) * 64 : (orow + dr) * 256 + (ocol + dc + 1) * 64,
                    ] = (0.5 * w2_ref[dr * 3 + dc].astype(F32)).astype(BF)
    w3_big[...] = jnp.zeros_like(w3_big)
    for dr, place, base in ((1, 0, 0), (2, 0, 128), (0, 2, 128)):
        for dc, shifted, at in ((1, 0, 0), (2, 0, 64), (0, 1, 64)):
            w3_big[(place + shifted) * 16 : (place + shifted + 1) * 16, base + at : base + at + 64] = (
                0.5 * w3_ref[dr * 3 + dc].astype(F32)
            ).astype(BF)

    def put_h1(m, h, value):
        v = value.astype(BF)
        even, odd = v[0:64], v[64:128]
        at = h + 2
        h1_ref[m, at, 64:128, :] = even
        h1_ref[m, at, 128:192, :] = odd
        h1_ref[m, at, 0:64, :] = shift_right(odd)
        h1_ref[m, at, 192:256, :] = shift_left(even)

    below = jnp.where(row_at == last, 0.0, 1.0).astype(F32)
    above = jnp.where(row_at == 0, 0.0, 1.0).astype(F32)
    for m in range(members):
        base = w1_own[0]
        for h in range(1, half):
            w = base if h == 1 else pltpu.roll(base.astype(F32), 2 * (h - 1), 1).astype(BF)
            put_h1(m, h, silu_of_half(dot(w, y_ref[m])))
        for kind, h in enumerate((-2, -1, 0, half)):
            v = dot(w1_halo[m, kind * 128 : (kind + 1) * 128, :], yh)
            if kind == 2:
                v = v + dot(w1_own[1], y_ref[m])
            if kind == 3:
                v = (v + dot(w1_own[2], y_ref[m])) * below
            put_h1(m, h, silu_of_half(v))

    def slab(m, first, count):
        return h1_ref[m, first + 2 : first + 2 + count].reshape(count * 256, wide // 4)

    for m in range(members):
        v = silu_of_half(dot(w2_big[0:128, 0:768], slab(m, -2, 3)) * above)
        h2_ref[m, 0:128, :] = v.astype(BF)
        for a in range(0, half, 2):
            v = silu_of_half(dot(w2_big[...], slab(m, a - 1, 4)))
            h2_ref[m, 128 * (a + 1) : 128 * (a + 3), :] = v.astype(BF)

    for m in range(members):
        carry = dot(w3_big[32:64, 128:256], h2_ref[m, 0:128, :])
        for r in range(half // 2):
            v = dot(w3_big[...], h2_ref[m, 128 * (2 * r + 1) : 128 * (2 * r + 3), :])
            w = v[0:32] + carry
            carry = v[32:64]
            acc_ref[r, m * 16 : (m + 1) * 16, :] = silu_of_half(w[0:16] + shift_right(w[16:32])).astype(BF)
    for r in range(half // 2):
        out_ref[r] = dot(mix_ref[...], acc_ref[r]).astype(BF)


def pack_kernel(members, channels, rows, x_ref, down_ref, up_ref, d_scr, u_scr):
    wide = x_ref.shape[1]
    lanes = down_ref.shape[1]
    nd, nu = members * channels * UP, members * channels * DOWN
    for t in range(wide // lanes):
        for g in range(members * channels):
            block = x_ref[g * rows : (g + 1) * rows, t * lanes : (t + 1) * lanes].astype(F32)
            d_scr[t * nd + g * UP : t * nd + (g + 1) * UP, :] = block[rows - UP : rows]
            u_scr[t * nu + g * DOWN : t * nu + (g + 1) * DOWN, :] = block[0:DOWN]
    down_ref[...] = d_scr[...].astype(BF)
    up_ref[...] = u_scr[...].astype(BF)


def decoder_kernel(nb, l_ref, w1_ref, w2_ref, p_ref, r_ref, out_ref, wd1, wd2, u_ref, g_ref):
    row_at, mem_at = lax.axis_index("row"), lax.axis_index("mem")
    row_last, mem_last = lax.axis_size("row") - 1, lax.axis_size("mem") - 1
    wide = l_ref.shape[2]
    rows = l_ref.shape[0] - 4
    wd1[...] = jnp.zeros_like(wd1)
    wd2[...] = jnp.zeros_like(wd2)
    for pr in range(2):
        for rr in range(3):
            tr = 2 * rr - pr
            if not 0 <= tr < 4:
                continue
            for pc in range(2):
                for cc in range(3):
                    tc = 2 * cc - pc
                    if not 0 <= tc < 4:
                        continue
                    wd1[(pr * 2 + pc) * 32 : (pr * 2 + pc + 1) * 32, (rr * 3 + cc) * 32 : (rr * 3 + cc + 1) * 32] = (
                        0.5 * w1_ref[tr * 4 + tc].astype(F32)
                    ).astype(BF)
                    for q in range(2):
                        at = pr * 4 + 2 * q + pc
                        to = rr * 4 + q + cc
                        wd2[at * 16 : (at + 1) * 16, to * 32 : (to + 1) * 32] = w2_ref[tr * 4 + tc]
    w1, w2 = wd1[...], wd2[...]
    left_lane = lax.broadcasted_iota(jnp.int32, (32, wide), 1)
    keep_left = jnp.where((left_lane == nb) & (mem_at == 0), 0.0, 1.0).astype(F32)
    keep_right = jnp.where((left_lane == nb + 1) & (mem_at == mem_last), 0.0, 1.0).astype(F32)
    for a in range(-1, rows + 1):
        v = silu_of_half(dot(w1, l_ref[a + 1 : a + 4].reshape(288, wide)))
        for pr in range(2):
            row = 2 * a + pr
            if not -1 <= row <= 2 * rows:
                continue
            even = v[pr * 64 : pr * 64 + 32] * keep_right
            odd = v[pr * 64 + 32 : pr * 64 + 64] * keep_left
            if row == -1:
                keep = jnp.where(row_at == 0, 0.0, 1.0).astype(F32)
                even, odd = even * keep, odd * keep
            if row == 2 * rows:
                keep = jnp.where(row_at == row_last, 0.0, 1.0).astype(F32)
                even, odd = even * keep, odd * keep
            before = jnp.concatenate([odd[:, nb : nb + 1], odd[:, 0 : nb - 1]], axis=1)
            after = jnp.concatenate([even[:, 1:nb], even[:, nb + 1 : nb + 2]], axis=1)
            at = (row + 1) * 128
            u_ref[at : at + 32, :] = before.astype(BF)
            u_ref[at + 32 : at + 64, :] = even[:, 0:nb].astype(BF)
            u_ref[at + 64 : at + 96, :] = odd[:, 0:nb].astype(BF)
            u_ref[at + 96 : at + 128, :] = after.astype(BF)
    for a in range(2 * rows):
        v = dot(w2, u_ref[a * 128 : (a + 3) * 128, :]).astype(BF)
        for pr in range(2):
            for ph in range(4):
                g_ref[(2 * a + pr) * 16 : (2 * a + pr + 1) * 16, ph * nb : (ph + 1) * nb] = v[
                    (pr * 4 + ph) * 16 : (pr * 4 + ph + 1) * 16
                ]
    g = dot(r_ref[...], g_ref[...]).astype(BF)
    out_ref[...] = dot(g, p_ref[...]).astype(BF).reshape(out_ref.shape)


def shifted(value, axis, by):
    peers = lax.axis_size(axis)
    return lax.ppermute(value, axis, [(i, i + by) for i in range(peers) if 0 <= i + by < peers])


def with_halo(cells, axis, dim):
    head = lax.slice_in_dim(cells, 0, 1, axis=dim)
    tail = lax.slice_in_dim(cells, cells.shape[dim] - 1, cells.shape[dim], axis=dim)
    return jnp.concatenate([shifted(tail, axis, 1), cells, shifted(head, axis, -1)], axis=dim)


VMEM = pl.BlockSpec(memory_space=pltpu.VMEM)


def per_device(members, enc_first, enc_second, enc_third, mix_weight, dec_first, dec_second):
    count, channels, rows, wide = members.shape
    own, halo, per, total = first_selectors(count, channels, rows)
    half, quarter = rows // 2, rows // 4
    cols = wide // 4
    tile = 128
    lanes = 4 * tile
    chunks = wide // lanes
    x = members.reshape(count * channels * rows, wide)
    nd, nu = count * channels * UP, count * channels * DOWN
    params = pltpu.CompilerParams(vmem_limit_bytes=56 * 2**20)
    down, up = pl.pallas_call(
        functools.partial(pack_kernel, count, channels, rows),
        out_shape=[jax.ShapeDtypeStruct((nd * chunks, lanes), BF), jax.ShapeDtypeStruct((nu * chunks, lanes), BF)],
        in_specs=[VMEM],
        out_specs=[VMEM, VMEM],
        scratch_shapes=[pltpu.VMEM((nd * chunks, lanes), F32), pltpu.VMEM((nu * chunks, lanes), F32)],
        compiler_params=params,
    )(x)
    down, up = shifted(down, "row", 1), shifted(up, "row", -1)
    w1 = jnp.pad(enc_first.transpose(1, 2, 3, 0).reshape(channels * 9, 64), ((0, 3), (0, 0)))
    w2 = enc_second.transpose(2, 3, 0, 1).reshape(9, 64, 64)
    w3 = enc_third.transpose(2, 3, 0, 1).reshape(9, 16, 64)
    mix = lax.dynamic_slice_in_dim(mix_weight, lax.axis_index("mem") * (count * CH_BOT), count * CH_BOT, 1)
    partial = pl.pallas_call(
        functools.partial(encoder_kernel, count, channels, rows, per),
        out_shape=jax.ShapeDtypeStruct((quarter, 32, cols), BF),
        in_specs=[VMEM] * 10,
        out_specs=VMEM,
        scratch_shapes=[
            pltpu.VMEM((count, 5 * channels * rows, cols), BF),
            pltpu.VMEM((total, cols), F32),
            pltpu.VMEM((3, 128, 5 * channels * rows), BF),
            pltpu.VMEM((count, 512, total), BF),
            pltpu.VMEM((256, 1024), BF),
            pltpu.VMEM((64, 256), BF),
            pltpu.VMEM((count, half + 3, 256, cols), BF),
            pltpu.VMEM((count, 128 * (half + 1), cols), BF),
            pltpu.VMEM((quarter, count * CH_BOT, cols), BF),
        ],
        compiler_params=params,
    )(x, down, up, w1, w2, w3, mix, jnp.asarray(own, BF), jnp.asarray(halo, BF), jnp.asarray(spread(4, tile), BF))

    peers = lax.axis_size("mem")
    nb = cols // peers
    sent = partial.reshape(quarter * 32, peers, nb).transpose(1, 0, 2)
    got = lax.all_to_all(sent, "mem", 0, 0)
    latent = jax.nn.silu(got.astype(F32).sum(0)).astype(BF).reshape(quarter, 32, nb)
    latent = with_halo(with_halo(latent, "mem", 2), "row", 0)
    latent = jnp.pad(latent, ((1, 1), (0, 0), (1, 1)))
    ext = -(-(nb + 2) // 128) * 128
    pieces = []
    for s in range(3):
        pieces.append(
            jnp.concatenate(
                [
                    latent[:, :, s + 1 : s + 1 + nb],
                    latent[:, :, s : s + 1],
                    latent[:, :, s + nb + 1 : s + nb + 2],
                    jnp.zeros((quarter + 4, 32, ext - nb - 2), BF),
                ],
                axis=2,
            )
        )
    spread_l = jnp.concatenate(pieces, axis=1)
    d1 = dec_first.transpose(2, 3, 0, 1).reshape(16, 32, 32)
    d2 = dec_second.transpose(2, 3, 0, 1).reshape(16, 16, 32)
    reorder = np.zeros((16 * rows, 16 * rows), np.float32)
    for r in range(rows):
        for level in range(16):
            reorder[level * rows + r, r * 16 + level] = 1
    return pl.pallas_call(
        functools.partial(decoder_kernel, nb),
        out_shape=jax.ShapeDtypeStruct((16, rows, 4 * nb), BF),
        in_specs=[VMEM] * 5,
        out_specs=VMEM,
        scratch_shapes=[
            pltpu.VMEM((128, 288), BF),
            pltpu.VMEM((128, 384), BF),
            pltpu.VMEM(((half + 2) * 128, nb), BF),
            pltpu.VMEM((16 * rows, 4 * nb), BF),
        ],
        compiler_params=params,
    )(spread_l, d1, d2, jnp.asarray(spread(4, nb).T, BF), jnp.asarray(reorder, BF))


def solution(mesh):
    placed = (P("mem", None, "row", None), P(), P(), P(), P(), P(), P())
    return jax.shard_map(
        per_device, mesh=mesh, in_specs=placed, out_specs=P(None, "row", "mem"), check_vma=False
    )
```

```python
import functools

import jax
import jax.numpy as jnp
import numpy as np
from jax import lax
from jax.experimental import pallas as pl
from jax.experimental.pallas import tpu as pltpu
from jax.sharding import PartitionSpec as P

BF = jnp.bfloat16
F32 = jnp.float32
CH_BOT = 16
UP = 5
DOWN = 2
TRANSPOSED = [(p, i, 2 * i - p) for p in range(2) for i in range(3) if 0 <= 2 * i - p < 4]


def dot(a, b):
    return lax.dot_general(a, b, (((1,), (0,)), ((), ())), preferred_element_type=F32)


def dot_t(a, b):
    return lax.dot_general(a, b, (((0,), (0,)), ((), ())), preferred_element_type=F32)


def silu_of_half(y):
    return y + y * jnp.tanh(y)


def spread(step, tile):
    one = np.zeros((step * tile, step * tile), np.float32)
    for q in range(step):
        for c in range(tile):
            one[step * c + q, q * tile + c] = 1
    return one


def padded(n, to):
    return -(-n // to) * to


def first_selectors(members, channels, rows):
    half = rows // 2
    own = np.zeros((3, 2, 48, 5 * channels * rows), np.float32)
    per = [padded(members * channels * n, 8) for n in (UP, DOWN)]
    total = [padded(5 * n, 16) for n in per]
    down = np.zeros((members, 3, 2, 48, total[0]), np.float32)
    up = np.zeros((members, 2, 48, total[1]), np.float32)
    for pc in range(2):
        for c in range(channels):
            for dr in range(3):
                for dc in range(3):
                    tap = (c * 3 + dr) * 3 + dc
                    ph = 2 * pc + dc
                    for kind, h in enumerate((1, 0, half)):
                        row = 2 * h + dr - 1
                        if 0 <= row < rows:
                            own[kind, pc, tap, (ph * channels + c) * rows + row] = 1
                    for m in range(members):
                        for kind, h in enumerate((-2, -1, 0)):
                            row = 2 * h + dr - 1
                            if row < 0:
                                down[m, kind, pc, tap, ph * per[0] + (m * channels + c) * UP + row + UP] = 1
                        row = 2 * half + dr - 1
                        if row >= rows:
                            up[m, pc, tap, ph * per[1] + (m * channels + c) * DOWN + row - rows] = 1
    return own, down, up, per, total


def shift_right(v):
    return jnp.concatenate([jnp.zeros_like(v[:, :1]), v[:, :-1]], axis=1)


def shift_left(v):
    return jnp.concatenate([v[:, 1:], jnp.zeros_like(v[:, :1])], axis=1)


def put_hidden(ref, m, at, value):
    v = value.astype(BF)
    even, odd = v[0:64], v[64:128]
    ref[m, at, 64:128, :] = even
    ref[m, at, 128:192, :] = odd
    ref[m, at, 0:64, :] = shift_right(odd)
    ref[m, at, 192:256, :] = shift_left(even)


def slab(ref, m, first, count):
    return ref[m, first : first + count].reshape(count * 256, ref.shape[3])


def place_halo(source, spreader, y_ref, count, per):
    tile = spreader.shape[0] // 4
    z = dot(source, spreader)
    y_ref[...] = jnp.zeros_like(y_ref)
    for t in range(y_ref.shape[1] // tile):
        for q in range(4):
            y_ref[(q + 1) * per : (q + 1) * per + count, t * tile : (t + 1) * tile] = z[
                t * count : (t + 1) * count, q * tile : (q + 1) * tile
            ]
    y_ref[0:per, :] = shift_right(y_ref[4 * per : 5 * per, :])
    return y_ref[...].astype(BF)


def pack_kernel(members, channels, rows, x_ref, down_ref, up_ref, d_scr, u_scr):
    wide = x_ref.shape[1]
    lanes = down_ref.shape[1]
    nd, nu = members * channels * UP, members * channels * DOWN
    for t in range(wide // lanes):
        for g in range(members * channels):
            block = x_ref[g * rows : (g + 1) * rows, t * lanes : (t + 1) * lanes].astype(F32)
            d_scr[t * nd + g * UP : t * nd + (g + 1) * UP, :] = block[rows - UP : rows]
            u_scr[t * nu + g * DOWN : t * nu + (g + 1) * DOWN, :] = block[0:DOWN]
    down_ref[...] = d_scr[...].astype(BF)
    up_ref[...] = u_scr[...].astype(BF)


def inner_kernel(
    members, channels, rows,
    x_ref, w1_ref, w2_ref, w3_ref, mix_ref, own_ref, down_ref, up_ref, p_ref, d1_ref, d2_ref,
    top_pre, low_pre, top_h1, low_h1, top_v, low_v, mixed_ref, w2_big, w3_big, w1_down, w1_up, wd1, wd2,
    y_ref, w1_own, h1_ref,
):
    half = rows // 2
    wide = x_ref.shape[1]
    tile = p_ref.shape[0] // 4
    cr = channels * rows
    spreader = p_ref[...]
    for t in range(wide // (4 * tile)):
        z = dot(x_ref[:, 4 * tile * t : 4 * tile * (t + 1)], spreader).astype(BF)
        for q in range(4):
            for m in range(members):
                y_ref[m, (q + 1) * cr : (q + 2) * cr, t * tile : (t + 1) * tile] = z[
                    m * cr : (m + 1) * cr, q * tile : (q + 1) * tile
                ]
    for m in range(members):
        y_ref[m, 0:cr, :] = shift_right(y_ref[m, 4 * cr : 5 * cr, :])

    w1 = w1_ref[...]
    for pc in range(2):
        lanes = slice(pc * 64, (pc + 1) * 64)
        for kind in range(3):
            w1_own[kind, lanes, :] = (0.5 * dot_t(w1, own_ref[kind, pc])).astype(BF)
        for m in range(members):
            for kind in range(3):
                w1_down[m, kind * 128 + pc * 64 : kind * 128 + (pc + 1) * 64, :] = (
                    0.5 * dot_t(w1, down_ref[m, kind, pc])
                ).astype(BF)
            w1_up[m, lanes, :] = (0.5 * dot_t(w1, up_ref[m, pc])).astype(BF)
    w2_big[...] = jnp.zeros_like(w2_big)
    for orow in range(2):
        for ocol in range(2):
            for dr in range(3):
                for dc in range(3):
                    w2_big[
                        (orow * 2 + ocol) * 64 : (orow * 2 + ocol + 1) * 64,
                        (orow + dr) * 256 + (ocol + dc) * 64 : (orow + dr) * 256 + (ocol + dc + 1) * 64,
                    ] = (0.5 * w2_ref[dr * 3 + dc].astype(F32)).astype(BF)
    w3_big[...] = jnp.zeros_like(w3_big)
    for dr, place, base in ((1, 0, 0), (2, 0, 128), (0, 2, 128)):
        for dc, shifted_out, at in ((1, 0, 0), (2, 0, 64), (0, 1, 64)):
            w3_big[(place + shifted_out) * 16 : (place + shifted_out + 1) * 16, base + at : base + at + 64] = (
                0.5 * w3_ref[dr * 3 + dc].astype(F32)
            ).astype(BF)
    wd1[...] = jnp.zeros_like(wd1)
    wd2[...] = jnp.zeros_like(wd2)
    for pr, rr, tr in TRANSPOSED:
        for pc, cc, tc in TRANSPOSED:
            wd1[(pr * 2 + pc) * 32 : (pr * 2 + pc + 1) * 32, (rr * 3 + cc) * 32 : (rr * 3 + cc + 1) * 32] = (
                0.5 * d1_ref[tr * 4 + tc].astype(F32)
            ).astype(BF)
            for q in range(2):
                at = pr * 4 + 2 * q + pc
                to = rr * 4 + q + cc
                wd2[at * 16 : (at + 1) * 16, to * 32 : (to + 1) * 32] = d2_ref[tr * 4 + tc]

    for m in range(members):
        base = w1_own[0]
        for h in range(1, half):
            w = base if h == 1 else pltpu.roll(base.astype(F32), 2 * (h - 1), 1).astype(BF)
            put_hidden(h1_ref, m, h - 1, silu_of_half(dot(w, y_ref[m])))
        top_pre[m] = dot(w1_own[1], y_ref[m])
        low_pre[m] = dot(w1_own[2], y_ref[m])
        top_h1[m] = h1_ref[m, 0:2]
        low_h1[m] = h1_ref[m, half - 4 : half - 1]

    mids = []
    for m in range(members):
        carry = None
        for a in range(2, half - 2, 2):
            h2 = silu_of_half(dot(w2_big[...], slab(h1_ref, m, a - 2, 4))).astype(BF)
            v = dot(w3_big[...], h2)
            if a == 2:
                top_v[m] = v[0:32]
            else:
                w = v[0:32] + carry
                mids.append((a // 2, m, silu_of_half(w[0:16] + shift_right(w[16:32])).astype(BF)))
            carry = v[32:64]
        low_v[m] = carry
    for r in range(2, half // 2 - 1):
        mixed_ref[r - 2] = dot(mix_ref[...], jnp.concatenate([b for s, _, b in mids if s == r], axis=0))


def low_kernel(
    members, channels, half, per,
    got_ref, p_ref, w1_ref, pre_ref, h1_in, w2_big, w3_big, v_ref, mix_ref, mixed_ref, y_ref, h1_ref,
):
    below = jnp.where(lax.axis_index("row") == lax.axis_size("row") - 1, 0.0, 1.0).astype(F32)
    y = place_halo(got_ref[...], p_ref[...], y_ref, members * channels * DOWN, per)
    parts = []
    for m in range(members):
        h1_ref[m, 0:3] = h1_in[m]
        put_hidden(h1_ref, m, 3, silu_of_half((dot(w1_ref[m], y) + pre_ref[m]) * below))
        h2 = silu_of_half(dot(w2_big[...], slab(h1_ref, m, 0, 4))).astype(BF)
        w = dot(w3_big[0:32], h2) + v_ref[m]
        parts.append(silu_of_half(w[0:16] + shift_right(w[16:32])).astype(BF))
    mixed_ref[...] = dot(mix_ref[...], jnp.concatenate(parts, axis=0))


def top_kernel(
    members, channels, half, per, nb,
    got_ref, p_ref, w1_ref, pre_ref, h1_in, w2_big, w3_big, v_ref, mix_ref, mid_ref, low_ref,
    keep_ref, send_ref, y_ref, h1_ref, mixed_ref,
):
    above = jnp.where(lax.axis_index("row") == 0, 0.0, 1.0).astype(F32)
    y = place_halo(got_ref[...], p_ref[...], y_ref, members * channels * UP, per)
    first, second = [], []
    for m in range(members):
        h1_ref[m, 3:5] = h1_in[m]
        fresh = dot(w1_ref[m], y)
        put_hidden(h1_ref, m, 0, silu_of_half(fresh[0:128]))
        put_hidden(h1_ref, m, 1, silu_of_half(fresh[128:256]))
        put_hidden(h1_ref, m, 2, silu_of_half(fresh[256:384] + pre_ref[m]))
        h2 = silu_of_half(dot(w2_big[0:128, 0:768], slab(h1_ref, m, 0, 3)) * above).astype(BF)
        carry = dot(w3_big[32:64, 128:256], h2)
        h2 = silu_of_half(dot(w2_big[...], slab(h1_ref, m, 1, 4))).astype(BF)
        v = dot(w3_big[...], h2)
        w = v[0:32] + carry
        first.append(silu_of_half(w[0:16] + shift_right(w[16:32])).astype(BF))
        w = v[32:64] + v_ref[m]
        second.append(silu_of_half(w[0:16] + shift_right(w[16:32])).astype(BF))
    cols = y_ref.shape[1]
    quarter = half // 2
    margin = jnp.zeros((quarter * 32, 128), F32)
    mixed_ref[:, 0:128] = margin
    mixed_ref[:, 128 + cols : 256 + cols] = margin
    mixed_ref[0:32, 128 : 128 + cols] = dot(mix_ref[...], jnp.concatenate(first, axis=0))
    mixed_ref[32:64, 128 : 128 + cols] = dot(mix_ref[...], jnp.concatenate(second, axis=0))
    for r in range(2, quarter - 1):
        mixed_ref[r * 32 : (r + 1) * 32, 128 : 128 + cols] = mid_ref[r - 2]
    mixed_ref[(quarter - 1) * 32 : quarter * 32, 128 : 128 + cols] = low_ref[...]

    me = lax.axis_index("mem")
    slots = lax.axis_size("mem") // 2
    tall = quarter * 32
    def lanes_from(lane):
        base = pl.multiple_of(lane // 128 * 128, 128)
        v = mixed_ref[:, pl.ds(base, 128)]
        return v if nb % 128 == 0 else pltpu.roll(v, (128 - lane % 128) % 128, 1)

    lane_at = lax.broadcasted_iota(jnp.int32, (tall, 128), 1)
    edges = jnp.zeros((tall, 128), F32)
    for side, ref in enumerate((keep_ref, send_ref)):
        for k in range(slots):
            block = me ^ (2 * k + side)
            start = 128 + block * nb
            ref[k, 0:tall, :] = lanes_from(start).astype(BF)
            if nb % 128 == 0:
                left = mixed_ref[:, pl.ds(pl.multiple_of(start - 128, 128), 128)][:, 127:128]
            else:
                left = lanes_from(start - 1)[:, 0:1]
            right = lanes_from(start + nb)[:, 0:1]
            at = 2 * (side * slots + k)
            edges = jnp.where(lane_at == at, left, edges)
            edges = jnp.where(lane_at == at + 1, right, edges)
    turned = edges.T
    for side, ref in enumerate((keep_ref, send_ref)):
        for k in range(slots):
            at = 2 * (side * slots + k)
            ref[k, tall : tall + 16, :] = jnp.concatenate(
                [turned[at : at + 2], jnp.zeros((14, 128), F32)], axis=0
            ).astype(BF)


def pair_kernel(keep_ref, got_ref, own_ref, *out_refs):
    own_ref[...] = keep_ref[0].astype(F32) + got_ref[0].astype(F32)
    for k, ref in enumerate(out_refs):
        ref[...] = (keep_ref[k + 1].astype(F32) + got_ref[k + 1].astype(F32)).astype(BF)


def latent_kernel(nb, quarter, own_ref, *refs):
    ext_ref, top_ref, low_ref = refs[-3:]
    total = own_ref[...]
    for ref in refs[:-3]:
        total = total + ref[...].astype(F32)
    latent = silu_of_half(0.5 * total)
    tall = quarter * 32
    turned = jnp.concatenate([latent[tall : tall + 16], jnp.zeros((112, 128), F32)], axis=0).T
    ext = ext_ref.shape[2]
    for r in range(quarter):
        rows = slice(r * 32, (r + 1) * 32)
        line = jnp.concatenate(
            [
                latent[rows, 0:nb],
                turned[rows, 1:2],
                jnp.zeros((32, ext - nb - 2), F32),
                turned[rows, 0:1],
            ],
            axis=1,
        )
        put_latent(ext_ref, r, line)
        if r == 0:
            top_ref[...] = line.astype(BF)
        if r == quarter - 1:
            low_ref[...] = line.astype(BF)


def put_latent(ref, at, line):
    ext = line.shape[1]
    ref[at, 0:32, :] = pltpu.roll(line, 1, 1).astype(BF)
    ref[at, 32:64, :] = line.astype(BF)
    ref[at, 64:96, :] = pltpu.roll(line, ext - 1, 1).astype(BF)


def decoder_kernel(nb, ext_ref, above_ref, below_ref, w1_ref, w2_ref, p_ref, r_ref, out_ref, l_ref, u_ref, g_ref):
    row_at, mem_at = lax.axis_index("row"), lax.axis_index("mem")
    row_last, mem_last = lax.axis_size("row") - 1, lax.axis_size("mem") - 1
    rows, _, wide = ext_ref.shape
    l_ref[0] = jnp.zeros_like(l_ref[0])
    l_ref[rows + 3] = jnp.zeros_like(l_ref[0])
    put_latent(l_ref, 1, above_ref[...].astype(F32))
    l_ref[2 : rows + 2] = ext_ref[...]
    put_latent(l_ref, rows + 2, below_ref[...].astype(F32))
    w1, w2 = w1_ref[...], w2_ref[...]
    lane = lax.broadcasted_iota(jnp.int32, (32, wide), 1)
    keep_odd = jnp.where((lane == wide - 1) & (mem_at == 0), 0.0, 1.0).astype(F32)
    keep_even = jnp.where((lane == nb) & (mem_at == mem_last), 0.0, 1.0).astype(F32)
    keep_first = jnp.where(row_at == 0, 0.0, 1.0).astype(F32)
    keep_last = jnp.where(row_at == row_last, 0.0, 1.0).astype(F32)
    for a in range(-1, rows + 1):
        v = silu_of_half(dot(w1, l_ref[a + 1 : a + 4].reshape(288, wide)))
        for pr in range(2):
            row = 2 * a + pr
            if not -1 <= row <= 2 * rows:
                continue
            even = v[pr * 64 : pr * 64 + 32] * keep_even
            odd = v[pr * 64 + 32 : pr * 64 + 64] * keep_odd
            if row == -1:
                even, odd = even * keep_first, odd * keep_first
            if row == 2 * rows:
                even, odd = even * keep_last, odd * keep_last
            at = (row + 1) * 128
            u_ref[at : at + 32, :] = pltpu.roll(odd, 1, 1)[:, 0:nb].astype(BF)
            u_ref[at + 32 : at + 64, :] = even[:, 0:nb].astype(BF)
            u_ref[at + 64 : at + 96, :] = odd[:, 0:nb].astype(BF)
            u_ref[at + 96 : at + 128, :] = pltpu.roll(even, wide - 1, 1)[:, 0:nb].astype(BF)
    for a in range(2 * rows):
        v = dot(w2, u_ref[a * 128 : (a + 3) * 128, :]).astype(BF)
        for pr in range(2):
            for ph in range(4):
                g_ref[(2 * a + pr) * 16 : (2 * a + pr + 1) * 16, ph * nb : (ph + 1) * nb] = v[
                    (pr * 4 + ph) * 16 : (pr * 4 + ph + 1) * 16
                ]
    g = dot(r_ref[...], g_ref[...]).astype(BF)
    out_ref[...] = dot(g, p_ref[...]).astype(BF).reshape(out_ref.shape)


def shifted(value, axis, by):
    peers = lax.axis_size(axis)
    return lax.ppermute(value, axis, [(i, i + by) for i in range(peers) if 0 <= i + by < peers])


def swapped(value, by):
    return lax.ppermute(value, "mem", [(i, i ^ by) for i in range(lax.axis_size("mem"))])


VMEM = pl.BlockSpec(memory_space=pltpu.VMEM)
PARAMS = pltpu.CompilerParams(vmem_limit_bytes=56 * 2**20)


def call(kernel, outs, scratch, *operands):
    return pl.pallas_call(
        kernel,
        out_shape=[jax.ShapeDtypeStruct(*o) for o in outs],
        in_specs=[VMEM] * len(operands),
        out_specs=[VMEM] * len(outs),
        scratch_shapes=[pltpu.VMEM(*s) for s in scratch],
        compiler_params=PARAMS,
    )(*operands)


def per_device(members, enc_first, enc_second, enc_third, mix_weight, dec_first, dec_second):
    count, channels, rows, wide = members.shape
    own, sel_down, sel_up, per, total = first_selectors(count, channels, rows)
    half, quarter = rows // 2, rows // 4
    cols = wide // 4
    peers = lax.axis_size("mem")
    nb = cols // peers
    tile = 128
    lanes = 4 * tile
    chunks = wide // lanes
    x = members.reshape(count * channels * rows, wide)
    nd, nu = count * channels * UP, count * channels * DOWN
    pack = functools.partial(pack_kernel, count, channels, rows)
    sizes = [(nd * chunks, lanes), (nu * chunks, lanes)]
    down, up = call(pack, [(s, BF) for s in sizes], [(s, F32) for s in sizes], x)
    up = shifted(up, "row", -1)
    down = shifted(down, "row", 1)

    w1 = jnp.pad(enc_first.transpose(1, 2, 3, 0).reshape(channels * 9, 64), ((0, 3), (0, 0)))
    w2 = enc_second.transpose(2, 3, 0, 1).reshape(9, 64, 64)
    w3 = enc_third.transpose(2, 3, 0, 1).reshape(9, 16, 64)
    d1 = dec_first.transpose(2, 3, 0, 1).reshape(16, 32, 32)
    d2 = dec_second.transpose(2, 3, 0, 1).reshape(16, 16, 32)
    mix = lax.dynamic_slice_in_dim(mix_weight, lax.axis_index("mem") * (count * CH_BOT), count * CH_BOT, 1)
    apart = jnp.asarray(spread(4, tile), BF)
    top_pre, low_pre, top_h1, low_h1, top_v, low_v, mid, w2_big, w3_big, w1_down, w1_up, wd1, wd2 = call(
        functools.partial(inner_kernel, count, channels, rows),
        [
            ((count, 128, cols), F32),
            ((count, 128, cols), F32),
            ((count, 2, 256, cols), BF),
            ((count, 3, 256, cols), BF),
            ((count, 32, cols), F32),
            ((count, 32, cols), F32),
            ((quarter - 3, 32, cols), F32),
            ((256, 1024), BF),
            ((64, 256), BF),
            ((count, 384, total[0]), BF),
            ((count, 128, total[1]), BF),
            ((128, 288), BF),
            ((128, 384), BF),
        ],
        [
            ((count, 5 * channels * rows, cols), BF),
            ((3, 128, 5 * channels * rows), BF),
            ((count, half - 1, 256, cols), BF),
        ],
        x, w1, w2, w3, mix, jnp.asarray(own, BF), jnp.asarray(sel_down, BF), jnp.asarray(sel_up, BF), apart, d1, d2,
    )
    (low,) = call(
        functools.partial(low_kernel, count, channels, half, per[1]),
        [((32, cols), F32)],
        [((total[1], cols), F32), ((count, 4, 256, cols), BF)],
        up, apart, w1_up, low_pre, low_h1, w2_big, w3_big, low_v, mix,
    )
    slots = peers // 2
    chunk = (quarter * 32 + 16, 128)
    keep, send = call(
        functools.partial(top_kernel, count, channels, half, per[0], nb),
        [((slots,) + chunk, BF)] * 2,
        [((total[0], cols), F32), ((count, 5, 256, cols), BF), ((quarter * 32, cols + 256), F32)],
        down, apart, w1_down, top_pre, top_h1, w2_big, w3_big, top_v, mix, mid, low,
    )
    got = swapped(send, 1)
    mine, *others = call(pair_kernel, [(chunk, F32)] + [(chunk, BF)] * (slots - 1), [], keep, got)
    others = [swapped(o, 2 * (k + 1)) for k, o in enumerate(others)]
    ext = padded(nb + 2, 128)
    latent, top, low = call(
        functools.partial(latent_kernel, nb, quarter),
        [((quarter, 96, ext), BF), ((32, ext), BF), ((32, ext), BF)],
        [],
        mine, *others,
    )
    above = shifted(low, "row", 1)
    below = shifted(top, "row", -1)
    reorder = np.zeros((16 * rows, 16 * rows), np.float32)
    for r in range(rows):
        for level in range(16):
            reorder[level * rows + r, r * 16 + level] = 1
    (out,) = call(
        functools.partial(decoder_kernel, nb),
        [((16, rows, 4 * nb), BF)],
        [((quarter + 4, 96, ext), BF), ((128 * (half + 2), nb), BF), ((16 * rows, 4 * nb), BF)],
        latent, above, below, wd1, wd2, jnp.asarray(spread(4, nb).T, BF), jnp.asarray(reorder, BF),
    )
    return out


def solution(mesh):
    placed = (P("mem", None, "row", None), P(), P(), P(), P(), P(), P())
    return jax.shard_map(
        per_device, mesh=mesh, in_specs=placed, out_specs=P(None, "row", "mem"), check_vma=False
    )
```

```python
import functools

import jax
import jax.numpy as jnp
import numpy as np
from jax import lax
from jax.experimental import pallas as pl
from jax.experimental.pallas import tpu as pltpu
from jax.sharding import PartitionSpec as P

BF = jnp.bfloat16
F32 = jnp.float32
CH_BOT = 16
UP = 5
DOWN = 2
TRANSPOSED = [(p, i, 2 * i - p) for p in range(2) for i in range(3) if 0 <= 2 * i - p < 4]


def dot(a, b):
    return lax.dot_general(a, b, (((1,), (0,)), ((), ())), preferred_element_type=F32)


def dot_t(a, b):
    return lax.dot_general(a, b, (((0,), (0,)), ((), ())), preferred_element_type=F32)


def silu_of_half(y):
    return y + y * jnp.tanh(y)


def spread(step, tile):
    one = np.zeros((step * tile, step * tile), np.float32)
    for q in range(step):
        for c in range(tile):
            one[step * c + q, q * tile + c] = 1
    return one


def padded(n, to):
    return -(-n // to) * to


def first_selectors(members, channels, rows):
    half = rows // 2
    own = np.zeros((3, 2, 48, 5 * channels * rows), np.float32)
    per = [padded(members * channels * n, 8) for n in (UP, DOWN)]
    total = [padded(5 * n, 16) for n in per]
    down = np.zeros((members, 3, 2, 48, total[0]), np.float32)
    up = np.zeros((members, 2, 48, total[1]), np.float32)
    for pc in range(2):
        for c in range(channels):
            for dr in range(3):
                for dc in range(3):
                    tap = (c * 3 + dr) * 3 + dc
                    ph = 2 * pc + dc
                    for kind, h in enumerate((1, 0, half)):
                        row = 2 * h + dr - 1
                        if 0 <= row < rows:
                            own[kind, pc, tap, (ph * channels + c) * rows + row] = 1
                    for m in range(members):
                        for kind, h in enumerate((-2, -1, 0)):
                            row = 2 * h + dr - 1
                            if row < 0:
                                down[m, kind, pc, tap, ph * per[0] + (m * channels + c) * UP + row + UP] = 1
                        row = 2 * half + dr - 1
                        if row >= rows:
                            up[m, pc, tap, ph * per[1] + (m * channels + c) * DOWN + row - rows] = 1
    return own, down, up, per, total


def shift_right(v):
    return jnp.concatenate([jnp.zeros_like(v[:, :1]), v[:, :-1]], axis=1)


def shift_left(v):
    return jnp.concatenate([v[:, 1:], jnp.zeros_like(v[:, :1])], axis=1)


def put_hidden(ref, m, at, value):
    v = value.astype(BF)
    even, odd = v[0:64], v[64:128]
    ref[m, at, 64:128, :] = even
    ref[m, at, 128:192, :] = odd
    ref[m, at, 0:64, :] = shift_right(odd)
    ref[m, at, 192:256, :] = shift_left(even)


def slab(ref, m, first, count):
    return ref[m, first : first + count].reshape(count * 256, ref.shape[3])


def place_halo(source, spreader, y_ref, count, per):
    tile = spreader.shape[0] // 4
    z = dot(source, spreader)
    y_ref[...] = jnp.zeros_like(y_ref)
    for t in range(y_ref.shape[1] // tile):
        for q in range(4):
            y_ref[(q + 1) * per : (q + 1) * per + count, t * tile : (t + 1) * tile] = z[
                t * count : (t + 1) * count, q * tile : (q + 1) * tile
            ]
    y_ref[0:per, :] = shift_right(y_ref[4 * per : 5 * per, :])
    return y_ref[...].astype(BF)


def pack_kernel(members, channels, rows, x_ref, down_ref, up_ref, d_scr, u_scr):
    wide = x_ref.shape[1]
    lanes = down_ref.shape[1]
    nd, nu = members * channels * UP, members * channels * DOWN
    for t in range(wide // lanes):
        for g in range(members * channels):
            block = x_ref[g * rows : (g + 1) * rows, t * lanes : (t + 1) * lanes].astype(F32)
            d_scr[t * nd + g * UP : t * nd + (g + 1) * UP, :] = block[rows - UP : rows]
            u_scr[t * nu + g * DOWN : t * nu + (g + 1) * DOWN, :] = block[0:DOWN]
    down_ref[...] = d_scr[...].astype(BF)
    up_ref[...] = u_scr[...].astype(BF)


def inner_kernel(
    members, channels, rows,
    x_ref, w1_ref, w2_ref, w3_ref, mix_ref, own_ref, down_ref, up_ref, p_ref, d1_ref, d2_ref,
    top_pre, low_pre, top_h1, low_h1, top_v, low_v, mixed_ref, w2_big, w3_big, w1_down, w1_up, wd1, wd2,
    y_ref, w1_own, h1_ref,
):
    half = rows // 2
    wide = x_ref.shape[1]
    tile = p_ref.shape[0] // 4
    cr = channels * rows
    spreader = p_ref[...]
    for t in range(wide // (4 * tile)):
        z = dot(x_ref[:, 4 * tile * t : 4 * tile * (t + 1)], spreader).astype(BF)
        for q in range(4):
            for m in range(members):
                y_ref[m, (q + 1) * cr : (q + 2) * cr, t * tile : (t + 1) * tile] = z[
                    m * cr : (m + 1) * cr, q * tile : (q + 1) * tile
                ]
    for m in range(members):
        y_ref[m, 0:cr, :] = shift_right(y_ref[m, 4 * cr : 5 * cr, :])

    w1 = w1_ref[...]
    for pc in range(2):
        lanes = slice(pc * 64, (pc + 1) * 64)
        for kind in range(3):
            w1_own[kind, lanes, :] = (0.5 * dot_t(w1, own_ref[kind, pc])).astype(BF)
        for m in range(members):
            for kind in range(3):
                w1_down[m, kind * 128 + pc * 64 : kind * 128 + (pc + 1) * 64, :] = (
                    0.5 * dot_t(w1, down_ref[m, kind, pc])
                ).astype(BF)
            w1_up[m, lanes, :] = (0.5 * dot_t(w1, up_ref[m, pc])).astype(BF)
    w2_big[...] = jnp.zeros_like(w2_big)
    for orow in range(2):
        for ocol in range(2):
            for dr in range(3):
                for dc in range(3):
                    w2_big[
                        (orow * 2 + ocol) * 64 : (orow * 2 + ocol + 1) * 64,
                        (orow + dr) * 256 + (ocol + dc) * 64 : (orow + dr) * 256 + (ocol + dc + 1) * 64,
                    ] = (0.5 * w2_ref[dr * 3 + dc].astype(F32)).astype(BF)
    w3_big[...] = jnp.zeros_like(w3_big)
    for dr, place, base in ((1, 0, 0), (2, 0, 128), (0, 2, 128)):
        for dc, shifted_out, at in ((1, 0, 0), (2, 0, 64), (0, 1, 64)):
            w3_big[(place + shifted_out) * 16 : (place + shifted_out + 1) * 16, base + at : base + at + 64] = (
                0.5 * w3_ref[dr * 3 + dc].astype(F32)
            ).astype(BF)
    wd1[...] = jnp.zeros_like(wd1)
    wd2[...] = jnp.zeros_like(wd2)
    for pr, rr, tr in TRANSPOSED:
        for pc, cc, tc in TRANSPOSED:
            wd1[(pr * 2 + pc) * 32 : (pr * 2 + pc + 1) * 32, (rr * 3 + cc) * 32 : (rr * 3 + cc + 1) * 32] = (
                0.5 * d1_ref[tr * 4 + tc].astype(F32)
            ).astype(BF)
            for q in range(2):
                at = pr * 4 + 2 * q + pc
                to = rr * 4 + q + cc
                wd2[at * 16 : (at + 1) * 16, to * 32 : (to + 1) * 32] = d2_ref[tr * 4 + tc]

    for m in range(members):
        base = w1_own[0]
        for h in range(1, half):
            w = base if h == 1 else pltpu.roll(base.astype(F32), 2 * (h - 1), 1).astype(BF)
            put_hidden(h1_ref, m, h - 1, silu_of_half(dot(w, y_ref[m])))
        top_pre[m] = dot(w1_own[1], y_ref[m])
        low_pre[m] = dot(w1_own[2], y_ref[m])
        top_h1[m] = h1_ref[m, 0:2]
        low_h1[m] = h1_ref[m, half - 4 : half - 1]

    mids = []
    for m in range(members):
        carry = None
        for a in range(2, half - 2, 2):
            h2 = silu_of_half(dot(w2_big[...], slab(h1_ref, m, a - 2, 4))).astype(BF)
            v = dot(w3_big[...], h2)
            if a == 2:
                top_v[m] = v[0:32]
            else:
                w = v[0:32] + carry
                mids.append((a // 2, m, silu_of_half(w[0:16] + shift_right(w[16:32])).astype(BF)))
            carry = v[32:64]
        low_v[m] = carry
    for r in range(2, half // 2 - 1):
        mixed_ref[r - 2] = dot(mix_ref[...], jnp.concatenate([b for s, _, b in mids if s == r], axis=0))


def low_kernel(
    members, channels, half, per,
    got_ref, p_ref, w1_ref, pre_ref, h1_in, w2_big, w3_big, v_ref, mix_ref, mixed_ref, y_ref, h1_ref,
):
    below = jnp.where(lax.axis_index("row") == lax.axis_size("row") - 1, 0.0, 1.0).astype(F32)
    y = place_halo(got_ref[...], p_ref[...], y_ref, members * channels * DOWN, per)
    parts = []
    for m in range(members):
        h1_ref[m, 0:3] = h1_in[m]
        put_hidden(h1_ref, m, 3, silu_of_half((dot(w1_ref[m], y) + pre_ref[m]) * below))
        h2 = silu_of_half(dot(w2_big[...], slab(h1_ref, m, 0, 4))).astype(BF)
        w = dot(w3_big[0:32], h2) + v_ref[m]
        parts.append(silu_of_half(w[0:16] + shift_right(w[16:32])).astype(BF))
    mixed_ref[...] = dot(mix_ref[...], jnp.concatenate(parts, axis=0))


def top_kernel(
    members, channels, half, per, nb,
    got_ref, p_ref, w1_ref, pre_ref, h1_in, w2_big, w3_big, v_ref, mix_ref, mid_ref, low_ref,
    keep_ref, send_ref, y_ref, h1_ref, mixed_ref,
):
    above = jnp.where(lax.axis_index("row") == 0, 0.0, 1.0).astype(F32)
    y = place_halo(got_ref[...], p_ref[...], y_ref, members * channels * UP, per)
    first, second = [], []
    for m in range(members):
        h1_ref[m, 3:5] = h1_in[m]
        fresh = dot(w1_ref[m], y)
        put_hidden(h1_ref, m, 0, silu_of_half(fresh[0:128]))
        put_hidden(h1_ref, m, 1, silu_of_half(fresh[128:256]))
        put_hidden(h1_ref, m, 2, silu_of_half(fresh[256:384] + pre_ref[m]))
        h2 = silu_of_half(dot(w2_big[0:128, 0:768], slab(h1_ref, m, 0, 3)) * above).astype(BF)
        carry = dot(w3_big[32:64, 128:256], h2)
        h2 = silu_of_half(dot(w2_big[...], slab(h1_ref, m, 1, 4))).astype(BF)
        v = dot(w3_big[...], h2)
        w = v[0:32] + carry
        first.append(silu_of_half(w[0:16] + shift_right(w[16:32])).astype(BF))
        w = v[32:64] + v_ref[m]
        second.append(silu_of_half(w[0:16] + shift_right(w[16:32])).astype(BF))
    cols = y_ref.shape[1]
    quarter = half // 2
    margin = jnp.zeros((quarter * 32, 128), F32)
    mixed_ref[:, 0:128] = margin
    mixed_ref[:, 128 + cols : 256 + cols] = margin
    mixed_ref[0:32, 128 : 128 + cols] = dot(mix_ref[...], jnp.concatenate(first, axis=0))
    mixed_ref[32:64, 128 : 128 + cols] = dot(mix_ref[...], jnp.concatenate(second, axis=0))
    for r in range(2, quarter - 1):
        mixed_ref[r * 32 : (r + 1) * 32, 128 : 128 + cols] = mid_ref[r - 2]
    mixed_ref[(quarter - 1) * 32 : quarter * 32, 128 : 128 + cols] = low_ref[...]

    me = lax.axis_index("mem")
    slots = lax.axis_size("mem") // 2
    tall = quarter * 32
    def lanes_from(lane):
        base = pl.multiple_of(lane // 128 * 128, 128)
        v = mixed_ref[:, pl.ds(base, 128)]
        return v if nb % 128 == 0 else pltpu.roll(v, (128 - lane % 128) % 128, 1)

    lane_at = lax.broadcasted_iota(jnp.int32, (tall, 128), 1)
    edges = jnp.zeros((tall, 128), F32)
    for side, ref in enumerate((keep_ref, send_ref)):
        for k in range(slots):
            block = me ^ (2 * k + side)
            start = 128 + block * nb
            ref[k, 0:tall, :] = lanes_from(start).astype(BF)
            if nb % 128 == 0:
                left = mixed_ref[:, pl.ds(pl.multiple_of(start - 128, 128), 128)][:, 127:128]
            else:
                left = lanes_from(start - 1)[:, 0:1]
            right = lanes_from(start + nb)[:, 0:1]
            at = 2 * (side * slots + k)
            edges = jnp.where(lane_at == at, left, edges)
            edges = jnp.where(lane_at == at + 1, right, edges)
    turned = edges.T
    for side, ref in enumerate((keep_ref, send_ref)):
        for k in range(slots):
            at = 2 * (side * slots + k)
            ref[k, tall : tall + 16, :] = jnp.concatenate(
                [turned[at : at + 2], jnp.zeros((14, 128), F32)], axis=0
            ).astype(BF)


def pair_kernel(keep_ref, got_ref, own_ref, *out_refs):
    own_ref[...] = keep_ref[0].astype(F32) + got_ref[0].astype(F32)
    for k, ref in enumerate(out_refs):
        ref[...] = (keep_ref[k + 1].astype(F32) + got_ref[k + 1].astype(F32)).astype(BF)


def latent_kernel(nb, quarter, own_ref, *refs):
    ext_ref, top_ref, low_ref = refs[-3:]
    total = own_ref[...]
    for ref in refs[:-3]:
        total = total + ref[...].astype(F32)
    latent = silu_of_half(0.5 * total)
    tall = quarter * 32
    turned = jnp.concatenate([latent[tall : tall + 16], jnp.zeros((112, 128), F32)], axis=0).T
    ext = ext_ref.shape[2]
    for r in range(quarter):
        rows = slice(r * 32, (r + 1) * 32)
        line = jnp.concatenate(
            [
                latent[rows, 0:nb],
                turned[rows, 1:2],
                jnp.zeros((32, ext - nb - 2), F32),
                turned[rows, 0:1],
            ],
            axis=1,
        )
        put_latent(ext_ref, r, line)
        if r == 0:
            top_ref[...] = line.astype(BF)
        if r == quarter - 1:
            low_ref[...] = line.astype(BF)


def put_latent(ref, at, line):
    ext = line.shape[1]
    ref[at, 0:32, :] = pltpu.roll(line, 1, 1).astype(BF)
    ref[at, 32:64, :] = line.astype(BF)
    ref[at, 64:96, :] = pltpu.roll(line, ext - 1, 1).astype(BF)


def decoder_kernel(nb, ext_ref, above_ref, below_ref, w1_ref, w2_ref, p_ref, r_ref, out_ref, l_ref, u_ref, g_ref):
    row_at, mem_at = lax.axis_index("row"), lax.axis_index("mem")
    row_last, mem_last = lax.axis_size("row") - 1, lax.axis_size("mem") - 1
    rows, _, wide = ext_ref.shape
    l_ref[0] = jnp.zeros_like(l_ref[0])
    l_ref[rows + 3] = jnp.zeros_like(l_ref[0])
    put_latent(l_ref, 1, above_ref[...].astype(F32))
    l_ref[2 : rows + 2] = ext_ref[...]
    put_latent(l_ref, rows + 2, below_ref[...].astype(F32))
    w1, w2 = w1_ref[...], w2_ref[...]
    lane = lax.broadcasted_iota(jnp.int32, (32, wide), 1)
    keep_odd = jnp.where((lane == wide - 1) & (mem_at == 0), 0.0, 1.0).astype(F32)
    keep_even = jnp.where((lane == nb) & (mem_at == mem_last), 0.0, 1.0).astype(F32)
    keep_first = jnp.where(row_at == 0, 0.0, 1.0).astype(F32)
    keep_last = jnp.where(row_at == row_last, 0.0, 1.0).astype(F32)
    for a in range(-1, rows + 1):
        v = silu_of_half(dot(w1, l_ref[a + 1 : a + 4].reshape(288, wide)))
        for pr in range(2):
            row = 2 * a + pr
            if not -1 <= row <= 2 * rows:
                continue
            even = v[pr * 64 : pr * 64 + 32] * keep_even
            odd = v[pr * 64 + 32 : pr * 64 + 64] * keep_odd
            if row == -1:
                even, odd = even * keep_first, odd * keep_first
            if row == 2 * rows:
                even, odd = even * keep_last, odd * keep_last
            at = (row + 1) * 128
            u_ref[at : at + 32, :] = pltpu.roll(odd, 1, 1)[:, 0:nb].astype(BF)
            u_ref[at + 32 : at + 64, :] = even[:, 0:nb].astype(BF)
            u_ref[at + 64 : at + 96, :] = odd[:, 0:nb].astype(BF)
            u_ref[at + 96 : at + 128, :] = pltpu.roll(even, wide - 1, 1)[:, 0:nb].astype(BF)
    for a in range(2 * rows):
        v = dot(w2, u_ref[a * 128 : (a + 3) * 128, :]).astype(BF)
        for pr in range(2):
            for ph in range(4):
                g_ref[(2 * a + pr) * 16 : (2 * a + pr + 1) * 16, ph * nb : (ph + 1) * nb] = v[
                    (pr * 4 + ph) * 16 : (pr * 4 + ph + 1) * 16
                ]
    g = dot(r_ref[...], g_ref[...]).astype(BF)
    out_ref[...] = dot(g, p_ref[...]).astype(BF).reshape(out_ref.shape)


def shifted(value, axis, by):
    peers = lax.axis_size(axis)
    return lax.ppermute(value, axis, [(i, i + by) for i in range(peers) if 0 <= i + by < peers])


def swapped(value, by):
    return lax.ppermute(value, "mem", [(i, i ^ by) for i in range(lax.axis_size("mem"))])


VMEM = pl.BlockSpec(memory_space=pltpu.VMEM)
def params(mb): return pltpu.CompilerParams(vmem_limit_bytes=mb * 2**20)


def call(kernel, outs, scratch, *operands, mb=16):
    return pl.pallas_call(
        kernel,
        out_shape=[jax.ShapeDtypeStruct(*o) for o in outs],
        in_specs=[VMEM] * len(operands),
        out_specs=[VMEM] * len(outs),
        scratch_shapes=[pltpu.VMEM(*s) for s in scratch],
        compiler_params=params(mb),
    )(*operands)


def per_device(members, enc_first, enc_second, enc_third, mix_weight, dec_first, dec_second):
    count, channels, rows, wide = members.shape
    own, sel_down, sel_up, per, total = first_selectors(count, channels, rows)
    half, quarter = rows // 2, rows // 4
    cols = wide // 4
    peers = lax.axis_size("mem")
    nb = cols // peers
    tile = 128
    lanes = 4 * tile
    chunks = wide // lanes
    x = members.reshape(count * channels * rows, wide)
    nd, nu = count * channels * UP, count * channels * DOWN
    pack = functools.partial(pack_kernel, count, channels, rows)
    sizes = [(nd * chunks, lanes), (nu * chunks, lanes)]
    down, up = call(pack, [(s, BF) for s in sizes], [(s, F32) for s in sizes], x)
    up = shifted(up, "row", -1)
    down = shifted(down, "row", 1)

    w1 = jnp.pad(enc_first.transpose(1, 2, 3, 0).reshape(channels * 9, 64), ((0, 3), (0, 0)))
    w2 = enc_second.transpose(2, 3, 0, 1).reshape(9, 64, 64)
    w3 = enc_third.transpose(2, 3, 0, 1).reshape(9, 16, 64)
    d1 = dec_first.transpose(2, 3, 0, 1).reshape(16, 32, 32)
    d2 = dec_second.transpose(2, 3, 0, 1).reshape(16, 16, 32)
    mix = lax.dynamic_slice_in_dim(mix_weight, lax.axis_index("mem") * (count * CH_BOT), count * CH_BOT, 1)
    apart = jnp.asarray(spread(4, tile), BF)
    top_pre, low_pre, top_h1, low_h1, top_v, low_v, mid, w2_big, w3_big, w1_down, w1_up, wd1, wd2 = call(
        functools.partial(inner_kernel, count, channels, rows),
        [
            ((count, 128, cols), F32),
            ((count, 128, cols), F32),
            ((count, 2, 256, cols), BF),
            ((count, 3, 256, cols), BF),
            ((count, 32, cols), F32),
            ((count, 32, cols), F32),
            ((quarter - 3, 32, cols), F32),
            ((256, 1024), BF),
            ((64, 256), BF),
            ((count, 384, total[0]), BF),
            ((count, 128, total[1]), BF),
            ((128, 288), BF),
            ((128, 384), BF),
        ],
        [
            ((count, 5 * channels * rows, cols), BF),
            ((3, 128, 5 * channels * rows), BF),
            ((count, half - 1, 256, cols), BF),
        ],
        x, w1, w2, w3, mix, jnp.asarray(own, BF), jnp.asarray(sel_down, BF), jnp.asarray(sel_up, BF), apart, d1, d2, mb=32,
    )
    (low,) = call(
        functools.partial(low_kernel, count, channels, half, per[1]),
        [((32, cols), F32)],
        [((total[1], cols), F32), ((count, 4, 256, cols), BF)],
        up, apart, w1_up, low_pre, low_h1, w2_big, w3_big, low_v, mix, mb=20,
    )
    slots = peers // 2
    chunk = (quarter * 32 + 16, 128)
    keep, send = call(
        functools.partial(top_kernel, count, channels, half, per[0], nb),
        [((slots,) + chunk, BF)] * 2,
        [((total[0], cols), F32), ((count, 5, 256, cols), BF), ((quarter * 32, cols + 256), F32)],
        down, apart, w1_down, top_pre, top_h1, w2_big, w3_big, top_v, mix, mid, low, mb=20,
    )
    got = swapped(send, 1)
    mine, *others = call(pair_kernel, [(chunk, F32)] + [(chunk, BF)] * (slots - 1), [], keep, got)
    others = [swapped(o, 2 * (k + 1)) for k, o in enumerate(others)]
    ext = padded(nb + 2, 128)
    latent, top, low = call(
        functools.partial(latent_kernel, nb, quarter),
        [((quarter, 96, ext), BF), ((32, ext), BF), ((32, ext), BF)],
        [],
        mine, *others,
    )
    above = shifted(low, "row", 1)
    below = shifted(top, "row", -1)
    reorder = np.zeros((16 * rows, 16 * rows), np.float32)
    for r in range(rows):
        for level in range(16):
            reorder[level * rows + r, r * 16 + level] = 1
    (out,) = call(
        functools.partial(decoder_kernel, nb),
        [((16, rows, 4 * nb), BF)],
        [((quarter + 4, 96, ext), BF), ((128 * (half + 2), nb), BF), ((16 * rows, 4 * nb), BF)],
        latent, above, below, wd1, wd2, jnp.asarray(spread(4, nb).T, BF), jnp.asarray(reorder, BF),
    )
    return out


def solution(mesh):
    placed = (P("mem", None, "row", None), P(), P(), P(), P(), P(), P())
    return jax.shard_map(
        per_device, mesh=mesh, in_specs=placed, out_specs=P(None, "row", "mem"), check_vma=False
    )
```

```python
import functools

import jax
import jax.numpy as jnp
import numpy as np
from jax import lax
from jax.experimental import pallas as pl
from jax.experimental.pallas import tpu as pltpu
from jax.sharding import PartitionSpec as P

BF = jnp.bfloat16
F32 = jnp.float32
CH_BOT = 16
UP = 3
DOWN = 2
TRANSPOSED = [(p, i, 2 * i - p) for p in range(2) for i in range(3) if 0 <= 2 * i - p < 4]


def dot(a, b):
    return lax.dot_general(a, b, (((1,), (0,)), ((), ())), preferred_element_type=F32)


def dot_t(a, b):
    return lax.dot_general(a, b, (((0,), (0,)), ((), ())), preferred_element_type=F32)


def silu_of_half(y):
    return y + y * jnp.tanh(y)


def padded(n, to):
    return -(-n // to) * to


def spread(step, tile):
    one = np.zeros((step * tile, step * tile), np.float32)
    for q in range(step):
        for c in range(tile):
            one[step * c + q, q * tile + c] = 1
    return one


def shift_right(v):
    return jnp.concatenate([jnp.zeros_like(v[:, :1]), v[:, :-1]], axis=1)


def shift_left(v):
    return jnp.concatenate([v[:, 1:], jnp.zeros_like(v[:, :1])], axis=1)


def is_row(at):
    return jnp.where(lax.axis_index("row") == at, 0.0, 1.0).astype(F32)


def put_hidden(ref, at, value):
    v = value.astype(BF)
    even, odd = v[0:64], v[64:128]
    ref[at * 256 + 64 : at * 256 + 128, :] = even
    ref[at * 256 + 128 : at * 256 + 192, :] = odd
    ref[at * 256 : at * 256 + 64, :] = shift_right(odd)
    ref[at * 256 + 192 : at * 256 + 256, :] = shift_left(even)


def apart(block, even_ref, odd_ref):
    first = dot(block[:, 0:256], even_ref)
    second = dot(block[:, 256:512], odd_ref)
    low = lax.broadcasted_iota(jnp.int32, (block.shape[0], 128), 1) < 64
    out = []
    for half in range(2):
        e, o = first[:, half * 128 : half * 128 + 128], second[:, half * 128 : half * 128 + 128]
        out.append(jnp.where(low, e, o))
        out.append(pltpu.roll(jnp.where(low, o, e), 64, 1))
    return out


def place_halo(source, spread_ref, y_ref, count, per):
    y_ref[...] = jnp.zeros_like(y_ref)
    for q, z in enumerate(apart(source, spread_ref[0], spread_ref[1])):
        for t in range(y_ref.shape[1] // 128):
            y_ref[(q + 1) * per : (q + 1) * per + count, t * 128 : (t + 1) * 128] = z[t * count : (t + 1) * count]
    y_ref[0:per, :] = shift_right(y_ref[4 * per : 5 * per, :])
    return y_ref[...].astype(BF)


def pack_kernel(members, channels, rows, x_ref, down_ref, up_ref, d_scr, u_scr):
    wide = x_ref.shape[1]
    lanes = down_ref.shape[1]
    nd, nu = members * channels * UP, members * channels * DOWN
    for t in range(wide // lanes):
        for g in range(members * channels):
            block = x_ref[g * rows : (g + 1) * rows, t * lanes : (t + 1) * lanes].astype(F32)
            d_scr[t * nd + g * UP : t * nd + (g + 1) * UP, :] = block[rows - UP : rows]
            u_scr[t * nu + g * DOWN : t * nu + (g + 1) * DOWN, :] = block[0:DOWN]
    down_ref[...] = d_scr[...].astype(BF)
    up_ref[...] = u_scr[...].astype(BF)


def inner_kernel(
    members, channels, rows, per,
    x_ref, w1_ref, w2_ref, w3_ref, mix_ref,
    h_first, h_last, a_first, a_second, a_last, v_second, v_last, mixed_ref,
    w2_big, w3_big, w1_down, w1_up, spread_ref, mix_own,
    w1_flat, w1_own, y_ref, out1_ref, h1_ref, h2_ref,
):
    half, groups = rows // 2, rows // 8
    wide = x_ref.shape[1]
    cols = wide // 4

    row_of = lax.broadcasted_iota(jnp.int32, (256, 256), 0)
    lane_of = lax.broadcasted_iota(jnp.int32, (256, 256), 1)
    place = lane_of // 64
    for odd in range(2):
        q = place ^ odd
        spread_ref[odd] = jnp.where(row_of == 4 * (lane_of - 64 * place) + q, 1.0, 0.0).astype(BF)

    w1_flat[...] = jnp.zeros_like(w1_flat)
    for c in range(channels):
        for dr in range(3):
            at = (c * 3 + dr) * 3
            w1_flat[at : at + 3, :] = 0.5 * w1_ref[c, dr].astype(F32)
    w1 = w1_flat[...].astype(BF)
    taps = w1.shape[0]

    def taps_at(lanes, target):
        tap = lax.broadcasted_iota(jnp.int32, (taps, lanes), 0)
        c = sum(((tap >= 9 * k).astype(jnp.int32) for k in range(1, channels)), jnp.zeros_like(tap))
        rest = tap - 9 * c
        dr = (rest >= 3).astype(jnp.int32) + (rest >= 6).astype(jnp.int32)
        dc = rest - 3 * dr
        to, valid = target(c, dr, dc)
        at = lax.broadcasted_iota(jnp.int32, (taps, lanes), 1)
        return dot_t(w1, jnp.where((at == to) & valid, 1.0, 0.0).astype(BF)).astype(BF)

    for pc in range(2):
        for j in range(5):
            def own(c, dr, dc):
                row = 2 * j + dr - 1
                return ((2 * pc + dc) * channels + c) * 8 + row, (row >= 0) & (row < 8)
            w1_own[j * 128 + pc * 64 : j * 128 + pc * 64 + 64, :] = taps_at(w1_own.shape[1], own)
        for m in range(members):
            for kind in range(2):
                def above(c, dr, dc):
                    slot = dr if kind == 0 else dr + 2
                    return (2 * pc + dc) * per[0] + (m * channels + c) * UP + slot, slot < UP
                w1_down[m, kind * 128 + pc * 64 : kind * 128 + pc * 64 + 64, :] = taps_at(w1_down.shape[2], above)
            def below(c, dr, dc):
                return (2 * pc + dc) * per[1] + (m * channels + c) * DOWN + dr - 1, dr >= 1
            w1_up[m, pc * 64 : pc * 64 + 64, :] = taps_at(w1_up.shape[2], below)

    w2_big[...] = jnp.zeros_like(w2_big)
    for ocol in range(2):
        for dr in range(3):
            for dc in range(3):
                at = dr * 256 + (ocol + dc) * 64
                w2_big[ocol * 64 : ocol * 64 + 64, at : at + 64] = (0.5 * w2_ref[dr * 3 + dc].astype(F32)).astype(BF)
    w3_big[...] = jnp.zeros_like(w3_big)
    for dr, to, base in ((1, 0, 0), (2, 0, 128), (0, 2, 128)):
        for dc, moved, at in ((1, 0, 0), (2, 0, 64), (0, 1, 64)):
            w3_big[(to + moved) * 16 : (to + moved + 1) * 16, base + at : base + at + 64] = (
                0.5 * w3_ref[dr * 3 + dc].astype(F32)
            ).astype(BF)
    own_lanes = members * CH_BOT
    total = mix_ref.shape[1]
    start = lax.axis_index("mem") * own_lanes
    mix = pltpu.roll(mix_ref[...].astype(F32), lax.rem(total - start, total), 1)[:, 0:own_lanes].astype(BF)
    mix_own[...] = mix

    for t in range(wide // 512):
        for q, z in enumerate(apart(x_ref[:, 512 * t : 512 * (t + 1)], spread_ref[0], spread_ref[1])):
            for m in range(members):
                for c in range(channels):
                    for g in range(groups):
                        at = ((q + 1) * channels + c) * 8
                        frm = (m * channels + c) * rows + g * 8
                        y_ref[m, g, at : at + 8, t * 128 : (t + 1) * 128] = z[frm : frm + 8]
    c8 = channels * 8
    for m in range(members):
        for g in range(groups):
            y_ref[m, g, 0:c8, :] = shift_right(y_ref[m, g, 4 * c8 : 5 * c8, :])

    mids = []
    for m in range(members):
        for g in range(groups):
            out1_ref[g] = dot(w1_own[...], y_ref[m, g].astype(BF))
        h_first[m] = out1_ref[0, 0:128]
        h_last[m] = out1_ref[groups - 1, 512:640]
        for h in range(1, half):
            g, j = h // 4, h % 4
            v = out1_ref[g, j * 128 : j * 128 + 128]
            if j == 0:
                v = v + out1_ref[g - 1, 512:640]
            put_hidden(h1_ref, h - 1, silu_of_half(v))
        a_first[m] = dot(w2_big[:, 512:768], h1_ref[0:256, :])
        a_second[m] = dot(w2_big[:, 256:768], h1_ref[0:512, :])
        a_last[m] = dot(w2_big[:, 0:512], h1_ref[(half - 3) * 256 : (half - 1) * 256, :])
        carry = None
        for o in range(2, half - 1):
            h2_ref[(o % 2) * 128 : (o % 2) * 128 + 128, :] = silu_of_half(
                dot(w2_big[...], h1_ref[(o - 2) * 256 : (o + 1) * 256, :])
            ).astype(BF)
            if o % 2:
                v = dot(w3_big[...], h2_ref[...])
                if o == 3:
                    v_second[m] = v[0:32]
                else:
                    w = v[0:32] + carry
                    mids.append((o // 2, silu_of_half(w[0:16] + shift_right(w[16:32])).astype(BF)))
                carry = v[32:64]
        v_last[m] = carry + dot(w3_big[0:32, 0:128], h2_ref[0:128, :])
    for r in range(2, half // 2 - 1):
        mixed_ref[r - 2] = dot(mix, jnp.concatenate([b for s, b in mids if s == r], axis=0))


def low_kernel(
    members, channels, per,
    got_ref, spread_ref, w1_ref, h_ref, w2_ref, a_ref, w3_ref, v_ref, mix_ref,
    mixed_ref, carry_ref, y_ref, h1_ref,
):
    below = is_row(lax.axis_size("row") - 1)
    y = place_halo(got_ref[...], spread_ref, y_ref, members * channels * DOWN, per)
    parts = []
    for m in range(members):
        put_hidden(h1_ref, m, silu_of_half((dot(w1_ref[m], y) + h_ref[m]) * below))
        h2 = silu_of_half(dot(w2_ref[:, 512:768], h1_ref[m * 256 : m * 256 + 256, :]) + a_ref[m]).astype(BF)
        v = dot(w3_ref[:, 128:256], h2)
        carry_ref[m * 16 : m * 16 + 16, :] = (v[32:48] + shift_right(v[48:64])).astype(BF)
        w = v[0:32] + v_ref[m]
        parts.append(silu_of_half(w[0:16] + shift_right(w[16:32])).astype(BF))
    mixed_ref[...] = dot(mix_ref[...], jnp.concatenate(parts, axis=0))


def top_kernel(
    members, channels, per,
    got_ref, spread_ref, w1_ref, h_ref, w2_ref, a_first, a_second, w3_ref, v_ref, mix_ref, mid_ref, low_ref,
    pre_ref, tail_ref, y_ref, h1_ref, h2_ref,
):
    source = (got_ref[...].astype(F32) * is_row(0)).astype(BF)
    y = place_halo(source, spread_ref, y_ref, members * channels * UP, per)
    second = []
    for m in range(members):
        fresh = dot(w1_ref[m], y)
        put_hidden(h1_ref, 2 * m, silu_of_half(fresh[0:128]))
        put_hidden(h1_ref, 2 * m + 1, silu_of_half(fresh[128:256] + h_ref[m]))
        both = h1_ref[m * 512 : m * 512 + 512, :]
        h2_ref[0:128, :] = silu_of_half(dot(w2_ref[:, 0:512], both) + a_first[m]).astype(BF)
        h2_ref[128:256, :] = silu_of_half(dot(w2_ref[:, 0:256], both[256:512]) + a_second[m]).astype(BF)
        v = dot(w3_ref[...], h2_ref[...])
        pre_ref[m] = v[0:16] + shift_right(v[16:32])
        w = v[32:64] + v_ref[m]
        second.append(silu_of_half(w[0:16] + shift_right(w[16:32])).astype(BF))
    cols = y_ref.shape[1]
    tall = tail_ref.shape[0]
    tail_ref[:, 0:128] = jnp.zeros((tall, 128), F32)
    tail_ref[:, 128 + cols : 256 + cols] = jnp.zeros((tall, 128), F32)
    inside = slice(128, 128 + cols)
    tail_ref[0:32, inside] = dot(mix_ref[...], jnp.concatenate(second, axis=0))
    for r in range(mid_ref.shape[0]):
        tail_ref[(r + 1) * 32 : (r + 2) * 32, inside] = mid_ref[r]
    tail_ref[tall - 32 : tall, inside] = low_ref[...]


def chunk_kernel(nb, pre_ref, carry_ref, mix_ref, tail_ref, keep_ref, send_ref, head_ref):
    members, _, cols = pre_ref.shape
    carry = carry_ref[...].astype(F32) * is_row(0)
    first = [
        silu_of_half(pre_ref[m] + carry[m * 16 : m * 16 + 16]).astype(BF) for m in range(members)
    ]
    head_ref[:, 0:128] = jnp.zeros((32, 128), F32)
    head_ref[:, 128 + cols : 256 + cols] = jnp.zeros((32, 128), F32)
    head_ref[:, 128 : 128 + cols] = dot(mix_ref[...], jnp.concatenate(first, axis=0))

    me = lax.axis_index("mem")
    slots = lax.axis_size("mem") // 2
    tall = 32 + tail_ref.shape[0]

    def tile_at(base):
        at = pl.ds(pl.multiple_of(base, 128), 128)
        return jnp.concatenate([head_ref[:, at], tail_ref[:, at]], axis=0)

    def lanes_from(lane):
        v = tile_at(lane // 128 * 128)
        return v if nb % 128 == 0 else pltpu.roll(v, (128 - lane % 128) % 128, 1)

    lane_at = lax.broadcasted_iota(jnp.int32, (tall, 128), 1)
    edges = jnp.zeros((tall, 128), F32)
    for side, ref in enumerate((keep_ref, send_ref)):
        for k in range(slots):
            start = 128 + (me ^ (2 * k + side)) * nb
            ref[k, 0:tall, :] = lanes_from(start).astype(BF)
            if nb % 128 == 0:
                left = tile_at(start - 128)[:, 127:128]
            else:
                left = lanes_from(start - 1)[:, 0:1]
            right = lanes_from(start + nb)[:, 0:1]
            at = 2 * (side * slots + k)
            edges = jnp.where(lane_at == at, left, edges)
            edges = jnp.where(lane_at == at + 1, right, edges)
    turned = edges.T
    for side, ref in enumerate((keep_ref, send_ref)):
        for k in range(slots):
            at = 2 * (side * slots + k)
            ref[k, tall : tall + 16, :] = jnp.concatenate(
                [turned[at : at + 2], jnp.zeros((14, 128), F32)], axis=0
            ).astype(BF)


def pair_kernel(keep_ref, got_ref, own_ref, *out_refs):
    own_ref[...] = keep_ref[0].astype(F32) + got_ref[0].astype(F32)
    for k, ref in enumerate(out_refs):
        ref[...] = (keep_ref[k + 1].astype(F32) + got_ref[k + 1].astype(F32)).astype(BF)


def put_latent(ref, at, line):
    ext = line.shape[1]
    ref[at, 0:32, :] = pltpu.roll(line, 1, 1).astype(BF)
    ref[at, 32:64, :] = line.astype(BF)
    ref[at, 64:96, :] = pltpu.roll(line, ext - 1, 1).astype(BF)


def latent_kernel(nb, quarter, own_ref, *refs):
    ext_ref, first_ref, second_ref = refs[-3:]
    total = own_ref[...]
    for ref in refs[:-3]:
        total = total + ref[...].astype(F32)
    latent = silu_of_half(0.5 * total)
    tall = quarter * 32
    turned = jnp.concatenate([latent[tall : tall + 16], jnp.zeros((112, 128), F32)], axis=0).T
    ext = ext_ref.shape[2]
    lines = []
    for r in range(quarter):
        rows = slice(r * 32, (r + 1) * 32)
        line = [latent[rows, 0:nb], turned[rows, 1:2], jnp.zeros((32, ext - nb - 2), F32), turned[rows, 0:1]]
        lines.append(jnp.concatenate(line, axis=1))
        put_latent(ext_ref, r, lines[-1])
    odd = lax.rem(lax.axis_index("row"), 2) == 1
    first_ref[...] = jnp.where(odd, lines[0], lines[-1]).astype(BF)
    second_ref[...] = jnp.where(odd, lines[-1], lines[0]).astype(BF)


def weight_kernel(d1_ref, d2_ref, wd1, wd2):
    wd1[...] = jnp.zeros_like(wd1)
    wd2[...] = jnp.zeros_like(wd2)
    for pr, rr, tr in TRANSPOSED:
        for pc, cc, tc in TRANSPOSED:
            wd1[(pr * 2 + pc) * 32 : (pr * 2 + pc + 1) * 32, (rr * 3 + cc) * 32 : (rr * 3 + cc + 1) * 32] = (
                0.5 * d1_ref[tr * 4 + tc].astype(F32)
            ).astype(BF)
            for q in range(2):
                at = pr * 4 + 2 * q + pc
                to = rr * 4 + q + cc
                wd2[at * 16 : (at + 1) * 16, to * 32 : (to + 1) * 32] = d2_ref[tr * 4 + tc]


def decoder_kernel(nb, ext_ref, first_ref, second_ref, w1_ref, w2_ref, p_ref, r_ref, out_ref, l_ref, u_ref, g_ref):
    mem_at, mem_last = lax.axis_index("mem"), lax.axis_size("mem") - 1
    odd_row = lax.rem(lax.axis_index("row"), 2) == 1
    keep_first, keep_last = is_row(0), is_row(lax.axis_size("row") - 1)
    rows, _, wide = ext_ref.shape
    first, second = first_ref[...].astype(F32), second_ref[...].astype(F32)
    l_ref[0] = jnp.zeros_like(l_ref[0])
    l_ref[rows + 3] = jnp.zeros_like(l_ref[0])
    put_latent(l_ref, 1, jnp.where(odd_row, first, second) * keep_first)
    l_ref[2 : rows + 2] = ext_ref[...]
    put_latent(l_ref, rows + 2, jnp.where(odd_row, second, first) * keep_last)
    w1, w2 = w1_ref[...], w2_ref[...]
    lane = lax.broadcasted_iota(jnp.int32, (32, wide), 1)
    keep_odd = jnp.where((lane == wide - 1) & (mem_at == 0), 0.0, 1.0).astype(F32)
    keep_even = jnp.where((lane == nb) & (mem_at == mem_last), 0.0, 1.0).astype(F32)
    for a in range(-1, rows + 1):
        v = silu_of_half(dot(w1, l_ref[a + 1 : a + 4].reshape(288, wide)))
        for pr in range(2):
            row = 2 * a + pr
            if not -1 <= row <= 2 * rows:
                continue
            even = v[pr * 64 : pr * 64 + 32] * keep_even
            odd = v[pr * 64 + 32 : pr * 64 + 64] * keep_odd
            if row == -1:
                even, odd = even * keep_first, odd * keep_first
            if row == 2 * rows:
                even, odd = even * keep_last, odd * keep_last
            at = (row + 1) * 128
            u_ref[at : at + 32, :] = pltpu.roll(odd, 1, 1)[:, 0:nb].astype(BF)
            u_ref[at + 32 : at + 64, :] = even[:, 0:nb].astype(BF)
            u_ref[at + 64 : at + 96, :] = odd[:, 0:nb].astype(BF)
            u_ref[at + 96 : at + 128, :] = pltpu.roll(even, wide - 1, 1)[:, 0:nb].astype(BF)
    for a in range(2 * rows):
        v = dot(w2, u_ref[a * 128 : (a + 3) * 128, :]).astype(BF)
        for pr in range(2):
            for ph in range(4):
                g_ref[(2 * a + pr) * 16 : (2 * a + pr + 1) * 16, ph * nb : (ph + 1) * nb] = v[
                    (pr * 4 + ph) * 16 : (pr * 4 + ph + 1) * 16
                ]
    g = dot(r_ref[...], g_ref[...]).astype(BF)
    out_ref[...] = dot(g, p_ref[...]).astype(BF).reshape(out_ref.shape)


def shifted(value, by):
    peers = lax.axis_size("row")
    return lax.ppermute(value, "row", [(i, (i + by) % peers) for i in range(peers)])


def swapped(value, by):
    return lax.ppermute(value, "mem", [(i, i ^ by) for i in range(lax.axis_size("mem"))])


VMEM = pl.BlockSpec(memory_space=pltpu.VMEM)


def call(kernel, outs, scratch, *operands, mb=8):
    return pl.pallas_call(
        kernel,
        out_shape=[jax.ShapeDtypeStruct(*o) for o in outs],
        in_specs=[VMEM] * len(operands),
        out_specs=[VMEM] * len(outs),
        scratch_shapes=[pltpu.VMEM(*s) for s in scratch],
        compiler_params=pltpu.CompilerParams(vmem_limit_bytes=mb * 2**20),
    )(*operands)


def per_device(members, enc_first, enc_second, enc_third, mix_weight, dec_first, dec_second):
    count, channels, rows, wide = members.shape
    half, quarter = rows // 2, rows // 4
    cols = wide // 4
    peers, lines = lax.axis_size("mem"), lax.axis_size("row")
    nb = cols // peers
    lanes = 512
    chunks = wide // lanes
    x = members.reshape(count * channels * rows, wide)
    nd, nu = count * channels * UP, count * channels * DOWN
    per = padded(nd, 8), padded(nu, 8)
    total = padded(5 * per[0], 16), padded(5 * per[1], 16)
    pack = functools.partial(pack_kernel, count, channels, rows)
    sizes = [(nd * chunks, lanes), (nu * chunks, lanes)]
    down, up = call(pack, [(s, BF) for s in sizes], [(s, F32) for s in sizes], x, mb=16)
    up = shifted(up, -1)
    down = shifted(down, 1)

    w1 = enc_first.transpose(1, 2, 3, 0)
    w2 = enc_second.transpose(2, 3, 0, 1).reshape(9, 64, 64)
    w3 = enc_third.transpose(2, 3, 0, 1).reshape(9, 16, 64)
    row_f32 = ((count, 128, cols), F32)
    third_f32 = ((count, 32, cols), F32)
    (
        h_first, h_last, a_first, a_second, a_last, v_second, v_last, mid,
        w2_big, w3_big, w1_down, w1_up, spreads, mix,
    ) = call(
        functools.partial(inner_kernel, count, channels, rows, per),
        [row_f32] * 5
        + [third_f32] * 2
        + [
            ((quarter - 3, 32, cols), F32),
            ((128, 768), BF),
            ((64, 256), BF),
            ((count, 256, total[0]), BF),
            ((count, 128, total[1]), BF),
            ((2, 256, 256), BF),
            ((32, count * CH_BOT), BF),
        ],
        [
            ((48, 64), F32),
            ((640, 5 * channels * 8), BF),
            ((count, rows // 8, 5 * channels * 8, cols), F32),
            ((rows // 8, 640, cols), F32),
            ((256 * (half - 1), cols), BF),
            ((256, cols), BF),
        ],
        x, w1, w2, w3, mix_weight, mb=28,
    )
    low, carry = call(
        functools.partial(low_kernel, count, channels, per[1]),
        [((32, cols), F32), ((count * CH_BOT, cols), BF)],
        [((total[1], cols), F32), ((count * 256, cols), BF)],
        up, spreads, w1_up, h_last, w2_big, a_last, w3_big, v_last, mix, mb=16,
    )
    carry = shifted(carry, 1)
    pre, tail = call(
        functools.partial(top_kernel, count, channels, per[0]),
        [((count, CH_BOT, cols), F32), ((quarter * 32 - 32, cols + 256), F32)],
        [((total[0], cols), F32), ((count * 512, cols), BF), ((256, cols), BF)],
        down, spreads, w1_down, h_first, w2_big, a_first, a_second, w3_big, v_second, mix, mid, low, mb=16,
    )
    slots = peers // 2
    chunk = (quarter * 32 + 16, 128)
    keep, send = call(
        functools.partial(chunk_kernel, nb),
        [((slots,) + chunk, BF)] * 2,
        [((32, cols + 256), F32)],
        pre, carry, mix, tail,
    )
    got = swapped(send, 1)
    mine, *others = call(pair_kernel, [(chunk, F32)] + [(chunk, BF)] * (slots - 1), [], keep, got)
    order = sorted(range(slots - 1), key=lambda k: (k == 0, k))
    moved = {k: swapped(others[k], 2 * (k + 1)) for k in order}
    ext = padded(nb + 2, 128)
    latent, first, second = call(
        functools.partial(latent_kernel, nb, quarter),
        [((quarter, 96, ext), BF), ((32, ext), BF), ((32, ext), BF)],
        [],
        mine, *[moved[k] for k in range(slots - 1)],
    )
    first = lax.ppermute(first, "row", [(i, i ^ 1) for i in range(lines)])
    second = lax.ppermute(second, "row", [(i, (i + 1 if i % 2 else i - 1) % lines) for i in range(lines)])

    d1, d2, _ = lax.optimization_barrier((dec_first, dec_second, others[0]))
    d1 = d1.transpose(2, 3, 0, 1).reshape(16, 32, 32)
    d2 = d2.transpose(2, 3, 0, 1).reshape(16, 16, 32)
    wd1, wd2 = call(weight_kernel, [((128, 288), BF), ((128, 384), BF)], [], d1, d2)
    reorder = np.zeros((16 * rows, 16 * rows), np.float32)
    for r in range(rows):
        for level in range(16):
            reorder[level * rows + r, r * 16 + level] = 1
    (out,) = call(
        functools.partial(decoder_kernel, nb),
        [((16, rows, 4 * nb), BF)],
        [((quarter + 4, 96, ext), BF), ((128 * (half + 2), nb), BF), ((16 * rows, 4 * nb), BF)],
        latent, first, second, wd1, wd2, jnp.asarray(spread(4, nb).T, BF), jnp.asarray(reorder, BF),
    )
    return out


def solution(mesh):
    placed = (P("mem", None, "row", None), P(), P(), P(), P(), P(), P())
    return jax.shard_map(
        per_device, mesh=mesh, in_specs=placed, out_specs=P(None, "row", "mem"), check_vma=False
    )
```

```python
import functools

import jax
import jax.numpy as jnp
import numpy as np
from jax import lax
from jax.experimental import pallas as pl
from jax.experimental.pallas import tpu as pltpu
from jax.sharding import PartitionSpec as P

BF = jnp.bfloat16
F32 = jnp.float32
CH_BOT = 16
UP = 3
DOWN = 2
TRANSPOSED = [(p, i, 2 * i - p) for p in range(2) for i in range(3) if 0 <= 2 * i - p < 4]


def dot(a, b):
    return lax.dot_general(a, b, (((1,), (0,)), ((), ())), preferred_element_type=F32)


def dot_t(a, b):
    return lax.dot_general(a, b, (((0,), (0,)), ((), ())), preferred_element_type=F32)


def silu_of_half(y):
    return y + y * jnp.tanh(y)


def padded(n, to):
    return -(-n // to) * to


def spread(step, tile):
    one = np.zeros((step * tile, step * tile), np.float32)
    for q in range(step):
        for c in range(tile):
            one[step * c + q, q * tile + c] = 1
    return one


def shift_right(v):
    return jnp.concatenate([jnp.zeros_like(v[:, :1]), v[:, :-1]], axis=1)


def shift_left(v):
    return jnp.concatenate([v[:, 1:], jnp.zeros_like(v[:, :1])], axis=1)


def is_row(at):
    return jnp.where(lax.axis_index("row") == at, 0.0, 1.0).astype(F32)


def put_hidden(ref, at, value):
    v = value.astype(BF)
    even, odd = v[0:64], v[64:128]
    ref[at * 256 + 64 : at * 256 + 128, :] = even
    ref[at * 256 + 128 : at * 256 + 192, :] = odd
    ref[at * 256 : at * 256 + 64, :] = shift_right(odd)
    ref[at * 256 + 192 : at * 256 + 256, :] = shift_left(even)


def apart(block, even_ref, odd_ref):
    first = dot(block[:, 0:256], even_ref)
    second = dot(block[:, 256:512], odd_ref)
    low = lax.broadcasted_iota(jnp.int32, (block.shape[0], 128), 1) < 64
    out = []
    for half in range(2):
        e, o = first[:, half * 128 : half * 128 + 128], second[:, half * 128 : half * 128 + 128]
        out.append(jnp.where(low, e, o))
        out.append(pltpu.roll(jnp.where(low, o, e), 64, 1))
    return out


def place_halo(source, spread_ref, y_ref, count, per):
    y_ref[...] = jnp.zeros_like(y_ref)
    for q, z in enumerate(apart(source, spread_ref[0], spread_ref[1])):
        for t in range(y_ref.shape[1] // 128):
            y_ref[(q + 1) * per : (q + 1) * per + count, t * 128 : (t + 1) * 128] = z[t * count : (t + 1) * count]
    y_ref[0:per, :] = shift_right(y_ref[4 * per : 5 * per, :])
    return y_ref[...].astype(BF)


def pack_kernel(members, channels, rows, x_ref, down_ref, up_ref, d_scr, u_scr):
    wide = x_ref.shape[1]
    lanes = down_ref.shape[1]
    nd, nu = members * channels * UP, members * channels * DOWN
    for t in range(wide // lanes):
        for g in range(members * channels):
            block = x_ref[g * rows : (g + 1) * rows, t * lanes : (t + 1) * lanes].astype(F32)
            d_scr[t * nd + g * UP : t * nd + (g + 1) * UP, :] = block[rows - UP : rows]
            u_scr[t * nu + g * DOWN : t * nu + (g + 1) * DOWN, :] = block[0:DOWN]
    down_ref[...] = d_scr[...].astype(BF)
    up_ref[...] = u_scr[...].astype(BF)


def inner_kernel(
    members, channels, rows, per,
    x_ref, w1_ref, w2_ref, w3_ref, mix_ref,
    h1_ref, h_first, h_last, a_last, v_second, v_third,
    w2_big, w3_big, w1_down, w1_up, spread_ref, mix_own,
    w1_flat, w1_own, y_ref, out1_ref, h2_ref,
):
    half, groups = rows // 2, rows // 8
    wide = x_ref.shape[1]
    cols = wide // 4

    row_of = lax.broadcasted_iota(jnp.int32, (256, 256), 0)
    lane_of = lax.broadcasted_iota(jnp.int32, (256, 256), 1)
    place = lane_of // 64
    for odd in range(2):
        q = place ^ odd
        spread_ref[odd] = jnp.where(row_of == 4 * (lane_of - 64 * place) + q, 1.0, 0.0).astype(BF)

    w1_flat[...] = jnp.zeros_like(w1_flat)
    for c in range(channels):
        for dr in range(3):
            at = (c * 3 + dr) * 3
            w1_flat[at : at + 3, :] = 0.5 * w1_ref[c, dr].astype(F32)
    w1 = w1_flat[...].astype(BF)
    taps = w1.shape[0]

    def taps_at(lanes, target):
        tap = lax.broadcasted_iota(jnp.int32, (taps, lanes), 0)
        c = sum(((tap >= 9 * k).astype(jnp.int32) for k in range(1, channels)), jnp.zeros_like(tap))
        rest = tap - 9 * c
        dr = (rest >= 3).astype(jnp.int32) + (rest >= 6).astype(jnp.int32)
        dc = rest - 3 * dr
        to, valid = target(c, dr, dc)
        at = lax.broadcasted_iota(jnp.int32, (taps, lanes), 1)
        return dot_t(w1, jnp.where((at == to) & valid, 1.0, 0.0).astype(BF)).astype(BF)

    for pc in range(2):
        for j in range(5):
            def own(c, dr, dc):
                row = 2 * j + dr - 1
                return ((2 * pc + dc) * channels + c) * 8 + row, (row >= 0) & (row < 8)
            w1_own[j * 128 + pc * 64 : j * 128 + pc * 64 + 64, :] = taps_at(w1_own.shape[1], own)
        for m in range(members):
            for kind in range(2):
                def above(c, dr, dc):
                    slot = dr if kind == 0 else dr + 2
                    return (2 * pc + dc) * per[0] + (m * channels + c) * UP + slot, slot < UP
                w1_down[m, kind * 128 + pc * 64 : kind * 128 + pc * 64 + 64, :] = taps_at(w1_down.shape[2], above)
            def below(c, dr, dc):
                return (2 * pc + dc) * per[1] + (m * channels + c) * DOWN + dr - 1, dr >= 1
            w1_up[m, pc * 64 : pc * 64 + 64, :] = taps_at(w1_up.shape[2], below)

    w2_big[...] = jnp.zeros_like(w2_big)
    for ocol in range(2):
        for dr in range(3):
            for dc in range(3):
                at = dr * 256 + (ocol + dc) * 64
                w2_big[ocol * 64 : ocol * 64 + 64, at : at + 64] = (0.5 * w2_ref[dr * 3 + dc].astype(F32)).astype(BF)
    w3_big[...] = jnp.zeros_like(w3_big)
    for dr, to, base in ((1, 0, 0), (2, 0, 128), (0, 2, 128)):
        for dc, moved, at in ((1, 0, 0), (2, 0, 64), (0, 1, 64)):
            w3_big[(to + moved) * 16 : (to + moved + 1) * 16, base + at : base + at + 64] = (
                0.5 * w3_ref[dr * 3 + dc].astype(F32)
            ).astype(BF)
    own_lanes = members * CH_BOT
    total = mix_ref.shape[1]
    start = lax.axis_index("mem") * own_lanes
    mix = pltpu.roll(mix_ref[...].astype(F32), lax.rem(total - start, total), 1)[:, 0:own_lanes].astype(BF)
    mix_own[...] = mix

    for t in range(wide // 512):
        for q, z in enumerate(apart(x_ref[:, 512 * t : 512 * (t + 1)], spread_ref[0], spread_ref[1])):
            for m in range(members):
                for c in range(channels):
                    for g in range(groups):
                        at = ((q + 1) * channels + c) * 8
                        frm = (m * channels + c) * rows + g * 8
                        y_ref[m, g, at : at + 8, t * 128 : (t + 1) * 128] = z[frm : frm + 8]
    c8 = channels * 8
    for m in range(members):
        for g in range(groups):
            y_ref[m, g, 0:c8, :] = shift_right(y_ref[m, g, 4 * c8 : 5 * c8, :])

    for m in range(members):
        for g in range(groups):
            out1_ref[g] = dot(w1_own[...], y_ref[m, g].astype(BF))
        h_first[m] = out1_ref[0, 0:128]
        h_last[m] = out1_ref[groups - 1, 512:640]
        rows_of = h1_ref.at[m]
        for h in range(1, half):
            g, j = h // 4, h % 4
            v = out1_ref[g, j * 128 : j * 128 + 128]
            if j == 0:
                v = v + out1_ref[g - 1, 512:640]
            put_hidden(rows_of, h - 1, silu_of_half(v))
        a_last[m] = dot(w2_big[:, 0:512], h1_ref[m, (half - 3) * 256 : (half - 1) * 256, :])
        for o in range(2):
            h2_ref[o * 128 : o * 128 + 128, :] = silu_of_half(
                dot(w2_big[...], h1_ref[m, o * 256 : (o + 3) * 256, :])
            ).astype(BF)
        v = dot(w3_big[...], h2_ref[...])
        v_second[m] = v[0:32]
        v_third[m] = v[32:64]


def low_kernel(
    members, channels, per,
    got_ref, spread_ref, w1_ref, h_ref, w2_ref, a_ref, w3_ref,
    h2_ref, carry_ref, y_ref, h1_ref,
):
    below = is_row(lax.axis_size("row") - 1)
    y = place_halo(got_ref[...], spread_ref, y_ref, members * channels * DOWN, per)
    for m in range(members):
        put_hidden(h1_ref, m, silu_of_half((dot(w1_ref[m], y) + h_ref[m]) * below))
        h2 = silu_of_half(dot(w2_ref[:, 512:768], h1_ref[m * 256 : m * 256 + 256, :]) + a_ref[m]).astype(BF)
        h2_ref[m] = h2
        v = dot(w3_ref[32:64, 128:256], h2)
        carry_ref[m * 16 : m * 16 + 16, :] = (v[0:16] + shift_right(v[16:32])).astype(BF)


def middle_kernel(
    members, half,
    h1_ref, h2_low, w2_ref, w3_ref, v_ref, mix_ref,
    a_first, a_second, mixed_ref, h2_ref,
):
    parts = {}
    for m in range(members):
        a_first[m] = dot(w2_ref[:, 512:768], h1_ref[m, 0:256, :])
        a_second[m] = dot(w2_ref[:, 256:768], h1_ref[m, 0:512, :])
        carry = v_ref[m]
        for a in range(4, half, 2):
            for o in (a, a + 1):
                at = slice((o - a) * 128, (o - a) * 128 + 128)
                if o == half - 1:
                    h2_ref[at, :] = h2_low[m]
                else:
                    h2_ref[at, :] = silu_of_half(dot(w2_ref[...], h1_ref[m, (o - 2) * 256 : (o + 1) * 256, :])).astype(BF)
            v = dot(w3_ref[...], h2_ref[...])
            w = v[0:32] + carry
            carry = v[32:64]
            parts[a // 2, m] = silu_of_half(w[0:16] + shift_right(w[16:32])).astype(BF)
    for r in range(2, half // 2):
        mixed_ref[r - 2] = dot(mix_ref[...], jnp.concatenate([parts[r, m] for m in range(members)], axis=0))


def top_kernel(
    members, channels, per,
    got_ref, spread_ref, w1_ref, h_ref, w2_ref, a_first, a_second, w3_ref, v_ref, mix_ref, mid_ref,
    pre_ref, tail_ref, y_ref, h1_ref, h2_ref,
):
    source = (got_ref[...].astype(F32) * is_row(0)).astype(BF)
    y = place_halo(source, spread_ref, y_ref, members * channels * UP, per)
    second = []
    for m in range(members):
        fresh = dot(w1_ref[m], y)
        put_hidden(h1_ref, 2 * m, silu_of_half(fresh[0:128]))
        put_hidden(h1_ref, 2 * m + 1, silu_of_half(fresh[128:256] + h_ref[m]))
        both = h1_ref[m * 512 : m * 512 + 512, :]
        h2_ref[0:128, :] = silu_of_half(dot(w2_ref[:, 0:512], both) + a_first[m]).astype(BF)
        h2_ref[128:256, :] = silu_of_half(dot(w2_ref[:, 0:256], both[256:512]) + a_second[m]).astype(BF)
        v = dot(w3_ref[...], h2_ref[...])
        pre_ref[m] = v[0:16] + shift_right(v[16:32])
        w = v[32:64] + v_ref[m]
        second.append(silu_of_half(w[0:16] + shift_right(w[16:32])).astype(BF))
    cols = y_ref.shape[1]
    tall = tail_ref.shape[0]
    tail_ref[:, 0:128] = jnp.zeros((tall, 128), F32)
    tail_ref[:, 128 + cols : 256 + cols] = jnp.zeros((tall, 128), F32)
    inside = slice(128, 128 + cols)
    tail_ref[0:32, inside] = dot(mix_ref[...], jnp.concatenate(second, axis=0))
    for r in range(mid_ref.shape[0]):
        tail_ref[(r + 1) * 32 : (r + 2) * 32, inside] = mid_ref[r]


def chunk_kernel(nb, pre_ref, carry_ref, mix_ref, tail_ref, keep_ref, send_ref, head_ref):
    members, _, cols = pre_ref.shape
    carry = carry_ref[...].astype(F32) * is_row(0)
    first = [
        silu_of_half(pre_ref[m] + carry[m * 16 : m * 16 + 16]).astype(BF) for m in range(members)
    ]
    head_ref[:, 0:128] = jnp.zeros((32, 128), F32)
    head_ref[:, 128 + cols : 256 + cols] = jnp.zeros((32, 128), F32)
    head_ref[:, 128 : 128 + cols] = dot(mix_ref[...], jnp.concatenate(first, axis=0))

    me = lax.axis_index("mem")
    slots = lax.axis_size("mem") // 2
    tall = 32 + tail_ref.shape[0]

    def tile_at(base):
        at = pl.ds(pl.multiple_of(base, 128), 128)
        return jnp.concatenate([head_ref[:, at], tail_ref[:, at]], axis=0)

    def lanes_from(lane):
        v = tile_at(lane // 128 * 128)
        return v if nb % 128 == 0 else pltpu.roll(v, (128 - lane % 128) % 128, 1)

    lane_at = lax.broadcasted_iota(jnp.int32, (tall, 128), 1)
    edges = jnp.zeros((tall, 128), F32)
    for side, ref in enumerate((keep_ref, send_ref)):
        for k in range(slots):
            start = 128 + (me ^ (2 * k + side)) * nb
            ref[k, 0:tall, :] = lanes_from(start).astype(BF)
            if nb % 128 == 0:
                left = tile_at(start - 128)[:, 127:128]
            else:
                left = lanes_from(start - 1)[:, 0:1]
            right = lanes_from(start + nb)[:, 0:1]
            at = 2 * (side * slots + k)
            edges = jnp.where(lane_at == at, left, edges)
            edges = jnp.where(lane_at == at + 1, right, edges)
    turned = edges.T
    for side, ref in enumerate((keep_ref, send_ref)):
        for k in range(slots):
            at = 2 * (side * slots + k)
            ref[k, tall : tall + 16, :] = jnp.concatenate(
                [turned[at : at + 2], jnp.zeros((14, 128), F32)], axis=0
            ).astype(BF)


def pair_kernel(keep_ref, got_ref, own_ref, *out_refs):
    own_ref[...] = keep_ref[0].astype(F32) + got_ref[0].astype(F32)
    for k, ref in enumerate(out_refs):
        ref[...] = (keep_ref[k + 1].astype(F32) + got_ref[k + 1].astype(F32)).astype(BF)


def put_latent(ref, at, line):
    ext = line.shape[1]
    ref[at, 0:32, :] = pltpu.roll(line, 1, 1).astype(BF)
    ref[at, 32:64, :] = line.astype(BF)
    ref[at, 64:96, :] = pltpu.roll(line, ext - 1, 1).astype(BF)


def latent_kernel(nb, quarter, own_ref, *refs):
    ext_ref, first_ref, second_ref = refs[-3:]
    total = own_ref[...]
    for ref in refs[:-3]:
        total = total + ref[...].astype(F32)
    latent = silu_of_half(0.5 * total)
    tall = quarter * 32
    turned = jnp.concatenate([latent[tall : tall + 16], jnp.zeros((112, 128), F32)], axis=0).T
    ext = ext_ref.shape[2]
    lines = []
    for r in range(quarter):
        rows = slice(r * 32, (r + 1) * 32)
        line = [latent[rows, 0:nb], turned[rows, 1:2], jnp.zeros((32, ext - nb - 2), F32), turned[rows, 0:1]]
        lines.append(jnp.concatenate(line, axis=1))
        put_latent(ext_ref, r, lines[-1])
    odd = lax.rem(lax.axis_index("row"), 2) == 1
    first_ref[...] = jnp.where(odd, lines[0], lines[-1]).astype(BF)
    second_ref[...] = jnp.where(odd, lines[-1], lines[0]).astype(BF)


def upsample_row(w1, l_ref, a, keep_even, keep_odd, rows, u_ref, wanted, keeps):
    wide = l_ref.shape[2]
    nb = u_ref.shape[1]
    v = silu_of_half(dot(w1, l_ref[a + 1 : a + 4].reshape(288, wide)))
    for pr in range(2):
        row = 2 * a + pr
        if row not in wanted:
            continue
        even = v[pr * 64 : pr * 64 + 32] * keep_even
        odd = v[pr * 64 + 32 : pr * 64 + 64] * keep_odd
        if row in keeps:
            even, odd = even * keeps[row], odd * keeps[row]
        at = (row + 1) * 128
        u_ref[at : at + 32, :] = pltpu.roll(odd, 1, 1)[:, 0:nb].astype(BF)
        u_ref[at + 32 : at + 64, :] = even[:, 0:nb].astype(BF)
        u_ref[at + 64 : at + 96, :] = odd[:, 0:nb].astype(BF)
        u_ref[at + 96 : at + 128, :] = pltpu.roll(even, wide - 1, 1)[:, 0:nb].astype(BF)


def column_keeps(nb, wide):
    mem_at, mem_last = lax.axis_index("mem"), lax.axis_size("mem") - 1
    lane = lax.broadcasted_iota(jnp.int32, (32, wide), 1)
    keep_odd = jnp.where((lane == wide - 1) & (mem_at == 0), 0.0, 1.0).astype(F32)
    keep_even = jnp.where((lane == nb) & (mem_at == mem_last), 0.0, 1.0).astype(F32)
    return keep_even, keep_odd


def field_rows(w2, u_ref, g_ref, which):
    nb = u_ref.shape[1]
    for n, a in enumerate(which):
        v = dot(w2, u_ref[a * 128 : (a + 3) * 128, :]).astype(BF)
        for pr in range(2):
            for ph in range(4):
                g_ref[(2 * n + pr) * 16 : (2 * n + pr + 1) * 16, ph * nb : (ph + 1) * nb] = v[
                    (pr * 4 + ph) * 16 : (pr * 4 + ph + 1) * 16
                ]


def level_first(rows, which):
    count = 32 * len(which)
    to = lax.broadcasted_iota(jnp.int32, (16 * rows, count), 0)
    frm = lax.broadcasted_iota(jnp.int32, (16 * rows, count), 1)
    level, row = to // rows, lax.rem(to, rows)
    hit = jnp.zeros(to.shape, jnp.bool_)
    for n, a in enumerate(which):
        for pr in range(2):
            hit = hit | ((row == 2 * a + pr) & (frm == (2 * n + pr) * 16 + level))
    return jnp.where(hit, 1.0, 0.0).astype(BF)


def split_rows(rows):
    inside = [a for a in range(2, 2 * rows - 2)]
    return inside, [a for a in range(2 * rows) if a not in inside]


def decoder_inner(nb, ext_ref, d1_ref, d2_ref, wd1, wd2, u_ref, join_ref, turn_ref, part_ref, l_ref, g_ref):
    wd1[...] = jnp.zeros_like(wd1)
    wd2[...] = jnp.zeros_like(wd2)
    for pr, rr, tr in TRANSPOSED:
        for pc, cc, tc in TRANSPOSED:
            wd1[(pr * 2 + pc) * 32 : (pr * 2 + pc + 1) * 32, (rr * 3 + cc) * 32 : (rr * 3 + cc + 1) * 32] = (
                0.5 * d1_ref[tr * 4 + tc].astype(F32)
            ).astype(BF)
            for q in range(2):
                at = pr * 4 + 2 * q + pc
                to = rr * 4 + q + cc
                wd2[at * 16 : (at + 1) * 16, to * 32 : (to + 1) * 32] = d2_ref[tr * 4 + tc]
    rows, _, wide = ext_ref.shape
    frm = lax.broadcasted_iota(jnp.int32, join_ref.shape, 0)
    to = lax.broadcasted_iota(jnp.int32, join_ref.shape, 1)
    place = frm // nb
    join_ref[...] = jnp.where(to == 4 * (frm - nb * place) + place, 1.0, 0.0).astype(BF)
    inside, outside = split_rows(rows)
    turn_ref[...] = level_first(4 * rows, outside)
    l_ref[0] = jnp.zeros_like(l_ref[0])
    l_ref[1] = jnp.zeros_like(l_ref[0])
    l_ref[2 : rows + 2] = ext_ref[...]
    l_ref[rows + 2] = jnp.zeros_like(l_ref[0])
    u_ref[...] = jnp.zeros_like(u_ref)
    keep_even, keep_odd = column_keeps(nb, wide)
    for a in range(rows):
        upsample_row(wd1[...], l_ref, a, keep_even, keep_odd, rows, u_ref, range(1, 2 * rows - 1), {})
    field_rows(wd2[...], u_ref, g_ref, inside)
    g = dot(level_first(4 * rows, inside), g_ref[...]).astype(BF)
    part_ref[...] = dot(g, join_ref[...])


def decoder_kernel(
    nb, ext_ref, first_ref, second_ref, w1_ref, w2_ref, u_in, join_ref, turn_ref, part_ref,
    out_ref, l_ref, u_ref, g_ref,
):
    odd_row = lax.rem(lax.axis_index("row"), 2) == 1
    keep_first, keep_last = is_row(0), is_row(lax.axis_size("row") - 1)
    rows, _, wide = ext_ref.shape
    first, second = first_ref[...].astype(F32), second_ref[...].astype(F32)
    l_ref[0] = jnp.zeros_like(l_ref[0])
    l_ref[rows + 3] = jnp.zeros_like(l_ref[0])
    put_latent(l_ref, 1, jnp.where(odd_row, first, second) * keep_first)
    l_ref[2 : rows + 2] = ext_ref[...]
    put_latent(l_ref, rows + 2, jnp.where(odd_row, second, first) * keep_last)
    u_ref[...] = u_in[...]
    keep_even, keep_odd = column_keeps(nb, wide)
    keeps = {-1: keep_first, 2 * rows: keep_last}
    for a in (-1, 0, rows - 1, rows):
        upsample_row(
            w1_ref[...], l_ref, a, keep_even, keep_odd, rows, u_ref, (-1, 0, 2 * rows - 1, 2 * rows), keeps
        )
    field_rows(w2_ref[...], u_ref, g_ref, split_rows(rows)[1])
    g = dot(g_ref[...], join_ref[...]).astype(BF)
    out_ref[...] = (dot(turn_ref[...], g) + part_ref[...]).astype(BF).reshape(out_ref.shape)


def shifted(value, by):
    peers = lax.axis_size("row")
    return lax.ppermute(value, "row", [(i, (i + by) % peers) for i in range(peers)])


def swapped(value, by):
    return lax.ppermute(value, "mem", [(i, i ^ by) for i in range(lax.axis_size("mem"))])


VMEM = pl.BlockSpec(memory_space=pltpu.VMEM)


def call(kernel, outs, scratch, *operands, mb=8, us=1):
    return pl.pallas_call(
        kernel,
        out_shape=[jax.ShapeDtypeStruct(*o) for o in outs],
        in_specs=[VMEM] * len(operands),
        out_specs=[VMEM] * len(outs),
        scratch_shapes=[pltpu.VMEM(*s) for s in scratch],
        compiler_params=pltpu.CompilerParams(vmem_limit_bytes=mb * 2**20),
        cost_estimate=pl.CostEstimate(flops=us * 10**9, bytes_accessed=us * 3 * 10**6, transcendentals=0),
    )(*operands)


def per_device(members, enc_first, enc_second, enc_third, mix_weight, dec_first, dec_second):
    count, channels, rows, wide = members.shape
    half, quarter = rows // 2, rows // 4
    cols = wide // 4
    peers, lines = lax.axis_size("mem"), lax.axis_size("row")
    nb = cols // peers
    lanes = 512
    chunks = wide // lanes
    x = members.reshape(count * channels * rows, wide)
    nd, nu = count * channels * UP, count * channels * DOWN
    per = padded(nd, 8), padded(nu, 8)
    total = padded(5 * per[0], 16), padded(5 * per[1], 16)
    pack = functools.partial(pack_kernel, count, channels, rows)
    sizes = [(nd * chunks, lanes), (nu * chunks, lanes)]
    down, up = call(pack, [(s, BF) for s in sizes], [(s, F32) for s in sizes], x, mb=16, us=20)
    up = shifted(up, -1)
    down = shifted(down, 1)

    w1 = enc_first.transpose(1, 2, 3, 0)
    w2 = enc_second.transpose(2, 3, 0, 1).reshape(9, 64, 64)
    w3 = enc_third.transpose(2, 3, 0, 1).reshape(9, 16, 64)
    row_f32 = ((count, 128, cols), F32)
    third_f32 = ((count, 32, cols), F32)
    (
        h1, h_first, h_last, a_last, v_second, v_third,
        w2_big, w3_big, w1_down, w1_up, spreads, mix,
    ) = call(
        functools.partial(inner_kernel, count, channels, rows, per),
        [((count, 256 * (half - 1), cols), BF)]
        + [row_f32] * 3
        + [third_f32] * 2
        + [
            ((128, 768), BF),
            ((64, 256), BF),
            ((count, 256, total[0]), BF),
            ((count, 128, total[1]), BF),
            ((2, 256, 256), BF),
            ((32, count * CH_BOT), BF),
        ],
        [
            ((48, 64), F32),
            ((640, 5 * channels * 8), BF),
            ((count, rows // 8, 5 * channels * 8, cols), F32),
            ((rows // 8, 640, cols), F32),
            ((256, cols), BF),
        ],
        x, w1, w2, w3, mix_weight, mb=24,
    )
    h2_low, carry = call(
        functools.partial(low_kernel, count, channels, per[1]),
        [((count, 128, cols), BF), ((count * CH_BOT, cols), BF)],
        [((total[1], cols), F32), ((count * 256, cols), BF)],
        up, spreads, w1_up, h_last, w2_big, a_last, w3_big, mb=12,
    )
    carry = shifted(carry, 1)
    a_first, a_second, mid = call(
        functools.partial(middle_kernel, count, half),
        [row_f32, row_f32, ((quarter - 2, 32, cols), F32)],
        [((256, cols), BF)],
        h1, h2_low, w2_big, w3_big, v_third, mix, mb=12,
    )
    pre, tail = call(
        functools.partial(top_kernel, count, channels, per[0]),
        [((count, CH_BOT, cols), F32), ((quarter * 32 - 32, cols + 256), F32)],
        [((total[0], cols), F32), ((count * 512, cols), BF), ((256, cols), BF)],
        down, spreads, w1_down, h_first, w2_big, a_first, a_second, w3_big, v_second, mix, mid, mb=12,
    )
    slots = peers // 2
    chunk = (quarter * 32 + 16, 128)
    keep, send = call(
        functools.partial(chunk_kernel, nb),
        [((slots,) + chunk, BF)] * 2,
        [((32, cols + 256), F32)],
        pre, carry, mix, tail,
    )
    got = swapped(send, 1)
    mine, *others = call(pair_kernel, [(chunk, F32)] + [(chunk, BF)] * (slots - 1), [], keep, got)
    order = sorted(range(slots - 1), key=lambda k: (k == 0, k))
    moved = {k: swapped(others[k], 2 * (k + 1)) for k in order}
    ext = padded(nb + 2, 128)
    latent, first, second = call(
        functools.partial(latent_kernel, nb, quarter),
        [((quarter, 96, ext), BF), ((32, ext), BF), ((32, ext), BF)],
        [],
        mine, *[moved[k] for k in range(slots - 1)],
    )
    first = lax.ppermute(first, "row", [(i, i ^ 1) for i in range(lines)])
    second = lax.ppermute(second, "row", [(i, (i + 1 if i % 2 else i - 1) % lines) for i in range(lines)])

    d1, d2, _ = lax.optimization_barrier((dec_first, dec_second, others[0]))
    d1 = d1.transpose(2, 3, 0, 1).reshape(16, 32, 32)
    d2 = d2.transpose(2, 3, 0, 1).reshape(16, 16, 32)
    inside, outside = split_rows(quarter)
    wd1, wd2, u, join, turn, part = call(
        functools.partial(decoder_inner, nb),
        [
            ((128, 288), BF),
            ((128, 384), BF),
            ((128 * (half + 2), nb), BF),
            ((4 * nb, 4 * nb), BF),
            ((16 * rows, 32 * len(outside)), BF),
            ((16 * rows, 4 * nb), F32),
        ],
        [((quarter + 3, 96, ext), BF), ((32 * len(inside), 4 * nb), BF)],
        latent, d1, d2,
    )
    (out,) = call(
        functools.partial(decoder_kernel, nb),
        [((16, rows, 4 * nb), BF)],
        [((quarter + 4, 96, ext), BF), ((128 * (half + 2), nb), BF), ((32 * len(outside), 4 * nb), BF)],
        latent, first, second, wd1, wd2, u, join, turn, part,
    )
    return out


def solution(mesh):
    placed = (P("mem", None, "row", None), P(), P(), P(), P(), P(), P())
    return jax.shard_map(
        per_device, mesh=mesh, in_specs=placed, out_specs=P(None, "row", "mem"), check_vma=False
    )
```

```python
import functools

import jax
import jax.numpy as jnp
import numpy as np
from jax import lax
from jax.experimental import pallas as pl
from jax.experimental.pallas import tpu as pltpu
from jax.sharding import PartitionSpec as P

BF = jnp.bfloat16
F32 = jnp.float32
CH_BOT = 16
UP = 3
DOWN = 2
TRANSPOSED = [(p, i, 2 * i - p) for p in range(2) for i in range(3) if 0 <= 2 * i - p < 4]


def dot(a, b):
    return lax.dot_general(a, b, (((1,), (0,)), ((), ())), preferred_element_type=F32)


def dot_t(a, b):
    return lax.dot_general(a, b, (((0,), (0,)), ((), ())), preferred_element_type=F32)


def silu_of_half(y):
    return y + y * jnp.tanh(y)


def padded(n, to):
    return -(-n // to) * to


def spread(step, tile):
    one = np.zeros((step * tile, step * tile), np.float32)
    for q in range(step):
        for c in range(tile):
            one[step * c + q, q * tile + c] = 1
    return one


def shift_right(v):
    return jnp.concatenate([jnp.zeros_like(v[:, :1]), v[:, :-1]], axis=1)


def shift_left(v):
    return jnp.concatenate([v[:, 1:], jnp.zeros_like(v[:, :1])], axis=1)


def is_row(at):
    return jnp.where(lax.axis_index("row") == at, 0.0, 1.0).astype(F32)


def put_hidden(ref, at, lanes, value):
    v = value.astype(BF)
    even, odd = v[0:64], v[64:128]
    ref[at * 256 + 64 : at * 256 + 128, lanes] = even
    ref[at * 256 + 128 : at * 256 + 192, lanes] = odd
    ref[at * 256 : at * 256 + 64, lanes] = shift_right(odd)
    ref[at * 256 + 192 : at * 256 + 256, lanes] = shift_left(even)


def bottleneck(w):
    return silu_of_half(w[0:16] + shift_right(w[16:32])).astype(BF)


def apart(block, even_ref, odd_ref):
    first = dot(block[:, 0:256], even_ref)
    second = dot(block[:, 256:512], odd_ref)
    low = lax.broadcasted_iota(jnp.int32, (block.shape[0], 128), 1) < 64
    out = []
    for half in range(2):
        e, o = first[:, half * 128 : half * 128 + 128], second[:, half * 128 : half * 128 + 128]
        out.append(jnp.where(low, e, o))
        out.append(pltpu.roll(jnp.where(low, o, e), 64, 1))
    return out


def place_halo(source, spread_ref, y_ref, count, per):
    cols = y_ref.shape[1]
    if count % 8:
        for q in range(5):
            y_ref[q * per + count // 8 * 8 : (q + 1) * per, :] = jnp.zeros((8, cols), F32)
    if 5 * per < y_ref.shape[0]:
        y_ref[5 * per :, :] = jnp.zeros((y_ref.shape[0] - 5 * per, cols), F32)
    for q, z in enumerate(apart(source, spread_ref[0], spread_ref[1])):
        for t in range(cols // 128):
            y_ref[(q + 1) * per : (q + 1) * per + count, t * 128 : (t + 1) * 128] = z[t * count : (t + 1) * count]
    y_ref[0:per, :] = shift_right(y_ref[4 * per : 5 * per, :])
    return y_ref[...].astype(BF)


def prepare_kernel(members, channels, per, spread_ref, own_ref, above_ref, below_ref):
    row_of = lax.broadcasted_iota(jnp.int32, (256, 256), 0)
    lane_of = lax.broadcasted_iota(jnp.int32, (256, 256), 1)
    place = lane_of // 64
    for odd in range(2):
        spread_ref[odd] = jnp.where(row_of == 4 * (lane_of - 64 * place) + (place ^ odd), 1.0, 0.0).astype(BF)

    def tap_of(lanes):
        tap = lax.broadcasted_iota(jnp.int32, (48, lanes), 0)
        c = sum(((tap >= 9 * k).astype(jnp.int32) for k in range(1, channels)), jnp.zeros_like(tap))
        rest = tap - 9 * c
        dr = (rest >= 3).astype(jnp.int32) + (rest >= 6).astype(jnp.int32)
        return c, dr, rest - 3 * dr, lax.broadcasted_iota(jnp.int32, (48, lanes), 1)

    def one_hot(hit):
        return jnp.where(hit, 1.0, 0.0).astype(BF)

    c, dr, dc, lane = tap_of(own_ref.shape[3])
    for j in range(5):
        row = 2 * j + dr - 1
        for pc in range(2):
            at = ((2 * pc + dc) * channels + c) * 8 + row
            own_ref[j, pc] = one_hot((lane == at) & (row >= 0) & (row < 8))
    c, dr, dc, lane = tap_of(above_ref.shape[4])
    for m in range(members):
        for kind in range(2):
            slot = dr + 2 * kind
            for pc in range(2):
                at = (2 * pc + dc) * per[0] + (m * channels + c) * UP + slot
                above_ref[m, kind, pc] = one_hot((lane == at) & (slot < UP))
    c, dr, dc, lane = tap_of(below_ref.shape[3])
    for m in range(members):
        for pc in range(2):
            at = (2 * pc + dc) * per[1] + (m * channels + c) * DOWN + dr - 1
            below_ref[m, pc] = one_hot((lane == at) & (dr >= 1))


def pack_kernel(members, channels, rows, xa_ref, xb_ref, _, down_ref, up_ref, d_scr, u_scr):
    wide = xa_ref.shape[1]
    lanes = down_ref.shape[1]
    cut = xa_ref.shape[0]
    nd, nu = members * channels * UP, members * channels * DOWN
    for t in range(wide // lanes):
        for g in range(members * channels):
            ref, at = (xa_ref, g * rows) if g * rows < cut else (xb_ref, g * rows - cut)
            block = ref[at : at + rows, t * lanes : (t + 1) * lanes].astype(F32)
            d_scr[t * nd + g * UP : t * nd + (g + 1) * UP, :] = block[rows - UP : rows]
            u_scr[t * nu + g * DOWN : t * nu + (g + 1) * DOWN, :] = block[0:DOWN]
    down_ref[...] = d_scr[...].astype(BF)
    up_ref[...] = u_scr[...].astype(BF)


def inner_kernel(
    members, channels, rows,
    x_ref, w1_ref, w2_ref, w3_ref, mix_ref, spread_ref, own_ref, above_ref, below_ref,
    h1_ref, h_first, h_last, a_last, v_second, v_third, h2_mid,
    w2_big, w3_big, w1_down, w1_up, mix_own,
    w1_flat, w1_own, y_ref, out1_ref, h2_ref,
):
    half, groups = rows // 2, rows // 8
    wide = x_ref.shape[1]
    cols = wide // 4

    w1_flat[...] = jnp.zeros_like(w1_flat)
    for c in range(channels):
        for dr in range(3):
            at = (c * 3 + dr) * 3
            w1_flat[at : at + 3, :] = 0.5 * w1_ref[c, dr].astype(F32)
    w1 = w1_flat[...].astype(BF)
    for pc in range(2):
        for j in range(5):
            at = j * 128 + pc * 64
            w1_own[at : at + 64, :] = dot_t(w1, own_ref[j, pc]).astype(BF)
        for m in range(members):
            for kind in range(2):
                at = m * 256 + kind * 128 + pc * 64
                w1_down[at : at + 64, :] = dot_t(w1, above_ref[m, kind, pc]).astype(BF)
            at = m * 128 + pc * 64
            w1_up[at : at + 64, :] = dot_t(w1, below_ref[m, pc]).astype(BF)
    w2_big[...] = jnp.zeros_like(w2_big)
    for ocol in range(2):
        for dr in range(3):
            for dc in range(3):
                at = dr * 256 + (ocol + dc) * 64
                w2_big[ocol * 64 : ocol * 64 + 64, at : at + 64] = (0.5 * w2_ref[dr * 3 + dc].astype(F32)).astype(BF)
    w3_big[...] = jnp.zeros_like(w3_big)
    for dr, to, base in ((1, 0, 0), (2, 0, 128), (0, 2, 128)):
        for dc, moved, at in ((1, 0, 0), (2, 0, 64), (0, 1, 64)):
            w3_big[(to + moved) * 16 : (to + moved + 1) * 16, base + at : base + at + 64] = (
                0.5 * w3_ref[dr * 3 + dc].astype(F32)
            ).astype(BF)
    own_lanes = members * CH_BOT
    total = mix_ref.shape[1]
    start = lax.axis_index("mem") * own_lanes
    mix = pltpu.roll(mix_ref[...].astype(F32), lax.rem(total - start, total), 1)[:, 0:own_lanes].astype(BF)
    mix_own[...] = mix

    for t in range(wide // 512):
        for q, z in enumerate(apart(x_ref[:, 512 * t : 512 * (t + 1)], spread_ref[0], spread_ref[1])):
            for m in range(members):
                for c in range(channels):
                    for g in range(groups):
                        at = ((q + 1) * channels + c) * 8
                        frm = (m * channels + c) * rows + g * 8
                        y_ref[m, g, at : at + 8, t * 128 : (t + 1) * 128] = z[frm : frm + 8]
    c8 = channels * 8
    for m in range(members):
        for g in range(groups):
            y_ref[m, g, 0:c8, :] = shift_right(y_ref[m, g, 4 * c8 : 5 * c8, :])

    for m in range(members):
        for g in range(groups):
            out1_ref[g] = dot(w1_own[...], y_ref[m, g].astype(BF))
        lanes = slice(m * cols, (m + 1) * cols)
        h_first[:, lanes] = out1_ref[0, 0:128]
        h_last[:, lanes] = out1_ref[groups - 1, 512:640]
        for h in range(1, half):
            g, j = h // 4, h % 4
            v = out1_ref[g, j * 128 : j * 128 + 128]
            if j == 0:
                v = v + out1_ref[g - 1, 512:640]
            put_hidden(h1_ref, h - 1, lanes, silu_of_half(v))
    a_last[...] = dot(w2_big[:, 0:512], h1_ref[(half - 3) * 256 : (half - 1) * 256, :])
    for o in range(2):
        h2_ref[o * 128 : o * 128 + 128, :] = silu_of_half(
            dot(w2_big[...], h1_ref[o * 256 : (o + 3) * 256, :])
        ).astype(BF)
    v = dot(w3_big[...], h2_ref[...])
    v_second[...] = v[0:32]
    v_third[...] = v[32:64]
    h2_mid[...] = silu_of_half(dot(w2_big[...], h1_ref[512:1280, :])).astype(BF)


def low_kernel(
    members, channels, per,
    got_ref, spread_ref, w1_ref, h_ref, w2_ref, a_ref, w3_ref,
    h2_ref, carry_ref, y_ref, h1_ref,
):
    below = is_row(lax.axis_size("row") - 1)
    y = place_halo(got_ref[...], spread_ref, y_ref, members * channels * DOWN, per)
    cols = y_ref.shape[1]
    fresh = dot(w1_ref[...], y)
    for m in range(members):
        lanes = slice(m * cols, (m + 1) * cols)
        put_hidden(h1_ref, 0, lanes, silu_of_half((fresh[m * 128 : m * 128 + 128] + h_ref[:, lanes]) * below))
    h2 = silu_of_half(dot(w2_ref[:, 512:768], h1_ref[...]) + a_ref[...]).astype(BF)
    h2_ref[...] = h2
    v = dot(w3_ref[32:64, 128:256], h2)
    for m in range(members):
        lanes = slice(m * cols, (m + 1) * cols)
        carry_ref[m * 16 : m * 16 + 16, :] = (v[0:16, lanes] + shift_right(v[16:32, lanes])).astype(BF)


def middle_kernel(
    members, half,
    h1_ref, h2_mid, h2_low, w2_ref, w3_ref, v_ref, mix_ref,
    a_first, a_second, mixed_ref, h2_ref,
):
    wide = h1_ref.shape[1]
    cols = wide // members
    a_first[...] = dot(w2_ref[:, 512:768], h1_ref[0:256, :])
    a_second[...] = dot(w2_ref[:, 256:768], h1_ref[0:512, :])
    pairs = range(4, half, 2)
    for n, a in enumerate(pairs):
        lanes = slice(n * wide, (n + 1) * wide)
        for o in (a, a + 1):
            at = slice((o - a) * 128, (o - a) * 128 + 128)
            if o == half - 1:
                h2_ref[at, lanes] = h2_low[...]
            elif o == 4:
                h2_ref[at, lanes] = h2_mid[...]
            else:
                h2_ref[at, lanes] = silu_of_half(
                    dot(w2_ref[...], h1_ref[(o - 2) * 256 : (o + 1) * 256, :])
                ).astype(BF)
    v = dot(w3_ref[...], h2_ref[...])
    carry = v_ref[...]
    for n in range(len(pairs)):
        w = v[0:32, n * wide : (n + 1) * wide] + carry
        carry = v[32:64, n * wide : (n + 1) * wide]
        parts = [bottleneck(w[:, m * cols : (m + 1) * cols]) for m in range(members)]
        mixed_ref[n] = dot(mix_ref[...], jnp.concatenate(parts, axis=0))


def top_kernel(
    members, channels, per,
    got_ref, spread_ref, w1_ref, h_ref, w2_ref, a_first, a_second, w3_ref, v_ref, mix_ref, mid_ref,
    pre_ref, tail_ref, y_ref, h1_ref, h2_ref,
):
    source = (got_ref[...].astype(F32) * is_row(0)).astype(BF)
    y = place_halo(source, spread_ref, y_ref, members * channels * UP, per)
    cols = y_ref.shape[1]
    fresh = dot(w1_ref[...], y)
    for m in range(members):
        lanes = slice(m * cols, (m + 1) * cols)
        put_hidden(h1_ref, 0, lanes, silu_of_half(fresh[m * 256 : m * 256 + 128]))
        put_hidden(h1_ref, 1, lanes, silu_of_half(fresh[m * 256 + 128 : m * 256 + 256] + h_ref[:, lanes]))
    h2_ref[0:128, :] = silu_of_half(dot(w2_ref[:, 0:512], h1_ref[...]) + a_first[...]).astype(BF)
    h2_ref[128:256, :] = silu_of_half(dot(w2_ref[:, 0:256], h1_ref[256:512, :]) + a_second[...]).astype(BF)
    v = dot(w3_ref[...], h2_ref[...])
    second = []
    for m in range(members):
        lanes = slice(m * cols, (m + 1) * cols)
        pre_ref[m] = v[0:16, lanes] + shift_right(v[16:32, lanes])
        second.append(bottleneck(v[32:64, lanes] + v_ref[:, lanes]))
    tall = tail_ref.shape[0]
    tail_ref[:, 0:128] = jnp.zeros((tall, 128), F32)
    tail_ref[:, 128 + cols : 256 + cols] = jnp.zeros((tall, 128), F32)
    inside = slice(128, 128 + cols)
    tail_ref[0:32, inside] = dot(mix_ref[...], jnp.concatenate(second, axis=0))
    for r in range(mid_ref.shape[0]):
        tail_ref[(r + 1) * 32 : (r + 2) * 32, inside] = mid_ref[r]


def chunk_kernel(nb, pre_ref, carry_ref, mix_ref, tail_ref, keep_ref, send_ref, head_ref):
    members, _, cols = pre_ref.shape
    carry = carry_ref[...].astype(F32) * is_row(0)
    first = [
        silu_of_half(pre_ref[m] + carry[m * 16 : m * 16 + 16]).astype(BF) for m in range(members)
    ]
    head_ref[:, 0:128] = jnp.zeros((32, 128), F32)
    head_ref[:, 128 + cols : 256 + cols] = jnp.zeros((32, 128), F32)
    head_ref[:, 128 : 128 + cols] = dot(mix_ref[...], jnp.concatenate(first, axis=0))

    me = lax.axis_index("mem")
    slots = lax.axis_size("mem") // 2
    tall = 32 + tail_ref.shape[0]

    def tile_at(base):
        at = pl.ds(pl.multiple_of(base, 128), 128)
        return jnp.concatenate([head_ref[:, at], tail_ref[:, at]], axis=0)

    def lanes_from(lane):
        v = tile_at(lane // 128 * 128)
        return v if nb % 128 == 0 else pltpu.roll(v, (128 - lane % 128) % 128, 1)

    lane_at = lax.broadcasted_iota(jnp.int32, (tall, 128), 1)
    edges = jnp.zeros((tall, 128), F32)
    for side, ref in enumerate((keep_ref, send_ref)):
        for k in range(slots):
            start = 128 + (me ^ (2 * k + side)) * nb
            ref[k, 0:tall, :] = lanes_from(start).astype(BF)
            if nb % 128 == 0:
                left = tile_at(start - 128)[:, 127:128]
            else:
                left = lanes_from(start - 1)[:, 0:1]
            right = lanes_from(start + nb)[:, 0:1]
            at = 2 * (side * slots + k)
            edges = jnp.where(lane_at == at, left, edges)
            edges = jnp.where(lane_at == at + 1, right, edges)
    turned = edges.T
    for side, ref in enumerate((keep_ref, send_ref)):
        for k in range(slots):
            at = 2 * (side * slots + k)
            ref[k, tall : tall + 16, :] = jnp.concatenate(
                [turned[at : at + 2], jnp.zeros((14, 128), F32)], axis=0
            ).astype(BF)


def pair_kernel(keep_ref, got_ref, own_ref, *out_refs):
    own_ref[...] = keep_ref[0].astype(F32) + got_ref[0].astype(F32)
    for k, ref in enumerate(out_refs):
        ref[...] = (keep_ref[k + 1].astype(F32) + got_ref[k + 1].astype(F32)).astype(BF)


def put_latent(ref, at, line):
    ext = line.shape[1]
    ref[at, 0:32, :] = pltpu.roll(line, 1, 1).astype(BF)
    ref[at, 32:64, :] = line.astype(BF)
    ref[at, 64:96, :] = pltpu.roll(line, ext - 1, 1).astype(BF)


def latent_kernel(nb, quarter, own_ref, *refs):
    ext_ref, first_ref, second_ref = refs[-3:]
    total = own_ref[...]
    for ref in refs[:-3]:
        total = total + ref[...].astype(F32)
    latent = silu_of_half(0.5 * total)
    tall = quarter * 32
    turned = jnp.concatenate([latent[tall : tall + 16], jnp.zeros((112, 128), F32)], axis=0).T
    ext = ext_ref.shape[2]
    lines = []
    for r in range(quarter):
        rows = slice(r * 32, (r + 1) * 32)
        line = [latent[rows, 0:nb], turned[rows, 1:2], jnp.zeros((32, ext - nb - 2), F32), turned[rows, 0:1]]
        lines.append(jnp.concatenate(line, axis=1))
        put_latent(ext_ref, r, lines[-1])
    odd = lax.rem(lax.axis_index("row"), 2) == 1
    first_ref[...] = jnp.where(odd, lines[0], lines[-1]).astype(BF)
    second_ref[...] = jnp.where(odd, lines[-1], lines[0]).astype(BF)


def upsample_row(w1, l_ref, a, keep_even, keep_odd, rows, u_ref, wanted, keeps):
    wide = l_ref.shape[2]
    nb = u_ref.shape[1]
    v = silu_of_half(dot(w1, l_ref[a + 1 : a + 4].reshape(288, wide)))
    for pr in range(2):
        row = 2 * a + pr
        if row not in wanted:
            continue
        even = v[pr * 64 : pr * 64 + 32] * keep_even
        odd = v[pr * 64 + 32 : pr * 64 + 64] * keep_odd
        if row in keeps:
            even, odd = even * keeps[row], odd * keeps[row]
        at = (row + 1) * 128
        u_ref[at : at + 32, :] = pltpu.roll(odd, 1, 1)[:, 0:nb].astype(BF)
        u_ref[at + 32 : at + 64, :] = even[:, 0:nb].astype(BF)
        u_ref[at + 64 : at + 96, :] = odd[:, 0:nb].astype(BF)
        u_ref[at + 96 : at + 128, :] = pltpu.roll(even, wide - 1, 1)[:, 0:nb].astype(BF)


def column_keeps(nb, wide):
    mem_at, mem_last = lax.axis_index("mem"), lax.axis_size("mem") - 1
    lane = lax.broadcasted_iota(jnp.int32, (32, wide), 1)
    keep_odd = jnp.where((lane == wide - 1) & (mem_at == 0), 0.0, 1.0).astype(F32)
    keep_even = jnp.where((lane == nb) & (mem_at == mem_last), 0.0, 1.0).astype(F32)
    return keep_even, keep_odd


def field_rows(w2, u_ref, g_ref, which):
    nb = u_ref.shape[1]
    for n, a in enumerate(which):
        v = dot(w2, u_ref[a * 128 : (a + 3) * 128, :]).astype(BF)
        for pr in range(2):
            for ph in range(4):
                g_ref[(2 * n + pr) * 16 : (2 * n + pr + 1) * 16, ph * nb : (ph + 1) * nb] = v[
                    (pr * 4 + ph) * 16 : (pr * 4 + ph + 1) * 16
                ]


def level_first(rows, which):
    count = 32 * len(which)
    to = lax.broadcasted_iota(jnp.int32, (16 * rows, count), 0)
    frm = lax.broadcasted_iota(jnp.int32, (16 * rows, count), 1)
    level, row = to // rows, lax.rem(to, rows)
    hit = jnp.zeros(to.shape, jnp.bool_)
    for n, a in enumerate(which):
        for pr in range(2):
            hit = hit | ((row == 2 * a + pr) & (frm == (2 * n + pr) * 16 + level))
    return jnp.where(hit, 1.0, 0.0).astype(BF)


def split_rows(rows):
    inside = [a for a in range(2, 2 * rows - 2)]
    return inside, [a for a in range(2 * rows) if a not in inside]


def by_phase(v):
    return jnp.concatenate(
        [v[(pr * 4 + ph) * 16 : (pr * 4 + ph + 1) * 16] for ph in range(4) for pr in range(2)], axis=0
    )


def merge_phases(a, b):
    return jnp.concatenate([v[ph * 32 : ph * 32 + 32] for ph in range(4) for v in (a, b)], axis=0)


def decoder_inner(
    nb, ext_ref, d1_ref, d2_ref,
    w_edge, w_field, up_part, field_part, join_ref, turn_ref, part_ref, wd1, wd2, l_ref, u_ref, g_ref,
):
    wd1[...] = jnp.zeros_like(wd1)
    wd2[...] = jnp.zeros_like(wd2)
    for pr, rr, tr in TRANSPOSED:
        for pc, cc, tc in TRANSPOSED:
            wd1[(pr * 2 + pc) * 32 : (pr * 2 + pc + 1) * 32, (rr * 3 + cc) * 32 : (rr * 3 + cc + 1) * 32] = (
                0.5 * d1_ref[tr * 4 + tc].astype(F32)
            ).astype(BF)
            for q in range(2):
                at = pr * 4 + 2 * q + pc
                to = rr * 4 + q + cc
                wd2[at * 16 : (at + 1) * 16, to * 32 : (to + 1) * 32] = d2_ref[tr * 4 + tc]
    rows, _, wide = ext_ref.shape
    frm = lax.broadcasted_iota(jnp.int32, join_ref.shape, 0)
    to = lax.broadcasted_iota(jnp.int32, join_ref.shape, 1)
    place = frm // nb
    join_ref[...] = jnp.where(to == 4 * (frm - nb * place) + place, 1.0, 0.0).astype(BF)
    inside, outside = split_rows(rows)
    turn_ref[...] = level_first(4 * rows, outside)

    l_ref[0] = jnp.zeros_like(l_ref[0])
    l_ref[1] = jnp.zeros_like(l_ref[0])
    l_ref[2 : rows + 2] = ext_ref[...]
    l_ref[rows + 2] = jnp.zeros_like(l_ref[0])
    u_ref[...] = jnp.zeros_like(u_ref)
    keep_even, keep_odd = column_keeps(nb, wide)
    for a in range(rows):
        upsample_row(wd1[...], l_ref, a, keep_even, keep_odd, rows, u_ref, range(1, 2 * rows - 1), {})
    field_rows(wd2[...], u_ref, g_ref, inside)
    g = dot(level_first(4 * rows, inside), g_ref[...]).astype(BF)
    part_ref[...] = dot(g, join_ref[...])

    w_edge[0, 0:64, :] = wd1[64:128, 96:192]
    w_edge[0, 64:128, :] = wd1[0:64, 0:96]
    w_edge[1, 0:64, :] = wd1[64:128, 192:288]
    w_edge[1, 64:128, :] = wd1[0:64, 96:192]
    up_part[0] = dot(w_edge[1], ext_ref[0])
    up_part[1] = dot(w_edge[0], ext_ref[rows - 1])

    def known(taps, first, count):
        return by_phase(dot(wd2[:, taps : taps + 128 * count], u_ref[(first + 1) * 128 : (first + 1 + count) * 128, :]))

    last = 2 * rows - 1
    field_part[0] = merge_phases(known(256, 1, 1), known(128, 1, 2))
    field_part[1] = merge_phases(known(0, last - 2, 2), known(0, last - 1, 1))
    none = jnp.zeros((128, 128), BF)
    w = [by_phase(wd2[:, rr * 128 : rr * 128 + 128]) for rr in range(3)]
    w_field[0] = merge_phases(jnp.concatenate([w[0], w[1]], axis=1), jnp.concatenate([none, w[0]], axis=1))
    w_field[1] = merge_phases(jnp.concatenate([w[2], none], axis=1), jnp.concatenate([w[1], w[2]], axis=1))


def decoder_kernel(
    nb, first_ref, second_ref, w_edge, w_field, up_part, field_part, join_ref, turn_ref, part_ref,
    out_ref, l_ref, u_ref, g_ref,
):
    odd_row = lax.rem(lax.axis_index("row"), 2) == 1
    keeps = is_row(0), is_row(lax.axis_size("row") - 1)
    wide = l_ref.shape[2]
    first, second = first_ref[...].astype(F32), second_ref[...].astype(F32)
    put_latent(l_ref, 0, jnp.where(odd_row, first, second) * keeps[0])
    put_latent(l_ref, 1, jnp.where(odd_row, second, first) * keeps[1])
    keep_even, keep_odd = column_keeps(nb, wide)
    for side in range(2):
        v = silu_of_half(dot(w_edge[side], l_ref[side]) + up_part[side])
        for line in range(2):
            even = v[line * 64 : line * 64 + 32] * keep_even
            odd = v[line * 64 + 32 : line * 64 + 64] * keep_odd
            if line == side:
                even, odd = even * keeps[side], odd * keeps[side]
            at = line * 128
            u_ref[side, at : at + 32, :] = pltpu.roll(odd, 1, 1)[:, 0:nb].astype(BF)
            u_ref[side, at + 32 : at + 64, :] = even[:, 0:nb].astype(BF)
            u_ref[side, at + 64 : at + 96, :] = odd[:, 0:nb].astype(BF)
            u_ref[side, at + 96 : at + 128, :] = pltpu.roll(even, wide - 1, 1)[:, 0:nb].astype(BF)
        v = (dot(w_field[side], u_ref[side]) + field_part[side]).astype(BF)
        for ph in range(4):
            g_ref[side * 64 : side * 64 + 64, ph * nb : (ph + 1) * nb] = v[ph * 64 : ph * 64 + 64]
    g = dot(g_ref[...], join_ref[...]).astype(BF)
    out_ref[...] = (dot(turn_ref[...], g) + part_ref[...]).astype(BF).reshape(out_ref.shape)


def shifted(value, by):
    peers = lax.axis_size("row")
    return lax.ppermute(value, "row", [(i, (i + by) % peers) for i in range(peers)])


def swapped(value, by):
    return lax.ppermute(value, "mem", [(i, i ^ by) for i in range(lax.axis_size("mem"))])


VMEM = pl.BlockSpec(memory_space=pltpu.VMEM)


def call(kernel, outs, scratch, *operands, mb=8, us=1):
    return pl.pallas_call(
        kernel,
        out_shape=[jax.ShapeDtypeStruct(*o) for o in outs],
        in_specs=[VMEM] * len(operands),
        out_specs=[VMEM] * len(outs),
        scratch_shapes=[pltpu.VMEM(*s) for s in scratch],
        compiler_params=pltpu.CompilerParams(vmem_limit_bytes=mb * 2**20),
        cost_estimate=pl.CostEstimate(flops=us * 10**9, bytes_accessed=us * 3 * 10**6, transcendentals=0),
    )(*operands)


def per_device(members, enc_first, enc_second, enc_third, mix_weight, dec_first, dec_second):
    count, channels, rows, wide = members.shape
    half, quarter = rows // 2, rows // 4
    cols = wide // 4
    peers, lines = lax.axis_size("mem"), lax.axis_size("row")
    nb = cols // peers
    lanes = 512
    chunks = wide // lanes
    x = members.reshape(count * channels * rows, wide)
    nd, nu = count * channels * UP, count * channels * DOWN
    per = padded(nd, 8), padded(nu, 8)
    total = padded(5 * per[0], 16), padded(5 * per[1], 16)
    pack = functools.partial(pack_kernel, count, channels, rows)
    sizes = [(nd * chunks, lanes), (nu * chunks, lanes)]
    cut = (count * channels) // 2 * rows
    spreads, own, above, below = call(
        functools.partial(prepare_kernel, count, channels, per),
        [
            ((2, 256, 256), BF),
            ((5, 2, 48, 5 * channels * 8), BF),
            ((count, 2, 2, 48, total[0]), BF),
            ((count, 2, 48, total[1]), BF),
        ],
        [],
    )
    down, up = call(pack, [(s, BF) for s in sizes], [(s, F32) for s in sizes], x[:cut], x[cut:], below, mb=16, us=20)
    up = shifted(up, -1)
    down = shifted(down, 1)

    w1 = enc_first.transpose(1, 2, 3, 0)
    w2 = enc_second.transpose(2, 3, 0, 1).reshape(9, 64, 64)
    w3 = enc_third.transpose(2, 3, 0, 1).reshape(9, 16, 64)
    wide_cols = count * cols
    row_f32 = ((128, wide_cols), F32)
    third_f32 = ((32, wide_cols), F32)
    (
        h1, h_first, h_last, a_last, v_second, v_third, h2_mid,
        w2_big, w3_big, w1_down, w1_up, mix,
    ) = call(
        functools.partial(inner_kernel, count, channels, rows),
        [((256 * (half - 1), wide_cols), BF)]
        + [row_f32] * 3
        + [third_f32] * 2
        + [
            ((128, wide_cols), BF),
            ((128, 768), BF),
            ((64, 256), BF),
            ((count * 256, total[0]), BF),
            ((count * 128, total[1]), BF),
            ((32, count * CH_BOT), BF),
        ],
        [
            ((48, 64), F32),
            ((640, 5 * channels * 8), BF),
            ((count, rows // 8, 5 * channels * 8, cols), F32),
            ((rows // 8, 640, cols), F32),
            ((256, wide_cols), BF),
        ],
        x, w1, w2, w3, mix_weight, spreads, own, above, below, mb=24,
    )
    h2_low, carry = call(
        functools.partial(low_kernel, count, channels, per[1]),
        [((128, wide_cols), BF), ((count * CH_BOT, cols), BF)],
        [((total[1], cols), F32), ((256, wide_cols), BF)],
        up, spreads, w1_up, h_last, w2_big, a_last, w3_big, mb=12,
    )
    carry = shifted(carry, 1)
    a_first, a_second, mid = call(
        functools.partial(middle_kernel, count, half),
        [row_f32, row_f32, ((quarter - 2, 32, cols), F32)],
        [((256, (half // 2 - 2) * wide_cols), BF)],
        h1, h2_mid, h2_low, w2_big, w3_big, v_third, mix, mb=12,
    )
    pre, tail = call(
        functools.partial(top_kernel, count, channels, per[0]),
        [((count, CH_BOT, cols), F32), ((quarter * 32 - 32, cols + 256), F32)],
        [((total[0], cols), F32), ((512, wide_cols), BF), ((256, wide_cols), BF)],
        down, spreads, w1_down, h_first, w2_big, a_first, a_second, w3_big, v_second, mix, mid, mb=12,
    )
    slots = peers // 2
    chunk = (quarter * 32 + 16, 128)
    keep, send = call(
        functools.partial(chunk_kernel, nb),
        [((slots,) + chunk, BF)] * 2,
        [((32, cols + 256), F32)],
        pre, carry, mix, tail,
    )
    got = swapped(send, 1)
    mine, *others = call(pair_kernel, [(chunk, F32)] + [(chunk, BF)] * (slots - 1), [], keep, got)
    order = sorted(range(slots - 1), key=lambda k: (k == 0, k))
    moved = {k: swapped(others[k], 2 * (k + 1)) for k in order}
    ext = padded(nb + 2, 128)
    latent, first, second = call(
        functools.partial(latent_kernel, nb, quarter),
        [((quarter, 96, ext), BF), ((32, ext), BF), ((32, ext), BF)],
        [],
        mine, *[moved[k] for k in range(slots - 1)],
    )
    first = lax.ppermute(first, "row", [(i, i ^ 1) for i in range(lines)])
    second = lax.ppermute(second, "row", [(i, (i + 1 if i % 2 else i - 1) % lines) for i in range(lines)])

    d1, d2, _ = lax.optimization_barrier((dec_first, dec_second, others[0]))
    d1 = d1.transpose(2, 3, 0, 1).reshape(16, 32, 32)
    d2 = d2.transpose(2, 3, 0, 1).reshape(16, 16, 32)
    inside, outside = split_rows(quarter)
    edge_parts = call(
        functools.partial(decoder_inner, nb),
        [
            ((2, 128, 96), BF),
            ((2, 256, 256), BF),
            ((2, 128, ext), F32),
            ((2, 256, nb), F32),
            ((4 * nb, 4 * nb), BF),
            ((16 * rows, 32 * len(outside)), BF),
            ((16 * rows, 4 * nb), F32),
        ],
        [
            ((128, 288), BF),
            ((128, 384), BF),
            ((quarter + 3, 96, ext), BF),
            ((128 * (half + 2), nb), BF),
            ((32 * len(inside), 4 * nb), BF),
        ],
        latent, d1, d2,
    )
    (out,) = call(
        functools.partial(decoder_kernel, nb),
        [((16, rows, 4 * nb), BF)],
        [((2, 96, ext), BF), ((2, 256, nb), BF), ((128, 4 * nb), BF)],
        first, second, *edge_parts,
    )
    return out


def solution(mesh):
    placed = (P("mem", None, "row", None), P(), P(), P(), P(), P(), P())
    return jax.shard_map(
        per_device, mesh=mesh, in_specs=placed, out_specs=P(None, "row", "mem"), check_vma=False
    )
```

```python
import functools

import jax
import jax.numpy as jnp
import numpy as np
from jax import lax
from jax.experimental import pallas as pl
from jax.experimental.pallas import tpu as pltpu
from jax.sharding import PartitionSpec as P

BF = jnp.bfloat16
F32 = jnp.float32
CH_BOT = 16
UP = 3
DOWN = 2
TRANSPOSED = [(p, i, 2 * i - p) for p in range(2) for i in range(3) if 0 <= 2 * i - p < 4]


def dot(a, b):
    return lax.dot_general(a, b, (((1,), (0,)), ((), ())), preferred_element_type=F32)


def dot_t(a, b):
    return lax.dot_general(a, b, (((0,), (0,)), ((), ())), preferred_element_type=F32)


def silu_of_half(y):
    return y + y * jnp.tanh(y)


def padded(n, to):
    return -(-n // to) * to


def spread(step, tile):
    one = np.zeros((step * tile, step * tile), np.float32)
    for q in range(step):
        for c in range(tile):
            one[step * c + q, q * tile + c] = 1
    return one


def shift_right(v):
    return jnp.concatenate([jnp.zeros_like(v[:, :1]), v[:, :-1]], axis=1)


def shift_left(v):
    return jnp.concatenate([v[:, 1:], jnp.zeros_like(v[:, :1])], axis=1)


def is_row(at):
    return jnp.where(lax.axis_index("row") == at, 0.0, 1.0).astype(F32)


def put_hidden(ref, at, lanes, value):
    v = value.astype(BF)
    even, odd = v[0:64], v[64:128]
    ref[at * 256 + 64 : at * 256 + 128, lanes] = even
    ref[at * 256 + 128 : at * 256 + 192, lanes] = odd
    ref[at * 256 : at * 256 + 64, lanes] = shift_right(odd)
    ref[at * 256 + 192 : at * 256 + 256, lanes] = shift_left(even)


def bottleneck(w):
    return silu_of_half(w[0:16] + shift_right(w[16:32])).astype(BF)


def apart(block, even_ref, odd_ref):
    first = dot(block[:, 0:256], even_ref)
    second = dot(block[:, 256:512], odd_ref)
    low = lax.broadcasted_iota(jnp.int32, (block.shape[0], 128), 1) < 64
    out = []
    for half in range(2):
        e, o = first[:, half * 128 : half * 128 + 128], second[:, half * 128 : half * 128 + 128]
        out.append(jnp.where(low, e, o))
        out.append(pltpu.roll(jnp.where(low, o, e), 64, 1))
    return out


def place_halo(source, spread_ref, y_ref, count, per):
    cols = y_ref.shape[1]
    if count % 8:
        for q in range(5):
            y_ref[q * per + count // 8 * 8 : (q + 1) * per, :] = jnp.zeros((8, cols), F32)
    if 5 * per < y_ref.shape[0]:
        y_ref[5 * per :, :] = jnp.zeros((y_ref.shape[0] - 5 * per, cols), F32)
    for q, z in enumerate(apart(source, spread_ref[0], spread_ref[1])):
        for t in range(cols // 128):
            y_ref[(q + 1) * per : (q + 1) * per + count, t * 128 : (t + 1) * 128] = z[t * count : (t + 1) * count]
    y_ref[0:per, :] = shift_right(y_ref[4 * per : 5 * per, :])
    return y_ref[...].astype(BF)


def prepare_kernel(members, channels, per, spread_ref, own_ref, above_ref, below_ref):
    row_of = lax.broadcasted_iota(jnp.int32, (256, 256), 0)
    lane_of = lax.broadcasted_iota(jnp.int32, (256, 256), 1)
    place = lane_of // 64
    for odd in range(2):
        spread_ref[odd] = jnp.where(row_of == 4 * (lane_of - 64 * place) + (place ^ odd), 1.0, 0.0).astype(BF)

    def tap_of(lanes):
        tap = lax.broadcasted_iota(jnp.int32, (48, lanes), 0)
        c = sum(((tap >= 9 * k).astype(jnp.int32) for k in range(1, channels)), jnp.zeros_like(tap))
        rest = tap - 9 * c
        dr = (rest >= 3).astype(jnp.int32) + (rest >= 6).astype(jnp.int32)
        return c, dr, rest - 3 * dr, lax.broadcasted_iota(jnp.int32, (48, lanes), 1)

    def one_hot(hit):
        return jnp.where(hit, 1.0, 0.0).astype(BF)

    c, dr, dc, lane = tap_of(own_ref.shape[3])
    for j in range(5):
        row = 2 * j + dr - 1
        for pc in range(2):
            at = ((2 * pc + dc) * channels + c) * 8 + row
            own_ref[j, pc] = one_hot((lane == at) & (row >= 0) & (row < 8))
    c, dr, dc, lane = tap_of(above_ref.shape[4])
    for m in range(members):
        for kind in range(2):
            slot = dr + 2 * kind
            for pc in range(2):
                at = (2 * pc + dc) * per[0] + (m * channels + c) * UP + slot
                above_ref[m, kind, pc] = one_hot((lane == at) & (slot < UP))
    c, dr, dc, lane = tap_of(below_ref.shape[3])
    for m in range(members):
        for pc in range(2):
            at = (2 * pc + dc) * per[1] + (m * channels + c) * DOWN + dr - 1
            below_ref[m, pc] = one_hot((lane == at) & (dr >= 1))


def pack_kernel(members, channels, rows, xa_ref, xb_ref, _, down_ref, up_ref, d_scr, u_scr):
    wide = xa_ref.shape[1]
    lanes = down_ref.shape[1]
    cut = xa_ref.shape[0]
    nd, nu = members * channels * UP, members * channels * DOWN
    for t in range(wide // lanes):
        for g in range(members * channels):
            ref, at = (xa_ref, g * rows) if g * rows < cut else (xb_ref, g * rows - cut)
            block = ref[at : at + rows, t * lanes : (t + 1) * lanes].astype(F32)
            d_scr[t * nd + g * UP : t * nd + (g + 1) * UP, :] = block[rows - UP : rows]
            u_scr[t * nu + g * DOWN : t * nu + (g + 1) * DOWN, :] = block[0:DOWN]
    down_ref[...] = d_scr[...].astype(BF)
    up_ref[...] = u_scr[...].astype(BF)


def inner_kernel(
    members, channels, rows,
    x_ref, w1_ref, w2_ref, w3_ref, mix_ref, spread_ref, own_ref, above_ref, below_ref,
    h1_ref, h_first, h_last, a_last, v_second, v_third, h2_mid,
    w2_big, w3_big, w1_down, w1_up, mix_own,
    w1_flat, w1_own, y_ref, out1_ref, h2_ref,
):
    half, groups = rows // 2, rows // 8
    wide = x_ref.shape[1]
    cols = wide // 4

    w1_flat[...] = jnp.zeros_like(w1_flat)
    for c in range(channels):
        for dr in range(3):
            at = (c * 3 + dr) * 3
            w1_flat[at : at + 3, :] = 0.5 * w1_ref[c, dr].astype(F32)
    w1 = w1_flat[...].astype(BF)
    for pc in range(2):
        for j in range(5):
            at = j * 128 + pc * 64
            w1_own[at : at + 64, :] = dot_t(w1, own_ref[j, pc]).astype(BF)
        for m in range(members):
            for kind in range(2):
                at = m * 256 + kind * 128 + pc * 64
                w1_down[at : at + 64, :] = dot_t(w1, above_ref[m, kind, pc]).astype(BF)
            at = m * 128 + pc * 64
            w1_up[at : at + 64, :] = dot_t(w1, below_ref[m, pc]).astype(BF)
    w2_big[...] = jnp.zeros_like(w2_big)
    for ocol in range(2):
        for dr in range(3):
            for dc in range(3):
                at = dr * 256 + (ocol + dc) * 64
                w2_big[ocol * 64 : ocol * 64 + 64, at : at + 64] = (0.5 * w2_ref[dr * 3 + dc].astype(F32)).astype(BF)
    w3_big[...] = jnp.zeros_like(w3_big)
    for dr, to, base in ((1, 0, 0), (2, 0, 128), (0, 2, 128)):
        for dc, moved, at in ((1, 0, 0), (2, 0, 64), (0, 1, 64)):
            w3_big[(to + moved) * 16 : (to + moved + 1) * 16, base + at : base + at + 64] = (
                0.5 * w3_ref[dr * 3 + dc].astype(F32)
            ).astype(BF)
    own_lanes = members * CH_BOT
    total = mix_ref.shape[1]
    start = lax.axis_index("mem") * own_lanes
    mix = pltpu.roll(mix_ref[...].astype(F32), lax.rem(total - start, total), 1)[:, 0:own_lanes].astype(BF)
    mix_own[...] = mix

    for t in range(wide // 512):
        for q, z in enumerate(apart(x_ref[:, 512 * t : 512 * (t + 1)], spread_ref[0], spread_ref[1])):
            for m in range(members):
                for c in range(channels):
                    for g in range(groups):
                        at = ((q + 1) * channels + c) * 8
                        frm = (m * channels + c) * rows + g * 8
                        y_ref[m, g, at : at + 8, t * 128 : (t + 1) * 128] = z[frm : frm + 8]
    c8 = channels * 8
    for m in range(members):
        for g in range(groups):
            y_ref[m, g, 0:c8, :] = shift_right(y_ref[m, g, 4 * c8 : 5 * c8, :])

    for m in range(members):
        for g in range(groups):
            out1_ref[g] = dot(w1_own[...], y_ref[m, g].astype(BF))
        lanes = slice(m * cols, (m + 1) * cols)
        h_first[:, lanes] = out1_ref[0, 0:128]
        h_last[:, lanes] = out1_ref[groups - 1, 512:640]
        for h in range(1, half):
            g, j = h // 4, h % 4
            v = out1_ref[g, j * 128 : j * 128 + 128]
            if j == 0:
                v = v + out1_ref[g - 1, 512:640]
            put_hidden(h1_ref, h - 1, lanes, silu_of_half(v))
    a_last[...] = dot(w2_big[:, 0:512], h1_ref[(half - 3) * 256 : (half - 1) * 256, :])
    for o in range(2):
        h2_ref[o * 128 : o * 128 + 128, :] = silu_of_half(
            dot(w2_big[...], h1_ref[o * 256 : (o + 3) * 256, :])
        ).astype(BF)
    v = dot(w3_big[...], h2_ref[...])
    v_second[...] = v[0:32]
    v_third[...] = v[32:64]
    h2_mid[...] = silu_of_half(dot(w2_big[...], h1_ref[512:1280, :])).astype(BF)


def low_kernel(
    members, channels, per,
    got_ref, spread_ref, w1_ref, h_ref, w2_ref, a_ref, w3_ref,
    h2_ref, carry_ref, y_ref, h1_ref,
):
    below = is_row(lax.axis_size("row") - 1)
    y = place_halo(got_ref[...], spread_ref, y_ref, members * channels * DOWN, per)
    cols = y_ref.shape[1]
    fresh = dot(w1_ref[...], y)
    for m in range(members):
        lanes = slice(m * cols, (m + 1) * cols)
        put_hidden(h1_ref, 0, lanes, silu_of_half((fresh[m * 128 : m * 128 + 128] + h_ref[:, lanes]) * below))
    h2 = silu_of_half(dot(w2_ref[:, 512:768], h1_ref[...]) + a_ref[...]).astype(BF)
    h2_ref[...] = h2
    v = dot(w3_ref[32:64, 128:256], h2)
    for m in range(members):
        lanes = slice(m * cols, (m + 1) * cols)
        carry_ref[m * 16 : m * 16 + 16, :] = (v[0:16, lanes] + shift_right(v[16:32, lanes])).astype(BF)


def middle_kernel(
    members, half,
    h1_ref, h2_mid, h2_low, w2_ref, w3_ref, v_ref, mix_ref,
    a_first, a_second, mixed_ref, h2_ref,
):
    wide = h1_ref.shape[1]
    cols = wide // members
    a_first[...] = dot(w2_ref[:, 512:768], h1_ref[0:256, :])
    a_second[...] = dot(w2_ref[:, 256:768], h1_ref[0:512, :])
    pairs = range(4, half, 2)
    for n, a in enumerate(pairs):
        lanes = slice(n * wide, (n + 1) * wide)
        for o in (a, a + 1):
            at = slice((o - a) * 128, (o - a) * 128 + 128)
            if o == half - 1:
                h2_ref[at, lanes] = h2_low[...]
            elif o == 4:
                h2_ref[at, lanes] = h2_mid[...]
            else:
                h2_ref[at, lanes] = silu_of_half(
                    dot(w2_ref[...], h1_ref[(o - 2) * 256 : (o + 1) * 256, :])
                ).astype(BF)
    v = dot(w3_ref[...], h2_ref[...])
    carry = v_ref[...]
    for n in range(len(pairs)):
        w = v[0:32, n * wide : (n + 1) * wide] + carry
        carry = v[32:64, n * wide : (n + 1) * wide]
        parts = [bottleneck(w[:, m * cols : (m + 1) * cols]) for m in range(members)]
        mixed_ref[n] = dot(mix_ref[...], jnp.concatenate(parts, axis=0))


def top_kernel(
    members, channels, per,
    got_ref, spread_ref, w1_ref, h_ref, w2_ref, a_first, a_second, w3_ref, v_ref, mix_ref, mid_ref,
    pre_ref, tail_ref, y_ref, h1_ref, h2_ref,
):
    source = (got_ref[...].astype(F32) * is_row(0)).astype(BF)
    y = place_halo(source, spread_ref, y_ref, members * channels * UP, per)
    cols = y_ref.shape[1]
    fresh = dot(w1_ref[...], y)
    for m in range(members):
        lanes = slice(m * cols, (m + 1) * cols)
        put_hidden(h1_ref, 0, lanes, silu_of_half(fresh[m * 256 : m * 256 + 128]))
        put_hidden(h1_ref, 1, lanes, silu_of_half(fresh[m * 256 + 128 : m * 256 + 256] + h_ref[:, lanes]))
    h2_ref[0:128, :] = silu_of_half(dot(w2_ref[:, 0:512], h1_ref[...]) + a_first[...]).astype(BF)
    h2_ref[128:256, :] = silu_of_half(dot(w2_ref[:, 0:256], h1_ref[256:512, :]) + a_second[...]).astype(BF)
    v = dot(w3_ref[...], h2_ref[...])
    second = []
    for m in range(members):
        lanes = slice(m * cols, (m + 1) * cols)
        pre_ref[m] = v[0:16, lanes] + shift_right(v[16:32, lanes])
        second.append(bottleneck(v[32:64, lanes] + v_ref[:, lanes]))
    tall = tail_ref.shape[0]
    tail_ref[:, 0:128] = jnp.zeros((tall, 128), F32)
    tail_ref[:, 128 + cols : 256 + cols] = jnp.zeros((tall, 128), F32)
    inside = slice(128, 128 + cols)
    tail_ref[0:32, inside] = dot(mix_ref[...], jnp.concatenate(second, axis=0))
    for r in range(mid_ref.shape[0]):
        tail_ref[(r + 1) * 32 : (r + 2) * 32, inside] = mid_ref[r]


def chunk_kernel(nb, pre_ref, carry_ref, mix_ref, tail_ref, keep_ref, send_ref, head_ref):
    members, _, cols = pre_ref.shape
    carry = carry_ref[...].astype(F32) * is_row(0)
    first = [
        silu_of_half(pre_ref[m] + carry[m * 16 : m * 16 + 16]).astype(BF) for m in range(members)
    ]
    head_ref[:, 0:128] = jnp.zeros((32, 128), F32)
    head_ref[:, 128 + cols : 256 + cols] = jnp.zeros((32, 128), F32)
    head_ref[:, 128 : 128 + cols] = dot(mix_ref[...], jnp.concatenate(first, axis=0))

    me = lax.axis_index("mem")
    slots = lax.axis_size("mem") // 2
    tall = 32 + tail_ref.shape[0]

    def tile_at(base):
        at = pl.ds(pl.multiple_of(base, 128), 128)
        return jnp.concatenate([head_ref[:, at], tail_ref[:, at]], axis=0)

    def lanes_from(lane):
        v = tile_at(lane // 128 * 128)
        return v if nb % 128 == 0 else pltpu.roll(v, (128 - lane % 128) % 128, 1)

    lane_at = lax.broadcasted_iota(jnp.int32, (tall, 128), 1)
    edges = jnp.zeros((tall, 128), F32)
    for side, ref in enumerate((keep_ref, send_ref)):
        for k in range(slots):
            start = 128 + (me ^ (2 * k + side)) * nb
            ref[k, 0:tall, :] = lanes_from(start).astype(BF)
            if nb % 128 == 0:
                left = tile_at(start - 128)[:, 127:128]
            else:
                left = lanes_from(start - 1)[:, 0:1]
            right = lanes_from(start + nb)[:, 0:1]
            at = 2 * (side * slots + k)
            edges = jnp.where(lane_at == at, left, edges)
            edges = jnp.where(lane_at == at + 1, right, edges)
    turned = edges.T
    for side, ref in enumerate((keep_ref, send_ref)):
        for k in range(slots):
            at = 2 * (side * slots + k)
            ref[k, tall : tall + 16, :] = jnp.concatenate(
                [turned[at : at + 2], jnp.zeros((14, 128), F32)], axis=0
            ).astype(BF)


def pair_kernel(keep_ref, got_ref, own_ref, *out_refs):
    own_ref[...] = keep_ref[0].astype(F32) + got_ref[0].astype(F32)
    for k, ref in enumerate(out_refs):
        ref[...] = (keep_ref[k + 1].astype(F32) + got_ref[k + 1].astype(F32)).astype(BF)


def put_latent(ref, at, line):
    ext = line.shape[1]
    ref[at, 0:32, :] = pltpu.roll(line, 1, 1).astype(BF)
    ref[at, 32:64, :] = line.astype(BF)
    ref[at, 64:96, :] = pltpu.roll(line, ext - 1, 1).astype(BF)


def latent_kernel(nb, quarter, own_ref, *refs):
    ext_ref, first_ref, second_ref = refs[-3:]
    total = own_ref[...]
    for ref in refs[:-3]:
        total = total + ref[...].astype(F32)
    latent = silu_of_half(0.5 * total)
    tall = quarter * 32
    turned = jnp.concatenate([latent[tall : tall + 16], jnp.zeros((112, 128), F32)], axis=0).T
    ext = ext_ref.shape[2]
    lines = []
    for r in range(quarter):
        rows = slice(r * 32, (r + 1) * 32)
        line = [latent[rows, 0:nb], turned[rows, 1:2], jnp.zeros((32, ext - nb - 2), F32), turned[rows, 0:1]]
        lines.append(jnp.concatenate(line, axis=1))
        put_latent(ext_ref, r, lines[-1])
    first_ref[...] = lines[-1].astype(BF)
    second_ref[...] = lines[0].astype(BF)


def upsample_row(w1, l_ref, a, keep_even, keep_odd, rows, u_ref, wanted, keeps):
    wide = l_ref.shape[2]
    nb = u_ref.shape[1]
    v = silu_of_half(dot(w1, l_ref[a + 1 : a + 4].reshape(288, wide)))
    for pr in range(2):
        row = 2 * a + pr
        if row not in wanted:
            continue
        even = v[pr * 64 : pr * 64 + 32] * keep_even
        odd = v[pr * 64 + 32 : pr * 64 + 64] * keep_odd
        if row in keeps:
            even, odd = even * keeps[row], odd * keeps[row]
        at = (row + 1) * 128
        u_ref[at : at + 32, :] = pltpu.roll(odd, 1, 1)[:, 0:nb].astype(BF)
        u_ref[at + 32 : at + 64, :] = even[:, 0:nb].astype(BF)
        u_ref[at + 64 : at + 96, :] = odd[:, 0:nb].astype(BF)
        u_ref[at + 96 : at + 128, :] = pltpu.roll(even, wide - 1, 1)[:, 0:nb].astype(BF)


def column_keeps(nb, wide):
    mem_at, mem_last = lax.axis_index("mem"), lax.axis_size("mem") - 1
    lane = lax.broadcasted_iota(jnp.int32, (32, wide), 1)
    keep_odd = jnp.where((lane == wide - 1) & (mem_at == 0), 0.0, 1.0).astype(F32)
    keep_even = jnp.where((lane == nb) & (mem_at == mem_last), 0.0, 1.0).astype(F32)
    return keep_even, keep_odd


def field_rows(w2, u_ref, g_ref, which):
    nb = u_ref.shape[1]
    for n, a in enumerate(which):
        v = dot(w2, u_ref[a * 128 : (a + 3) * 128, :]).astype(BF)
        for pr in range(2):
            for ph in range(4):
                g_ref[(2 * n + pr) * 16 : (2 * n + pr + 1) * 16, ph * nb : (ph + 1) * nb] = v[
                    (pr * 4 + ph) * 16 : (pr * 4 + ph + 1) * 16
                ]


def level_first(rows, which):
    count = 32 * len(which)
    to = lax.broadcasted_iota(jnp.int32, (16 * rows, count), 0)
    frm = lax.broadcasted_iota(jnp.int32, (16 * rows, count), 1)
    level, row = to // rows, lax.rem(to, rows)
    hit = jnp.zeros(to.shape, jnp.bool_)
    for n, a in enumerate(which):
        for pr in range(2):
            hit = hit | ((row == 2 * a + pr) & (frm == (2 * n + pr) * 16 + level))
    return jnp.where(hit, 1.0, 0.0).astype(BF)


def split_rows(rows):
    inside = [a for a in range(2, 2 * rows - 2)]
    return inside, [a for a in range(2 * rows) if a not in inside]


def by_phase(v):
    return jnp.concatenate(
        [v[(pr * 4 + ph) * 16 : (pr * 4 + ph + 1) * 16] for ph in range(4) for pr in range(2)], axis=0
    )


def merge_phases(a, b):
    return jnp.concatenate([v[ph * 32 : ph * 32 + 32] for ph in range(4) for v in (a, b)], axis=0)


def decoder_inner(
    nb, ext_ref, d1_ref, d2_ref,
    w_edge, w_field, up_part, field_part, join_ref, turn_ref, part_ref, wd1, wd2, l_ref, u_ref, g_ref,
):
    wd1[...] = jnp.zeros_like(wd1)
    wd2[...] = jnp.zeros_like(wd2)
    for pr, rr, tr in TRANSPOSED:
        for pc, cc, tc in TRANSPOSED:
            wd1[(pr * 2 + pc) * 32 : (pr * 2 + pc + 1) * 32, (rr * 3 + cc) * 32 : (rr * 3 + cc + 1) * 32] = (
                0.5 * d1_ref[tr * 4 + tc].astype(F32)
            ).astype(BF)
            for q in range(2):
                at = pr * 4 + 2 * q + pc
                to = rr * 4 + q + cc
                wd2[at * 16 : (at + 1) * 16, to * 32 : (to + 1) * 32] = d2_ref[tr * 4 + tc]
    rows, _, wide = ext_ref.shape
    frm = lax.broadcasted_iota(jnp.int32, join_ref.shape, 0)
    to = lax.broadcasted_iota(jnp.int32, join_ref.shape, 1)
    place = frm // nb
    join_ref[...] = jnp.where(to == 4 * (frm - nb * place) + place, 1.0, 0.0).astype(BF)
    inside, outside = split_rows(rows)
    turn_ref[...] = level_first(4 * rows, outside)

    l_ref[0] = jnp.zeros_like(l_ref[0])
    l_ref[1] = jnp.zeros_like(l_ref[0])
    l_ref[2 : rows + 2] = ext_ref[...]
    l_ref[rows + 2] = jnp.zeros_like(l_ref[0])
    u_ref[...] = jnp.zeros_like(u_ref)
    keep_even, keep_odd = column_keeps(nb, wide)
    for a in range(rows):
        upsample_row(wd1[...], l_ref, a, keep_even, keep_odd, rows, u_ref, range(1, 2 * rows - 1), {})
    field_rows(wd2[...], u_ref, g_ref, inside)
    g = dot(level_first(4 * rows, inside), g_ref[...]).astype(BF)
    part_ref[...] = dot(g, join_ref[...])

    w_edge[0, 0:64, :] = wd1[64:128, 96:192]
    w_edge[0, 64:128, :] = wd1[0:64, 0:96]
    w_edge[1, 0:64, :] = wd1[64:128, 192:288]
    w_edge[1, 64:128, :] = wd1[0:64, 96:192]
    up_part[0] = dot(w_edge[1], ext_ref[0])
    up_part[1] = dot(w_edge[0], ext_ref[rows - 1])

    def known(taps, first, count):
        return by_phase(dot(wd2[:, taps : taps + 128 * count], u_ref[(first + 1) * 128 : (first + 1 + count) * 128, :]))

    last = 2 * rows - 1
    field_part[0] = merge_phases(known(256, 1, 1), known(128, 1, 2))
    field_part[1] = merge_phases(known(0, last - 2, 2), known(0, last - 1, 1))
    none = jnp.zeros((128, 128), BF)
    w = [by_phase(wd2[:, rr * 128 : rr * 128 + 128]) for rr in range(3)]
    w_field[0] = merge_phases(jnp.concatenate([w[0], w[1]], axis=1), jnp.concatenate([none, w[0]], axis=1))
    w_field[1] = merge_phases(jnp.concatenate([w[2], none], axis=1), jnp.concatenate([w[1], w[2]], axis=1))


def decoder_kernel(
    nb, first_ref, second_ref, w_edge, w_field, up_part, field_part, join_ref, turn_ref, part_ref,
    out_ref, l_ref, u_ref, g_ref,
):
    odd_row = lax.rem(lax.axis_index("row"), 2) == 1
    keeps = is_row(0), is_row(lax.axis_size("row") - 1)
    wide = l_ref.shape[2]
    first, second = first_ref[...].astype(F32), second_ref[...].astype(F32)
    put_latent(l_ref, 0, first * keeps[0])
    put_latent(l_ref, 1, second * keeps[1])
    keep_even, keep_odd = column_keeps(nb, wide)
    for side in range(2):
        v = silu_of_half(dot(w_edge[side], l_ref[side]) + up_part[side])
        for line in range(2):
            even = v[line * 64 : line * 64 + 32] * keep_even
            odd = v[line * 64 + 32 : line * 64 + 64] * keep_odd
            if line == side:
                even, odd = even * keeps[side], odd * keeps[side]
            at = line * 128
            u_ref[side, at : at + 32, :] = pltpu.roll(odd, 1, 1)[:, 0:nb].astype(BF)
            u_ref[side, at + 32 : at + 64, :] = even[:, 0:nb].astype(BF)
            u_ref[side, at + 64 : at + 96, :] = odd[:, 0:nb].astype(BF)
            u_ref[side, at + 96 : at + 128, :] = pltpu.roll(even, wide - 1, 1)[:, 0:nb].astype(BF)
        v = (dot(w_field[side], u_ref[side]) + field_part[side]).astype(BF)
        for ph in range(4):
            g_ref[side * 64 : side * 64 + 64, ph * nb : (ph + 1) * nb] = v[ph * 64 : ph * 64 + 64]
    g = dot(g_ref[...], join_ref[...]).astype(BF)
    out_ref[...] = (dot(turn_ref[...], g) + part_ref[...]).astype(BF).reshape(out_ref.shape)


def shifted(value, by):
    peers = lax.axis_size("row")
    return lax.ppermute(value, "row", [(i, (i + by) % peers) for i in range(peers)])


def swapped(value, by):
    return lax.ppermute(value, "mem", [(i, i ^ by) for i in range(lax.axis_size("mem"))])


VMEM = pl.BlockSpec(memory_space=pltpu.VMEM)


def call(kernel, outs, scratch, *operands, mb=8, us=1):
    return pl.pallas_call(
        kernel,
        out_shape=[jax.ShapeDtypeStruct(*o) for o in outs],
        in_specs=[VMEM] * len(operands),
        out_specs=[VMEM] * len(outs),
        scratch_shapes=[pltpu.VMEM(*s) for s in scratch],
        compiler_params=pltpu.CompilerParams(vmem_limit_bytes=mb * 2**20),
        cost_estimate=pl.CostEstimate(flops=us * 10**9, bytes_accessed=us * 3 * 10**6, transcendentals=0),
    )(*operands)


def per_device(members, enc_first, enc_second, enc_third, mix_weight, dec_first, dec_second):
    count, channels, rows, wide = members.shape
    half, quarter = rows // 2, rows // 4
    cols = wide // 4
    peers, lines = lax.axis_size("mem"), lax.axis_size("row")
    nb = cols // peers
    lanes = 512
    chunks = wide // lanes
    x = members.reshape(count * channels * rows, wide)
    nd, nu = count * channels * UP, count * channels * DOWN
    per = padded(nd, 8), padded(nu, 8)
    total = padded(5 * per[0], 16), padded(5 * per[1], 16)
    pack = functools.partial(pack_kernel, count, channels, rows)
    sizes = [(nd * chunks, lanes), (nu * chunks, lanes)]
    cut = (count * channels) // 2 * rows
    spreads, own, above, below = call(
        functools.partial(prepare_kernel, count, channels, per),
        [
            ((2, 256, 256), BF),
            ((5, 2, 48, 5 * channels * 8), BF),
            ((count, 2, 2, 48, total[0]), BF),
            ((count, 2, 48, total[1]), BF),
        ],
        [],
    )
    down, up = call(pack, [(s, BF) for s in sizes], [(s, F32) for s in sizes], x[:cut], x[cut:], below, mb=16, us=20)
    up = shifted(up, -1)
    down = shifted(down, 1)

    w1 = enc_first.transpose(1, 2, 3, 0)
    w2 = enc_second.transpose(2, 3, 0, 1).reshape(9, 64, 64)
    w3 = enc_third.transpose(2, 3, 0, 1).reshape(9, 16, 64)
    wide_cols = count * cols
    row_f32 = ((128, wide_cols), F32)
    third_f32 = ((32, wide_cols), F32)
    (
        h1, h_first, h_last, a_last, v_second, v_third, h2_mid,
        w2_big, w3_big, w1_down, w1_up, mix,
    ) = call(
        functools.partial(inner_kernel, count, channels, rows),
        [((256 * (half - 1), wide_cols), BF)]
        + [row_f32] * 3
        + [third_f32] * 2
        + [
            ((128, wide_cols), BF),
            ((128, 768), BF),
            ((64, 256), BF),
            ((count * 256, total[0]), BF),
            ((count * 128, total[1]), BF),
            ((32, count * CH_BOT), BF),
        ],
        [
            ((48, 64), F32),
            ((640, 5 * channels * 8), BF),
            ((count, rows // 8, 5 * channels * 8, cols), F32),
            ((rows // 8, 640, cols), F32),
            ((256, wide_cols), BF),
        ],
        x, w1, w2, w3, mix_weight, spreads, own, above, below, mb=24,
    )
    h2_low, carry = call(
        functools.partial(low_kernel, count, channels, per[1]),
        [((128, wide_cols), BF), ((count * CH_BOT, cols), BF)],
        [((total[1], cols), F32), ((256, wide_cols), BF)],
        up, spreads, w1_up, h_last, w2_big, a_last, w3_big, mb=12,
    )
    carry = shifted(carry, 1)
    a_first, a_second, mid = call(
        functools.partial(middle_kernel, count, half),
        [row_f32, row_f32, ((quarter - 2, 32, cols), F32)],
        [((256, (half // 2 - 2) * wide_cols), BF)],
        h1, h2_mid, h2_low, w2_big, w3_big, v_third, mix, mb=12,
    )
    pre, tail = call(
        functools.partial(top_kernel, count, channels, per[0]),
        [((count, CH_BOT, cols), F32), ((quarter * 32 - 32, cols + 256), F32)],
        [((total[0], cols), F32), ((512, wide_cols), BF), ((256, wide_cols), BF)],
        down, spreads, w1_down, h_first, w2_big, a_first, a_second, w3_big, v_second, mix, mid, mb=12,
    )
    slots = peers // 2
    chunk = (quarter * 32 + 16, 128)
    keep, send = call(
        functools.partial(chunk_kernel, nb),
        [((slots,) + chunk, BF)] * 2,
        [((32, cols + 256), F32)],
        pre, carry, mix, tail,
    )
    got = swapped(send, 1)
    mine, *others = call(pair_kernel, [(chunk, F32)] + [(chunk, BF)] * (slots - 1), [], keep, got)
    order = sorted(range(slots - 1), key=lambda k: (k == 0, k))
    moved = {k: swapped(others[k], 2 * (k + 1)) for k in order}
    ext = padded(nb + 2, 128)
    latent, first, second = call(
        functools.partial(latent_kernel, nb, quarter),
        [((quarter, 96, ext), BF), ((32, ext), BF), ((32, ext), BF)],
        [],
        mine, *[moved[k] for k in range(slots - 1)],
    )
    first = shifted(first, 1)
    second = shifted(second, -1)

    d1, d2, _ = lax.optimization_barrier((dec_first, dec_second, others[0]))
    d1 = d1.transpose(2, 3, 0, 1).reshape(16, 32, 32)
    d2 = d2.transpose(2, 3, 0, 1).reshape(16, 16, 32)
    inside, outside = split_rows(quarter)
    edge_parts = call(
        functools.partial(decoder_inner, nb),
        [
            ((2, 128, 96), BF),
            ((2, 256, 256), BF),
            ((2, 128, ext), F32),
            ((2, 256, nb), F32),
            ((4 * nb, 4 * nb), BF),
            ((16 * rows, 32 * len(outside)), BF),
            ((16 * rows, 4 * nb), F32),
        ],
        [
            ((128, 288), BF),
            ((128, 384), BF),
            ((quarter + 3, 96, ext), BF),
            ((128 * (half + 2), nb), BF),
            ((32 * len(inside), 4 * nb), BF),
        ],
        latent, d1, d2,
    )
    (out,) = call(
        functools.partial(decoder_kernel, nb),
        [((16, rows, 4 * nb), BF)],
        [((2, 96, ext), BF), ((2, 256, nb), BF), ((128, 4 * nb), BF)],
        first, second, *edge_parts,
    )
    return out


def solution(mesh):
    placed = (P("mem", None, "row", None), P(), P(), P(), P(), P(), P())
    return jax.shard_map(
        per_device, mesh=mesh, in_specs=placed, out_specs=P(None, "row", "mem"), check_vma=False
    )
```

```python
import functools

import jax
import jax.numpy as jnp
import numpy as np
from jax import lax
from jax.experimental import pallas as pl
from jax.experimental.pallas import tpu as pltpu
from jax.sharding import PartitionSpec as P

BF = jnp.bfloat16
F32 = jnp.float32
CH_BOT = 16
UP = 3
DOWN = 2
TRANSPOSED = [(p, i, 2 * i - p) for p in range(2) for i in range(3) if 0 <= 2 * i - p < 4]


def dot(a, b):
    return lax.dot_general(a, b, (((1,), (0,)), ((), ())), preferred_element_type=F32)


def dot_t(a, b):
    return lax.dot_general(a, b, (((0,), (0,)), ((), ())), preferred_element_type=F32)


def silu_of_half(y):
    return y + y * jnp.tanh(y)


def padded(n, to):
    return -(-n // to) * to


def spread(step, tile):
    one = np.zeros((step * tile, step * tile), np.float32)
    for q in range(step):
        for c in range(tile):
            one[step * c + q, q * tile + c] = 1
    return one


def shift_right(v):
    return jnp.concatenate([jnp.zeros_like(v[:, :1]), v[:, :-1]], axis=1)


def shift_left(v):
    return jnp.concatenate([v[:, 1:], jnp.zeros_like(v[:, :1])], axis=1)


def is_row(at):
    return jnp.where(lax.axis_index("row") == at, 0.0, 1.0).astype(F32)


def put_hidden(ref, at, lanes, value):
    v = value.astype(BF)
    even, odd = v[0:64], v[64:128]
    ref[at * 256 + 64 : at * 256 + 128, lanes] = even
    ref[at * 256 + 128 : at * 256 + 192, lanes] = odd
    ref[at * 256 : at * 256 + 64, lanes] = shift_right(odd)
    ref[at * 256 + 192 : at * 256 + 256, lanes] = shift_left(even)


def bottleneck(w):
    return silu_of_half(w[0:16] + shift_right(w[16:32])).astype(BF)


def apart(block, even_ref, odd_ref):
    first = dot(block[:, 0:256], even_ref)
    second = dot(block[:, 256:512], odd_ref)
    low = lax.broadcasted_iota(jnp.int32, (block.shape[0], 128), 1) < 64
    out = []
    for half in range(2):
        e, o = first[:, half * 128 : half * 128 + 128], second[:, half * 128 : half * 128 + 128]
        out.append(jnp.where(low, e, o))
        out.append(pltpu.roll(jnp.where(low, o, e), 64, 1))
    return out


def place_halo(source, spread_ref, y_ref, count, per):
    cols = y_ref.shape[1]
    if count % 8:
        for q in range(5):
            y_ref[q * per + count // 8 * 8 : (q + 1) * per, :] = jnp.zeros((8, cols), F32)
    if 5 * per < y_ref.shape[0]:
        y_ref[5 * per :, :] = jnp.zeros((y_ref.shape[0] - 5 * per, cols), F32)
    for q, z in enumerate(apart(source, spread_ref[0], spread_ref[1])):
        for t in range(cols // 128):
            y_ref[(q + 1) * per : (q + 1) * per + count, t * 128 : (t + 1) * 128] = z[t * count : (t + 1) * count]
    y_ref[0:per, :] = shift_right(y_ref[4 * per : 5 * per, :])
    return y_ref[...].astype(BF)


def prepare_kernel(members, channels, per, spread_ref, own_ref, above_ref, below_ref):
    row_of = lax.broadcasted_iota(jnp.int32, (256, 256), 0)
    lane_of = lax.broadcasted_iota(jnp.int32, (256, 256), 1)
    place = lane_of // 64
    for odd in range(2):
        spread_ref[odd] = jnp.where(row_of == 4 * (lane_of - 64 * place) + (place ^ odd), 1.0, 0.0).astype(BF)

    def tap_of(lanes):
        tap = lax.broadcasted_iota(jnp.int32, (48, lanes), 0)
        c = sum(((tap >= 9 * k).astype(jnp.int32) for k in range(1, channels)), jnp.zeros_like(tap))
        rest = tap - 9 * c
        dr = (rest >= 3).astype(jnp.int32) + (rest >= 6).astype(jnp.int32)
        return c, dr, rest - 3 * dr, lax.broadcasted_iota(jnp.int32, (48, lanes), 1)

    def one_hot(hit):
        return jnp.where(hit, 1.0, 0.0).astype(BF)

    c, dr, dc, lane = tap_of(own_ref.shape[3])
    for j in range(5):
        row = 2 * j + dr - 1
        for pc in range(2):
            at = ((2 * pc + dc) * channels + c) * 8 + row
            own_ref[j, pc] = one_hot((lane == at) & (row >= 0) & (row < 8))
    c, dr, dc, lane = tap_of(above_ref.shape[4])
    for m in range(members):
        for kind in range(2):
            slot = dr + 2 * kind
            for pc in range(2):
                at = (2 * pc + dc) * per[0] + (m * channels + c) * UP + slot
                above_ref[m, kind, pc] = one_hot((lane == at) & (slot < UP))
    c, dr, dc, lane = tap_of(below_ref.shape[3])
    for m in range(members):
        for pc in range(2):
            at = (2 * pc + dc) * per[1] + (m * channels + c) * DOWN + dr - 1
            below_ref[m, pc] = one_hot((lane == at) & (dr >= 1))


def pack_kernel(members, channels, rows, x_ref, _, down_ref, up_ref, d_scr, u_scr):
    wide = x_ref.shape[1]
    lanes = down_ref.shape[1]
    nd, nu = members * channels * UP, members * channels * DOWN
    for t in range(wide // lanes):
        for g in range(members * channels):
            block = x_ref[g * rows : (g + 1) * rows, t * lanes : (t + 1) * lanes].astype(F32)
            d_scr[t * nd + g * UP : t * nd + (g + 1) * UP, :] = block[rows - UP : rows]
            u_scr[t * nu + g * DOWN : t * nu + (g + 1) * DOWN, :] = block[0:DOWN]
    down_ref[...] = d_scr[...].astype(BF)
    up_ref[...] = u_scr[...].astype(BF)


def inner_kernel(
    members, channels, rows,
    x_ref, w1_ref, w2_ref, w3_ref, mix_ref, spread_ref, own_ref, above_ref, below_ref,
    h1_ref, h_first, h_last, a_last, v_second, v_third, h2_mid,
    w2_big, w3_big, w1_down, w1_up, mix_own,
    w1_flat, w1_own, y_ref, out1_ref, h2_ref,
):
    half, groups = rows // 2, rows // 8
    wide = x_ref.shape[1]
    cols = wide // 4

    w1_flat[...] = jnp.zeros_like(w1_flat)
    for c in range(channels):
        for dr in range(3):
            at = (c * 3 + dr) * 3
            w1_flat[at : at + 3, :] = 0.5 * w1_ref[c, dr].astype(F32)
    w1 = w1_flat[...].astype(BF)
    for pc in range(2):
        for j in range(5):
            at = j * 128 + pc * 64
            w1_own[at : at + 64, :] = dot_t(w1, own_ref[j, pc]).astype(BF)
        for m in range(members):
            for kind in range(2):
                at = m * 256 + kind * 128 + pc * 64
                w1_down[at : at + 64, :] = dot_t(w1, above_ref[m, kind, pc]).astype(BF)
            at = m * 128 + pc * 64
            w1_up[at : at + 64, :] = dot_t(w1, below_ref[m, pc]).astype(BF)
    w2_big[...] = jnp.zeros_like(w2_big)
    for ocol in range(2):
        for dr in range(3):
            for dc in range(3):
                at = dr * 256 + (ocol + dc) * 64
                w2_big[ocol * 64 : ocol * 64 + 64, at : at + 64] = (0.5 * w2_ref[dr * 3 + dc].astype(F32)).astype(BF)
    w3_big[...] = jnp.zeros_like(w3_big)
    for dr, to, base in ((1, 0, 0), (2, 0, 128), (0, 2, 128)):
        for dc, moved, at in ((1, 0, 0), (2, 0, 64), (0, 1, 64)):
            w3_big[(to + moved) * 16 : (to + moved + 1) * 16, base + at : base + at + 64] = (
                0.5 * w3_ref[dr * 3 + dc].astype(F32)
            ).astype(BF)
    own_lanes = members * CH_BOT
    total = mix_ref.shape[1]
    start = lax.axis_index("mem") * own_lanes
    mix = pltpu.roll(mix_ref[...].astype(F32), lax.rem(total - start, total), 1)[:, 0:own_lanes].astype(BF)
    mix_own[...] = mix

    for t in range(wide // 512):
        for q, z in enumerate(apart(x_ref[:, 512 * t : 512 * (t + 1)], spread_ref[0], spread_ref[1])):
            for m in range(members):
                for c in range(channels):
                    for g in range(groups):
                        at = ((q + 1) * channels + c) * 8
                        frm = (m * channels + c) * rows + g * 8
                        y_ref[m, g, at : at + 8, t * 128 : (t + 1) * 128] = z[frm : frm + 8]
    c8 = channels * 8
    for m in range(members):
        for g in range(groups):
            y_ref[m, g, 0:c8, :] = shift_right(y_ref[m, g, 4 * c8 : 5 * c8, :])

    for m in range(members):
        for g in range(groups):
            out1_ref[g] = dot(w1_own[...], y_ref[m, g].astype(BF))
        lanes = slice(m * cols, (m + 1) * cols)
        h_first[:, lanes] = out1_ref[0, 0:128]
        h_last[:, lanes] = out1_ref[groups - 1, 512:640]
        for h in range(1, half):
            g, j = h // 4, h % 4
            v = out1_ref[g, j * 128 : j * 128 + 128]
            if j == 0:
                v = v + out1_ref[g - 1, 512:640]
            put_hidden(h1_ref, h - 1, lanes, silu_of_half(v))
    a_last[...] = dot(w2_big[:, 0:512], h1_ref[(half - 3) * 256 : (half - 1) * 256, :])
    for o in range(2):
        h2_ref[o * 128 : o * 128 + 128, :] = silu_of_half(
            dot(w2_big[...], h1_ref[o * 256 : (o + 3) * 256, :])
        ).astype(BF)
    v = dot(w3_big[...], h2_ref[...])
    v_second[...] = v[0:32]
    v_third[...] = v[32:64]
    h2_mid[...] = silu_of_half(dot(w2_big[...], h1_ref[512:1280, :])).astype(BF)


def low_kernel(
    members, channels, per,
    got_ref, spread_ref, w1_ref, h_ref, w2_ref, a_ref, w3_ref,
    h2_ref, carry_ref, y_ref, h1_ref,
):
    below = is_row(lax.axis_size("row") - 1)
    y = place_halo(got_ref[...], spread_ref, y_ref, members * channels * DOWN, per)
    cols = y_ref.shape[1]
    fresh = dot(w1_ref[...], y)
    for m in range(members):
        lanes = slice(m * cols, (m + 1) * cols)
        put_hidden(h1_ref, 0, lanes, silu_of_half((fresh[m * 128 : m * 128 + 128] + h_ref[:, lanes]) * below))
    h2 = silu_of_half(dot(w2_ref[:, 512:768], h1_ref[...]) + a_ref[...]).astype(BF)
    h2_ref[...] = h2
    v = dot(w3_ref[32:64, 128:256], h2)
    for m in range(members):
        lanes = slice(m * cols, (m + 1) * cols)
        carry_ref[m * 16 : m * 16 + 16, :] = (v[0:16, lanes] + shift_right(v[16:32, lanes])).astype(BF)


def middle_kernel(
    members, half,
    h1_ref, h2_mid, h2_low, w2_ref, w3_ref, v_ref, mix_ref,
    a_first, a_second, mixed_ref, h2_ref,
):
    wide = h1_ref.shape[1]
    cols = wide // members
    a_first[...] = dot(w2_ref[:, 512:768], h1_ref[0:256, :])
    a_second[...] = dot(w2_ref[:, 256:768], h1_ref[0:512, :])
    pairs = range(4, half, 2)
    for n, a in enumerate(pairs):
        lanes = slice(n * wide, (n + 1) * wide)
        for o in (a, a + 1):
            at = slice((o - a) * 128, (o - a) * 128 + 128)
            if o == half - 1:
                h2_ref[at, lanes] = h2_low[...]
            elif o == 4:
                h2_ref[at, lanes] = h2_mid[...]
            else:
                h2_ref[at, lanes] = silu_of_half(
                    dot(w2_ref[...], h1_ref[(o - 2) * 256 : (o + 1) * 256, :])
                ).astype(BF)
    v = dot(w3_ref[...], h2_ref[...])
    carry = v_ref[...]
    for n in range(len(pairs)):
        w = v[0:32, n * wide : (n + 1) * wide] + carry
        carry = v[32:64, n * wide : (n + 1) * wide]
        parts = [bottleneck(w[:, m * cols : (m + 1) * cols]) for m in range(members)]
        mixed_ref[n] = dot(mix_ref[...], jnp.concatenate(parts, axis=0))


def top_kernel(
    members, channels, per,
    got_ref, spread_ref, w1_ref, h_ref, w2_ref, a_first, a_second, w3_ref, v_ref, mix_ref, mid_ref,
    pre_ref, tail_ref, y_ref, h1_ref, h2_ref,
):
    source = (got_ref[...].astype(F32) * is_row(0)).astype(BF)
    y = place_halo(source, spread_ref, y_ref, members * channels * UP, per)
    cols = y_ref.shape[1]
    fresh = dot(w1_ref[...], y)
    for m in range(members):
        lanes = slice(m * cols, (m + 1) * cols)
        put_hidden(h1_ref, 0, lanes, silu_of_half(fresh[m * 256 : m * 256 + 128]))
        put_hidden(h1_ref, 1, lanes, silu_of_half(fresh[m * 256 + 128 : m * 256 + 256] + h_ref[:, lanes]))
    h2_ref[0:128, :] = silu_of_half(dot(w2_ref[:, 0:512], h1_ref[...]) + a_first[...]).astype(BF)
    h2_ref[128:256, :] = silu_of_half(dot(w2_ref[:, 0:256], h1_ref[256:512, :]) + a_second[...]).astype(BF)
    v = dot(w3_ref[...], h2_ref[...])
    second = []
    for m in range(members):
        lanes = slice(m * cols, (m + 1) * cols)
        pre_ref[m] = v[0:16, lanes] + shift_right(v[16:32, lanes])
        second.append(bottleneck(v[32:64, lanes] + v_ref[:, lanes]))
    tall = tail_ref.shape[0]
    tail_ref[:, 0:128] = jnp.zeros((tall, 128), F32)
    tail_ref[:, 128 + cols : 256 + cols] = jnp.zeros((tall, 128), F32)
    inside = slice(128, 128 + cols)
    tail_ref[0:32, inside] = dot(mix_ref[...], jnp.concatenate(second, axis=0))
    for r in range(mid_ref.shape[0]):
        tail_ref[(r + 1) * 32 : (r + 2) * 32, inside] = mid_ref[r]


def chunk_kernel(nb, pre_ref, carry_ref, mix_ref, tail_ref, keep_ref, send_ref, head_ref):
    members, _, cols = pre_ref.shape
    carry = carry_ref[...].astype(F32) * is_row(0)
    first = [
        silu_of_half(pre_ref[m] + carry[m * 16 : m * 16 + 16]).astype(BF) for m in range(members)
    ]
    head_ref[:, 0:128] = jnp.zeros((32, 128), F32)
    head_ref[:, 128 + cols : 256 + cols] = jnp.zeros((32, 128), F32)
    head_ref[:, 128 : 128 + cols] = dot(mix_ref[...], jnp.concatenate(first, axis=0))

    me = lax.axis_index("mem")
    slots = lax.axis_size("mem") // 2
    tall = 32 + tail_ref.shape[0]

    def tile_at(base):
        at = pl.ds(pl.multiple_of(base, 128), 128)
        return jnp.concatenate([head_ref[:, at], tail_ref[:, at]], axis=0)

    def lanes_from(lane):
        v = tile_at(lane // 128 * 128)
        return v if nb % 128 == 0 else pltpu.roll(v, (128 - lane % 128) % 128, 1)

    lane_at = lax.broadcasted_iota(jnp.int32, (tall, 128), 1)
    edges = jnp.zeros((tall, 128), F32)
    for side, ref in enumerate((keep_ref, send_ref)):
        for k in range(slots):
            start = 128 + (me ^ (2 * k + side)) * nb
            ref[k, 0:tall, :] = lanes_from(start).astype(BF)
            if nb % 128 == 0:
                left = tile_at(start - 128)[:, 127:128]
            else:
                left = lanes_from(start - 1)[:, 0:1]
            right = lanes_from(start + nb)[:, 0:1]
            at = 2 * (side * slots + k)
            edges = jnp.where(lane_at == at, left, edges)
            edges = jnp.where(lane_at == at + 1, right, edges)
    turned = edges.T
    for side, ref in enumerate((keep_ref, send_ref)):
        for k in range(slots):
            at = 2 * (side * slots + k)
            ref[k, tall : tall + 16, :] = jnp.concatenate(
                [turned[at : at + 2], jnp.zeros((14, 128), F32)], axis=0
            ).astype(BF)


def pair_kernel(keep_ref, got_ref, own_ref, *out_refs):
    own_ref[...] = keep_ref[0].astype(F32) + got_ref[0].astype(F32)
    for k, ref in enumerate(out_refs):
        ref[...] = (keep_ref[k + 1].astype(F32) + got_ref[k + 1].astype(F32)).astype(BF)


def put_latent(ref, at, line):
    ext = line.shape[1]
    ref[at, 0:32, :] = pltpu.roll(line, 1, 1).astype(BF)
    ref[at, 32:64, :] = line.astype(BF)
    ref[at, 64:96, :] = pltpu.roll(line, ext - 1, 1).astype(BF)


def latent_kernel(nb, quarter, own_ref, *refs):
    line_ref, first_ref, second_ref = refs[-3:]
    total = own_ref[...]
    for ref in refs[:-3]:
        total = total + ref[...].astype(F32)
    latent = silu_of_half(0.5 * total)
    tall = quarter * 32
    turned = jnp.concatenate([latent[tall : tall + 16], jnp.zeros((112, 128), F32)], axis=0).T
    ext = line_ref.shape[1]
    lines = []
    for r in range(quarter):
        rows = slice(r * 32, (r + 1) * 32)
        line = [latent[rows, 0:nb], turned[rows, 1:2], jnp.zeros((32, ext - nb - 2), F32), turned[rows, 0:1]]
        lines.append(jnp.concatenate(line, axis=1))
        line_ref[rows, :] = lines[-1].astype(BF)
    first_ref[...] = lines[-1].astype(BF)
    second_ref[...] = lines[0].astype(BF)


def upsample_row(w1, l_ref, a, keep_even, keep_odd, rows, u_ref, wanted, keeps):
    wide = l_ref.shape[2]
    nb = u_ref.shape[1]
    v = silu_of_half(dot(w1, l_ref[a + 1 : a + 4].reshape(288, wide)))
    for pr in range(2):
        row = 2 * a + pr
        if row not in wanted:
            continue
        even = v[pr * 64 : pr * 64 + 32] * keep_even
        odd = v[pr * 64 + 32 : pr * 64 + 64] * keep_odd
        if row in keeps:
            even, odd = even * keeps[row], odd * keeps[row]
        at = (row + 1) * 128
        u_ref[at : at + 32, :] = pltpu.roll(odd, 1, 1)[:, 0:nb].astype(BF)
        u_ref[at + 32 : at + 64, :] = even[:, 0:nb].astype(BF)
        u_ref[at + 64 : at + 96, :] = odd[:, 0:nb].astype(BF)
        u_ref[at + 96 : at + 128, :] = pltpu.roll(even, wide - 1, 1)[:, 0:nb].astype(BF)


def column_keeps(nb, wide):
    mem_at, mem_last = lax.axis_index("mem"), lax.axis_size("mem") - 1
    lane = lax.broadcasted_iota(jnp.int32, (32, wide), 1)
    keep_odd = jnp.where((lane == wide - 1) & (mem_at == 0), 0.0, 1.0).astype(F32)
    keep_even = jnp.where((lane == nb) & (mem_at == mem_last), 0.0, 1.0).astype(F32)
    return keep_even, keep_odd


def field_rows(w2, u_ref, g_ref, which):
    nb = u_ref.shape[1]
    for n, a in enumerate(which):
        v = dot(w2, u_ref[a * 128 : (a + 3) * 128, :]).astype(BF)
        for pr in range(2):
            for ph in range(4):
                g_ref[(2 * n + pr) * 16 : (2 * n + pr + 1) * 16, ph * nb : (ph + 1) * nb] = v[
                    (pr * 4 + ph) * 16 : (pr * 4 + ph + 1) * 16
                ]


def level_first(rows, which):
    count = 32 * len(which)
    to = lax.broadcasted_iota(jnp.int32, (16 * rows, count), 0)
    frm = lax.broadcasted_iota(jnp.int32, (16 * rows, count), 1)
    level, row = to // rows, lax.rem(to, rows)
    hit = jnp.zeros(to.shape, jnp.bool_)
    for n, a in enumerate(which):
        for pr in range(2):
            hit = hit | ((row == 2 * a + pr) & (frm == (2 * n + pr) * 16 + level))
    return jnp.where(hit, 1.0, 0.0).astype(BF)


def split_rows(rows):
    inside = [a for a in range(2, 2 * rows - 2)]
    return inside, [a for a in range(2 * rows) if a not in inside]


def by_phase(v):
    return jnp.concatenate(
        [v[(pr * 4 + ph) * 16 : (pr * 4 + ph + 1) * 16] for ph in range(4) for pr in range(2)], axis=0
    )


def merge_phases(a, b):
    return jnp.concatenate([v[ph * 32 : ph * 32 + 32] for ph in range(4) for v in (a, b)], axis=0)


def decoder_inner(
    nb, line_ref, d1_ref, d2_ref,
    w_edge, w_field, up_part, field_part, join_ref, turn_ref, part_ref, wd1, wd2, l_ref, u_ref, g_ref,
):
    wd1[...] = jnp.zeros_like(wd1)
    wd2[...] = jnp.zeros_like(wd2)
    for pr, rr, tr in TRANSPOSED:
        for pc, cc, tc in TRANSPOSED:
            wd1[(pr * 2 + pc) * 32 : (pr * 2 + pc + 1) * 32, (rr * 3 + cc) * 32 : (rr * 3 + cc + 1) * 32] = (
                0.5 * d1_ref[tr * 4 + tc].astype(F32)
            ).astype(BF)
            for q in range(2):
                at = pr * 4 + 2 * q + pc
                to = rr * 4 + q + cc
                wd2[at * 16 : (at + 1) * 16, to * 32 : (to + 1) * 32] = d2_ref[tr * 4 + tc]
    rows, wide = line_ref.shape[0] // 32, line_ref.shape[1]
    frm = lax.broadcasted_iota(jnp.int32, join_ref.shape, 0)
    to = lax.broadcasted_iota(jnp.int32, join_ref.shape, 1)
    place = frm // nb
    join_ref[...] = jnp.where(to == 4 * (frm - nb * place) + place, 1.0, 0.0).astype(BF)
    inside, outside = split_rows(rows)
    turn_ref[...] = level_first(4 * rows, outside)

    l_ref[0] = jnp.zeros_like(l_ref[0])
    l_ref[1] = jnp.zeros_like(l_ref[0])
    for r in range(rows):
        put_latent(l_ref, r + 2, line_ref[r * 32 : r * 32 + 32, :].astype(F32))
    l_ref[rows + 2] = jnp.zeros_like(l_ref[0])
    u_ref[...] = jnp.zeros_like(u_ref)
    keep_even, keep_odd = column_keeps(nb, wide)
    for a in range(rows):
        upsample_row(wd1[...], l_ref, a, keep_even, keep_odd, rows, u_ref, range(1, 2 * rows - 1), {})
    field_rows(wd2[...], u_ref, g_ref, inside)
    g = dot(level_first(4 * rows, inside), g_ref[...]).astype(BF)
    part_ref[...] = dot(g, join_ref[...])

    w_edge[0, 0:64, :] = wd1[64:128, 96:192]
    w_edge[0, 64:128, :] = wd1[0:64, 0:96]
    w_edge[1, 0:64, :] = wd1[64:128, 192:288]
    w_edge[1, 64:128, :] = wd1[0:64, 96:192]
    up_part[0] = dot(w_edge[1], l_ref[2])
    up_part[1] = dot(w_edge[0], l_ref[rows + 1])

    def known(taps, first, count):
        return by_phase(dot(wd2[:, taps : taps + 128 * count], u_ref[(first + 1) * 128 : (first + 1 + count) * 128, :]))

    last = 2 * rows - 1
    field_part[0] = merge_phases(known(256, 1, 1), known(128, 1, 2))
    field_part[1] = merge_phases(known(0, last - 2, 2), known(0, last - 1, 1))
    none = jnp.zeros((128, 128), BF)
    w = [by_phase(wd2[:, rr * 128 : rr * 128 + 128]) for rr in range(3)]
    w_field[0] = merge_phases(jnp.concatenate([w[0], w[1]], axis=1), jnp.concatenate([none, w[0]], axis=1))
    w_field[1] = merge_phases(jnp.concatenate([w[2], none], axis=1), jnp.concatenate([w[1], w[2]], axis=1))


def decoder_kernel(
    nb, first_ref, second_ref, w_edge, w_field, up_part, field_part, join_ref, turn_ref, part_ref,
    out_ref, l_ref, u_ref, g_ref,
):
    odd_row = lax.rem(lax.axis_index("row"), 2) == 1
    keeps = is_row(0), is_row(lax.axis_size("row") - 1)
    wide = l_ref.shape[2]
    first, second = first_ref[...].astype(F32), second_ref[...].astype(F32)
    put_latent(l_ref, 0, first * keeps[0])
    put_latent(l_ref, 1, second * keeps[1])
    keep_even, keep_odd = column_keeps(nb, wide)
    for side in range(2):
        v = silu_of_half(dot(w_edge[side], l_ref[side]) + up_part[side])
        for line in range(2):
            even = v[line * 64 : line * 64 + 32] * keep_even
            odd = v[line * 64 + 32 : line * 64 + 64] * keep_odd
            if line == side:
                even, odd = even * keeps[side], odd * keeps[side]
            at = line * 128
            u_ref[side, at : at + 32, :] = pltpu.roll(odd, 1, 1)[:, 0:nb].astype(BF)
            u_ref[side, at + 32 : at + 64, :] = even[:, 0:nb].astype(BF)
            u_ref[side, at + 64 : at + 96, :] = odd[:, 0:nb].astype(BF)
            u_ref[side, at + 96 : at + 128, :] = pltpu.roll(even, wide - 1, 1)[:, 0:nb].astype(BF)
        v = (dot(w_field[side], u_ref[side]) + field_part[side]).astype(BF)
        for ph in range(4):
            g_ref[side * 64 : side * 64 + 64, ph * nb : (ph + 1) * nb] = v[ph * 64 : ph * 64 + 64]
    g = dot(g_ref[...], join_ref[...]).astype(BF)
    out_ref[...] = (dot(turn_ref[...], g) + part_ref[...]).astype(BF).reshape(out_ref.shape)


def shifted(value, by):
    peers = lax.axis_size("row")
    return lax.ppermute(value, "row", [(i, (i + by) % peers) for i in range(peers)])


def swapped(value, by):
    return lax.ppermute(value, "mem", [(i, i ^ by) for i in range(lax.axis_size("mem"))])


VMEM = pl.BlockSpec(memory_space=pltpu.VMEM)


def call(kernel, outs, scratch, *operands, mb=8, us=1):
    return pl.pallas_call(
        kernel,
        out_shape=[jax.ShapeDtypeStruct(*o) for o in outs],
        in_specs=[VMEM] * len(operands),
        out_specs=[VMEM] * len(outs),
        scratch_shapes=[pltpu.VMEM(*s) for s in scratch],
        compiler_params=pltpu.CompilerParams(vmem_limit_bytes=mb * 2**20),
        cost_estimate=pl.CostEstimate(flops=us * 10**9, bytes_accessed=us * 3 * 10**6, transcendentals=0),
    )(*operands)


def per_device(members, enc_first, enc_second, enc_third, mix_weight, dec_first, dec_second):
    count, channels, rows, wide = members.shape
    half, quarter = rows // 2, rows // 4
    cols = wide // 4
    peers, lines = lax.axis_size("mem"), lax.axis_size("row")
    nb = cols // peers
    lanes = 512
    chunks = wide // lanes
    x = members.reshape(count * channels * rows, wide)
    nd, nu = count * channels * UP, count * channels * DOWN
    per = padded(nd, 8), padded(nu, 8)
    total = padded(5 * per[0], 16), padded(5 * per[1], 16)
    pack = functools.partial(pack_kernel, count, channels, rows)
    sizes = [(nd * chunks, lanes), (nu * chunks, lanes)]
    spreads, own, above, below = call(
        functools.partial(prepare_kernel, count, channels, per),
        [
            ((2, 256, 256), BF),
            ((5, 2, 48, 5 * channels * 8), BF),
            ((count, 2, 2, 48, total[0]), BF),
            ((count, 2, 48, total[1]), BF),
        ],
        [],
        us=20,
    )
    down, up = call(pack, [(s, BF) for s in sizes], [(s, F32) for s in sizes], x, below, mb=16, us=20)
    up = shifted(up, -1)
    down = shifted(down, 1)

    w1 = enc_first.transpose(1, 2, 3, 0)
    w2 = enc_second.transpose(2, 3, 0, 1).reshape(9, 64, 64)
    w3 = enc_third.transpose(2, 3, 0, 1).reshape(9, 16, 64)
    wide_cols = count * cols
    row_f32 = ((128, wide_cols), F32)
    third_f32 = ((32, wide_cols), F32)
    (
        h1, h_first, h_last, a_last, v_second, v_third, h2_mid,
        w2_big, w3_big, w1_down, w1_up, mix,
    ) = call(
        functools.partial(inner_kernel, count, channels, rows),
        [((256 * (half - 1), wide_cols), BF)]
        + [row_f32] * 3
        + [third_f32] * 2
        + [
            ((128, wide_cols), BF),
            ((128, 768), BF),
            ((64, 256), BF),
            ((count * 256, total[0]), BF),
            ((count * 128, total[1]), BF),
            ((32, count * CH_BOT), BF),
        ],
        [
            ((48, 64), F32),
            ((640, 5 * channels * 8), BF),
            ((count, rows // 8, 5 * channels * 8, cols), F32),
            ((rows // 8, 640, cols), F32),
            ((256, wide_cols), BF),
        ],
        x, w1, w2, w3, mix_weight, spreads, own, above, below, mb=24,
    )
    h2_low, carry = call(
        functools.partial(low_kernel, count, channels, per[1]),
        [((128, wide_cols), BF), ((count * CH_BOT, cols), BF)],
        [((total[1], cols), F32), ((256, wide_cols), BF)],
        up, spreads, w1_up, h_last, w2_big, a_last, w3_big, mb=12,
    )
    carry = shifted(carry, 1)
    a_first, a_second, mid = call(
        functools.partial(middle_kernel, count, half),
        [row_f32, row_f32, ((quarter - 2, 32, cols), F32)],
        [((256, (half // 2 - 2) * wide_cols), BF)],
        h1, h2_mid, h2_low, w2_big, w3_big, v_third, mix, mb=12,
    )
    pre, tail = call(
        functools.partial(top_kernel, count, channels, per[0]),
        [((count, CH_BOT, cols), F32), ((quarter * 32 - 32, cols + 256), F32)],
        [((total[0], cols), F32), ((512, wide_cols), BF), ((256, wide_cols), BF)],
        down, spreads, w1_down, h_first, w2_big, a_first, a_second, w3_big, v_second, mix, mid, mb=12,
    )
    slots = peers // 2
    chunk = (quarter * 32 + 16, 128)
    keep, send = call(
        functools.partial(chunk_kernel, nb),
        [((slots,) + chunk, BF)] * 2,
        [((32, cols + 256), F32)],
        pre, carry, mix, tail,
    )
    got = swapped(send, 1)
    mine, *others = call(pair_kernel, [(chunk, F32)] + [(chunk, BF)] * (slots - 1), [], keep, got)
    order = sorted(range(slots - 1), key=lambda k: (k == 0, k))
    moved = {k: swapped(others[k], 2 * (k + 1)) for k in order}
    ext = padded(nb + 2, 128)
    latent, first, second = call(
        functools.partial(latent_kernel, nb, quarter),
        [((quarter * 32, ext), BF), ((32, ext), BF), ((32, ext), BF)],
        [],
        mine, *[moved[k] for k in range(slots - 1)],
    )
    first = shifted(first, 1)
    second = shifted(second, -1)

    d1, d2, _ = lax.optimization_barrier((dec_first, dec_second, others[0]))
    d1 = d1.transpose(2, 3, 0, 1).reshape(16, 32, 32)
    d2 = d2.transpose(2, 3, 0, 1).reshape(16, 16, 32)
    inside, outside = split_rows(quarter)
    edge_parts = call(
        functools.partial(decoder_inner, nb),
        [
            ((2, 128, 96), BF),
            ((2, 256, 256), BF),
            ((2, 128, ext), F32),
            ((2, 256, nb), F32),
            ((4 * nb, 4 * nb), BF),
            ((16 * rows, 32 * len(outside)), BF),
            ((16 * rows, 4 * nb), F32),
        ],
        [
            ((128, 288), BF),
            ((128, 384), BF),
            ((quarter + 3, 96, ext), BF),
            ((128 * (half + 2), nb), BF),
            ((32 * len(inside), 4 * nb), BF),
        ],
        latent, d1, d2,
    )
    (out,) = call(
        functools.partial(decoder_kernel, nb),
        [((16, rows, 4 * nb), BF)],
        [((2, 96, ext), BF), ((2, 256, nb), BF), ((128, 4 * nb), BF)],
        first, second, *edge_parts,
    )
    return out


def solution(mesh):
    placed = (P("mem", None, "row", None), P(), P(), P(), P(), P(), P())
    return jax.shard_map(
        per_device, mesh=mesh, in_specs=placed, out_specs=P(None, "row", "mem"), check_vma=False
    )
```

```python
import functools

import jax
import jax.numpy as jnp
import numpy as np
from jax import lax
from jax.experimental import pallas as pl
from jax.experimental.pallas import tpu as pltpu
from jax.sharding import PartitionSpec as P

BF = jnp.bfloat16
F32 = jnp.float32
CH_BOT = 16
EDGES = 8
UP = 3
DOWN = 2
TRANSPOSED = [(p, i, 2 * i - p) for p in range(2) for i in range(3) if 0 <= 2 * i - p < 4]


def dot(a, b):
    return lax.dot_general(a, b, (((1,), (0,)), ((), ())), preferred_element_type=F32)


def dot_t(a, b):
    return lax.dot_general(a, b, (((0,), (0,)), ((), ())), preferred_element_type=F32)


def silu_of_half(y):
    return y + y * jnp.tanh(y)


def padded(n, to):
    return -(-n // to) * to


def spread(step, tile):
    one = np.zeros((step * tile, step * tile), np.float32)
    for q in range(step):
        for c in range(tile):
            one[step * c + q, q * tile + c] = 1
    return one


def shift_right(v):
    return jnp.concatenate([jnp.zeros_like(v[:, :1]), v[:, :-1]], axis=1)


def shift_left(v):
    return jnp.concatenate([v[:, 1:], jnp.zeros_like(v[:, :1])], axis=1)


def is_row(at):
    return jnp.where(lax.axis_index("row") == at, 0.0, 1.0).astype(F32)


def put_hidden(ref, at, lanes, value):
    v = value.astype(BF)
    even, odd = v[0:64], v[64:128]
    ref[at * 256 + 64 : at * 256 + 128, lanes] = even
    ref[at * 256 + 128 : at * 256 + 192, lanes] = odd
    ref[at * 256 : at * 256 + 64, lanes] = shift_right(odd)
    ref[at * 256 + 192 : at * 256 + 256, lanes] = shift_left(even)


def put_line(ref, at, line):
    rows, cols = slice(at, at + 32), line.shape[1]
    ref[rows, 0:128] = jnp.zeros((32, 128), F32)
    ref[rows, 128 : 128 + cols] = line
    ref[rows, 128 + cols : 256 + cols] = jnp.zeros((32, 128), F32)


def bottleneck(w):
    return silu_of_half(w[0:16] + shift_right(w[16:32])).astype(BF)


def apart(block, even_ref, odd_ref):
    first = dot(block[:, 0:256], even_ref)
    second = dot(block[:, 256:512], odd_ref)
    low = lax.broadcasted_iota(jnp.int32, (block.shape[0], 128), 1) < 64
    out = []
    for half in range(2):
        e, o = first[:, half * 128 : half * 128 + 128], second[:, half * 128 : half * 128 + 128]
        out.append(jnp.where(low, e, o))
        out.append(pltpu.roll(jnp.where(low, o, e), 64, 1))
    return out


def place_halo(source, spread_ref, y_ref, count, per):
    cols = y_ref.shape[1]
    if count % 8:
        for q in range(5):
            y_ref[q * per + count // 8 * 8 : (q + 1) * per, :] = jnp.zeros((8, cols), F32)
    if 5 * per < y_ref.shape[0]:
        y_ref[5 * per :, :] = jnp.zeros((y_ref.shape[0] - 5 * per, cols), F32)
    for q, z in enumerate(apart(source, spread_ref[0], spread_ref[1])):
        for t in range(cols // 128):
            y_ref[(q + 1) * per : (q + 1) * per + count, t * 128 : (t + 1) * 128] = z[t * count : (t + 1) * count]
    y_ref[0:per, :] = shift_right(y_ref[4 * per : 5 * per, :])
    return y_ref[...].astype(BF)


def prepare_kernel(members, channels, per, spread_ref, own_ref, above_ref, below_ref):
    row_of = lax.broadcasted_iota(jnp.int32, (256, 256), 0)
    lane_of = lax.broadcasted_iota(jnp.int32, (256, 256), 1)
    place = lane_of // 64
    for odd in range(2):
        spread_ref[odd] = jnp.where(row_of == 4 * (lane_of - 64 * place) + (place ^ odd), 1.0, 0.0).astype(BF)

    def tap_of(lanes):
        tap = lax.broadcasted_iota(jnp.int32, (48, lanes), 0)
        c = sum(((tap >= 9 * k).astype(jnp.int32) for k in range(1, channels)), jnp.zeros_like(tap))
        rest = tap - 9 * c
        dr = (rest >= 3).astype(jnp.int32) + (rest >= 6).astype(jnp.int32)
        return c, dr, rest - 3 * dr, lax.broadcasted_iota(jnp.int32, (48, lanes), 1)

    def one_hot(hit):
        return jnp.where(hit, 1.0, 0.0).astype(BF)

    c, dr, dc, lane = tap_of(own_ref.shape[3])
    for j in range(5):
        row = 2 * j + dr - 1
        for pc in range(2):
            at = ((2 * pc + dc) * channels + c) * 8 + row
            own_ref[j, pc] = one_hot((lane == at) & (row >= 0) & (row < 8))
    c, dr, dc, lane = tap_of(above_ref.shape[4])
    for m in range(members):
        for kind in range(2):
            slot = dr + 2 * kind
            for pc in range(2):
                at = (2 * pc + dc) * per[0] + (m * channels + c) * UP + slot
                above_ref[m, kind, pc] = one_hot((lane == at) & (slot < UP))
    c, dr, dc, lane = tap_of(below_ref.shape[3])
    for m in range(members):
        for pc in range(2):
            at = (2 * pc + dc) * per[1] + (m * channels + c) * DOWN + dr - 1
            below_ref[m, pc] = one_hot((lane == at) & (dr >= 1))


def pack_kernel(members, channels, rows, x_ref, _, down_ref, up_ref, d_scr, u_scr):
    wide = x_ref.shape[1]
    lanes = down_ref.shape[1]
    nd, nu = members * channels * UP, members * channels * DOWN
    for t in range(wide // lanes):
        for g in range(members * channels):
            block = x_ref[g * rows : (g + 1) * rows, t * lanes : (t + 1) * lanes].astype(F32)
            d_scr[t * nd + g * UP : t * nd + (g + 1) * UP, :] = block[rows - UP : rows]
            u_scr[t * nu + g * DOWN : t * nu + (g + 1) * DOWN, :] = block[0:DOWN]
    down_ref[...] = d_scr[...].astype(BF)
    up_ref[...] = u_scr[...].astype(BF)


def inner_kernel(
    members, channels, rows,
    x_ref, w1_ref, w2_ref, w3_ref, mix_ref, spread_ref, own_ref, above_ref, below_ref,
    h1_ref, h_first, h_last, a_last, v_second, v_third, h2_mid,
    w2_big, w3_big, w1_down, w1_up, mix_own,
    w1_flat, w1_own, y_ref, out1_ref, h2_ref,
):
    half, groups = rows // 2, rows // 8
    wide = x_ref.shape[1]
    cols = wide // 4

    w1_flat[...] = jnp.zeros_like(w1_flat)
    for c in range(channels):
        for dr in range(3):
            at = (c * 3 + dr) * 3
            w1_flat[at : at + 3, :] = 0.5 * w1_ref[c, dr].astype(F32)
    w1 = w1_flat[...].astype(BF)
    for pc in range(2):
        for j in range(5):
            at = j * 128 + pc * 64
            w1_own[at : at + 64, :] = dot_t(w1, own_ref[j, pc]).astype(BF)
        for m in range(members):
            for kind in range(2):
                at = m * 256 + kind * 128 + pc * 64
                w1_down[at : at + 64, :] = dot_t(w1, above_ref[m, kind, pc]).astype(BF)
            at = m * 128 + pc * 64
            w1_up[at : at + 64, :] = dot_t(w1, below_ref[m, pc]).astype(BF)
    w2_big[...] = jnp.zeros_like(w2_big)
    for ocol in range(2):
        for dr in range(3):
            for dc in range(3):
                at = dr * 256 + (ocol + dc) * 64
                w2_big[ocol * 64 : ocol * 64 + 64, at : at + 64] = (0.5 * w2_ref[dr * 3 + dc].astype(F32)).astype(BF)
    w3_big[...] = jnp.zeros_like(w3_big)
    for dr, to, base in ((1, 0, 0), (2, 0, 128), (0, 2, 128)):
        for dc, moved, at in ((1, 0, 0), (2, 0, 64), (0, 1, 64)):
            w3_big[(to + moved) * 16 : (to + moved + 1) * 16, base + at : base + at + 64] = (
                0.5 * w3_ref[dr * 3 + dc].astype(F32)
            ).astype(BF)
    own_lanes = members * CH_BOT
    total = mix_ref.shape[1]
    start = lax.axis_index("mem") * own_lanes
    mix = pltpu.roll(mix_ref[...].astype(F32), lax.rem(total - start, total), 1)[:, 0:own_lanes].astype(BF)
    mix_own[...] = mix

    for t in range(wide // 512):
        for q, z in enumerate(apart(x_ref[:, 512 * t : 512 * (t + 1)], spread_ref[0], spread_ref[1])):
            for m in range(members):
                for c in range(channels):
                    for g in range(groups):
                        at = ((q + 1) * channels + c) * 8
                        frm = (m * channels + c) * rows + g * 8
                        y_ref[m, g, at : at + 8, t * 128 : (t + 1) * 128] = z[frm : frm + 8]
    c8 = channels * 8
    for m in range(members):
        for g in range(groups):
            y_ref[m, g, 0:c8, :] = shift_right(y_ref[m, g, 4 * c8 : 5 * c8, :])

    for m in range(members):
        for g in range(groups):
            out1_ref[g] = dot(w1_own[...], y_ref[m, g].astype(BF))
        lanes = slice(m * cols, (m + 1) * cols)
        h_first[:, lanes] = out1_ref[0, 0:128]
        h_last[:, lanes] = out1_ref[groups - 1, 512:640]
        for h in range(1, half):
            g, j = h // 4, h % 4
            v = out1_ref[g, j * 128 : j * 128 + 128]
            if j == 0:
                v = v + out1_ref[g - 1, 512:640]
            put_hidden(h1_ref, h - 1, lanes, silu_of_half(v))
    a_last[...] = dot(w2_big[:, 0:512], h1_ref[(half - 3) * 256 : (half - 1) * 256, :])
    for o in range(2):
        h2_ref[o * 128 : o * 128 + 128, :] = silu_of_half(
            dot(w2_big[...], h1_ref[o * 256 : (o + 3) * 256, :])
        ).astype(BF)
    v = dot(w3_big[...], h2_ref[...])
    v_second[...] = v[0:32]
    v_third[...] = v[32:64]
    h2_mid[...] = silu_of_half(dot(w2_big[...], h1_ref[512:1280, :])).astype(BF)


def low_kernel(
    members, channels, per,
    got_ref, spread_ref, w1_ref, h_ref, w2_ref, a_ref, w3_ref,
    h2_ref, carry_ref, y_ref, h1_ref,
):
    below = is_row(lax.axis_size("row") - 1)
    y = place_halo(got_ref[...], spread_ref, y_ref, members * channels * DOWN, per)
    cols = y_ref.shape[1]
    fresh = dot(w1_ref[...], y)
    for m in range(members):
        lanes = slice(m * cols, (m + 1) * cols)
        put_hidden(h1_ref, 0, lanes, silu_of_half((fresh[m * 128 : m * 128 + 128] + h_ref[:, lanes]) * below))
    h2 = silu_of_half(dot(w2_ref[:, 512:768], h1_ref[...]) + a_ref[...]).astype(BF)
    h2_ref[...] = h2
    v = dot(w3_ref[32:64, 128:256], h2)
    for m in range(members):
        lanes = slice(m * cols, (m + 1) * cols)
        carry_ref[m * 16 : m * 16 + 16, :] = (v[0:16, lanes] + shift_right(v[16:32, lanes])).astype(BF)


def middle_kernel(
    members, half,
    h1_ref, h2_mid, h2_low, w2_ref, w3_ref, v_ref, mix_ref,
    a_first, a_second, mixed_ref, h2_ref,
):
    wide = h1_ref.shape[1]
    cols = wide // members
    a_first[...] = dot(w2_ref[:, 512:768], h1_ref[0:256, :])
    a_second[...] = dot(w2_ref[:, 256:768], h1_ref[0:512, :])
    pairs = range(4, half, 2)
    for n, a in enumerate(pairs):
        lanes = slice(n * wide, (n + 1) * wide)
        for o in (a, a + 1):
            at = slice((o - a) * 128, (o - a) * 128 + 128)
            if o == half - 1:
                h2_ref[at, lanes] = h2_low[...]
            elif o == 4:
                h2_ref[at, lanes] = h2_mid[...]
            else:
                h2_ref[at, lanes] = silu_of_half(
                    dot(w2_ref[...], h1_ref[(o - 2) * 256 : (o + 1) * 256, :])
                ).astype(BF)
    v = dot(w3_ref[...], h2_ref[...])
    carry = v_ref[...]
    for n in range(len(pairs)):
        w = v[0:32, n * wide : (n + 1) * wide] + carry
        carry = v[32:64, n * wide : (n + 1) * wide]
        parts = [bottleneck(w[:, m * cols : (m + 1) * cols]) for m in range(members)]
        put_line(mixed_ref, n * 32, dot(mix_ref[...], jnp.concatenate(parts, axis=0)))


def top_kernel(
    members, channels, per,
    got_ref, spread_ref, w1_ref, h_ref, w2_ref, a_first, a_second, w3_ref, v_ref, mix_ref,
    pre_ref, second_ref, y_ref, h1_ref, h2_ref,
):
    source = (got_ref[...].astype(F32) * is_row(0)).astype(BF)
    y = place_halo(source, spread_ref, y_ref, members * channels * UP, per)
    cols = y_ref.shape[1]
    fresh = dot(w1_ref[...], y)
    for m in range(members):
        lanes = slice(m * cols, (m + 1) * cols)
        put_hidden(h1_ref, 0, lanes, silu_of_half(fresh[m * 256 : m * 256 + 128]))
        put_hidden(h1_ref, 1, lanes, silu_of_half(fresh[m * 256 + 128 : m * 256 + 256] + h_ref[:, lanes]))
    h2_ref[0:128, :] = silu_of_half(dot(w2_ref[:, 0:512], h1_ref[...]) + a_first[...]).astype(BF)
    h2_ref[128:256, :] = silu_of_half(dot(w2_ref[:, 0:256], h1_ref[256:512, :]) + a_second[...]).astype(BF)
    v = dot(w3_ref[...], h2_ref[...])
    second = []
    for m in range(members):
        lanes = slice(m * cols, (m + 1) * cols)
        pre_ref[m] = v[0:16, lanes] + shift_right(v[16:32, lanes])
        second.append(bottleneck(v[32:64, lanes] + v_ref[:, lanes]))
    put_line(second_ref, 0, dot(mix_ref[...], jnp.concatenate(second, axis=0)))


def chunk_kernel(nb, pre_ref, carry_ref, mix_ref, second_ref, tail_ref, keep_ref, send_ref, head_ref):
    members = pre_ref.shape[0]
    carry = carry_ref[...].astype(F32) * is_row(0)
    first = [
        silu_of_half(pre_ref[m] + carry[m * 16 : m * 16 + 16]).astype(BF) for m in range(members)
    ]
    put_line(head_ref, 0, dot(mix_ref[...], jnp.concatenate(first, axis=0)))

    me = lax.axis_index("mem")
    slots = lax.axis_size("mem") // 2
    tall = 64 + tail_ref.shape[0]

    def tile_at(base):
        at = pl.ds(pl.multiple_of(base, 128), 128)
        return jnp.concatenate([head_ref[:, at], second_ref[:, at], tail_ref[:, at]], axis=0)

    def lanes_from(lane):
        v = tile_at(lane // 128 * 128)
        return v if nb % 128 == 0 else pltpu.roll(v, (128 - lane % 128) % 128, 1)

    lane_at = lax.broadcasted_iota(jnp.int32, (tall, 128), 1)
    edges = jnp.zeros((tall, 128), F32)
    for side, ref in enumerate((keep_ref, send_ref)):
        for k in range(slots):
            start = 128 + (me ^ (2 * k + side)) * nb
            ref[k, 0:tall, :] = lanes_from(start).astype(BF)
            if nb % 128 == 0:
                left = tile_at(start - 128)[:, 127:128]
            else:
                left = lanes_from(start - 1)[:, 0:1]
            right = lanes_from(start + nb)[:, 0:1]
            at = 2 * (side * slots + k)
            edges = jnp.where(lane_at == at, left, edges)
            edges = jnp.where(lane_at == at + 1, right, edges)
    turned = edges.T
    for side, ref in enumerate((keep_ref, send_ref)):
        for k in range(slots):
            at = 2 * (side * slots + k)
            ref[k, tall : tall + EDGES, :] = jnp.concatenate(
                [turned[at : at + 2], jnp.zeros((EDGES - 2, 128), F32)], axis=0
            ).astype(BF)


def pair_kernel(keep_ref, got_ref, own_ref, *out_refs):
    own_ref[...] = keep_ref[0].astype(F32) + got_ref[0].astype(F32)
    for k, ref in enumerate(out_refs):
        ref[...] = (keep_ref[k + 1].astype(F32) + got_ref[k + 1].astype(F32)).astype(BF)


def put_latent(ref, at, line):
    ext = line.shape[1]
    ref[at, 0:32, :] = pltpu.roll(line, 1, 1).astype(BF)
    ref[at, 32:64, :] = line.astype(BF)
    ref[at, 64:96, :] = pltpu.roll(line, ext - 1, 1).astype(BF)


def latent_kernel(nb, quarter, own_ref, *refs):
    line_ref, first_ref, second_ref = refs[-3:]
    total = own_ref[...]
    for ref in refs[:-3]:
        total = total + ref[...].astype(F32)
    latent = silu_of_half(0.5 * total)
    tall = quarter * 32
    turned = jnp.concatenate([latent[tall : tall + EDGES], jnp.zeros((128 - EDGES, 128), F32)], axis=0).T
    ext = line_ref.shape[1]
    lines = []
    for r in range(quarter):
        rows = slice(r * 32, (r + 1) * 32)
        line = [latent[rows, 0:nb], turned[rows, 1:2], jnp.zeros((32, ext - nb - 2), F32), turned[rows, 0:1]]
        lines.append(jnp.concatenate(line, axis=1))
        line_ref[rows, :] = lines[-1].astype(BF)
    first_ref[...] = lines[-1].astype(BF)
    second_ref[...] = lines[0].astype(BF)


def upsample_row(w1, l_ref, a, keep_even, keep_odd, rows, u_ref, wanted, keeps):
    wide = l_ref.shape[2]
    nb = u_ref.shape[1]
    v = silu_of_half(dot(w1, l_ref[a + 1 : a + 4].reshape(288, wide)))
    for pr in range(2):
        row = 2 * a + pr
        if row not in wanted:
            continue
        even = v[pr * 64 : pr * 64 + 32] * keep_even
        odd = v[pr * 64 + 32 : pr * 64 + 64] * keep_odd
        if row in keeps:
            even, odd = even * keeps[row], odd * keeps[row]
        at = (row + 1) * 128
        u_ref[at : at + 32, :] = pltpu.roll(odd, 1, 1)[:, 0:nb].astype(BF)
        u_ref[at + 32 : at + 64, :] = even[:, 0:nb].astype(BF)
        u_ref[at + 64 : at + 96, :] = odd[:, 0:nb].astype(BF)
        u_ref[at + 96 : at + 128, :] = pltpu.roll(even, wide - 1, 1)[:, 0:nb].astype(BF)


def column_keeps(nb, wide):
    mem_at, mem_last = lax.axis_index("mem"), lax.axis_size("mem") - 1
    lane = lax.broadcasted_iota(jnp.int32, (32, wide), 1)
    keep_odd = jnp.where((lane == wide - 1) & (mem_at == 0), 0.0, 1.0).astype(F32)
    keep_even = jnp.where((lane == nb) & (mem_at == mem_last), 0.0, 1.0).astype(F32)
    return keep_even, keep_odd


def field_rows(w2, u_ref, g_ref, which):
    nb = u_ref.shape[1]
    for n, a in enumerate(which):
        v = dot(w2, u_ref[a * 128 : (a + 3) * 128, :]).astype(BF)
        for pr in range(2):
            for ph in range(4):
                g_ref[(2 * n + pr) * 16 : (2 * n + pr + 1) * 16, ph * nb : (ph + 1) * nb] = v[
                    (pr * 4 + ph) * 16 : (pr * 4 + ph + 1) * 16
                ]


def level_first(rows, which):
    count = 32 * len(which)
    to = lax.broadcasted_iota(jnp.int32, (16 * rows, count), 0)
    frm = lax.broadcasted_iota(jnp.int32, (16 * rows, count), 1)
    level, row = to // rows, lax.rem(to, rows)
    hit = jnp.zeros(to.shape, jnp.bool_)
    for n, a in enumerate(which):
        for pr in range(2):
            hit = hit | ((row == 2 * a + pr) & (frm == (2 * n + pr) * 16 + level))
    return jnp.where(hit, 1.0, 0.0).astype(BF)


def split_rows(rows):
    inside = [a for a in range(2, 2 * rows - 2)]
    return inside, [a for a in range(2 * rows) if a not in inside]


def by_phase(v):
    return jnp.concatenate(
        [v[(pr * 4 + ph) * 16 : (pr * 4 + ph + 1) * 16] for ph in range(4) for pr in range(2)], axis=0
    )


def merge_phases(a, b):
    return jnp.concatenate([v[ph * 32 : ph * 32 + 32] for ph in range(4) for v in (a, b)], axis=0)


def decoder_inner(
    nb, line_ref, d1_ref, d2_ref,
    w_edge, w_field, up_part, field_part, join_ref, turn_ref, part_ref, wd1, wd2, l_ref, u_ref, g_ref,
):
    wd1[...] = jnp.zeros_like(wd1)
    wd2[...] = jnp.zeros_like(wd2)
    for pr, rr, tr in TRANSPOSED:
        for pc, cc, tc in TRANSPOSED:
            wd1[(pr * 2 + pc) * 32 : (pr * 2 + pc + 1) * 32, (rr * 3 + cc) * 32 : (rr * 3 + cc + 1) * 32] = (
                0.5 * d1_ref[tr * 4 + tc].astype(F32)
            ).astype(BF)
            for q in range(2):
                at = pr * 4 + 2 * q + pc
                to = rr * 4 + q + cc
                wd2[at * 16 : (at + 1) * 16, to * 32 : (to + 1) * 32] = d2_ref[tr * 4 + tc]
    rows, wide = line_ref.shape[0] // 32, line_ref.shape[1]
    frm = lax.broadcasted_iota(jnp.int32, join_ref.shape, 0)
    to = lax.broadcasted_iota(jnp.int32, join_ref.shape, 1)
    place = frm // nb
    join_ref[...] = jnp.where(to == 4 * (frm - nb * place) + place, 1.0, 0.0).astype(BF)
    inside, outside = split_rows(rows)
    turn_ref[...] = level_first(4 * rows, outside)

    l_ref[0] = jnp.zeros_like(l_ref[0])
    l_ref[1] = jnp.zeros_like(l_ref[0])
    for r in range(rows):
        put_latent(l_ref, r + 2, line_ref[r * 32 : r * 32 + 32, :].astype(F32))
    l_ref[rows + 2] = jnp.zeros_like(l_ref[0])
    u_ref[...] = jnp.zeros_like(u_ref)
    keep_even, keep_odd = column_keeps(nb, wide)
    for a in range(rows):
        upsample_row(wd1[...], l_ref, a, keep_even, keep_odd, rows, u_ref, range(1, 2 * rows - 1), {})
    field_rows(wd2[...], u_ref, g_ref, inside)
    g = dot(level_first(4 * rows, inside), g_ref[...]).astype(BF)
    part_ref[...] = dot(g, join_ref[...])

    w_edge[0, 0:64, :] = wd1[64:128, 96:192]
    w_edge[0, 64:128, :] = wd1[0:64, 0:96]
    w_edge[1, 0:64, :] = wd1[64:128, 192:288]
    w_edge[1, 64:128, :] = wd1[0:64, 96:192]
    up_part[0] = dot(w_edge[1], l_ref[2])
    up_part[1] = dot(w_edge[0], l_ref[rows + 1])

    def known(taps, first, count):
        return by_phase(dot(wd2[:, taps : taps + 128 * count], u_ref[(first + 1) * 128 : (first + 1 + count) * 128, :]))

    last = 2 * rows - 1
    field_part[0] = merge_phases(known(256, 1, 1), known(128, 1, 2))
    field_part[1] = merge_phases(known(0, last - 2, 2), known(0, last - 1, 1))
    none = jnp.zeros((128, 128), BF)
    w = [by_phase(wd2[:, rr * 128 : rr * 128 + 128]) for rr in range(3)]
    w_field[0] = merge_phases(jnp.concatenate([w[0], w[1]], axis=1), jnp.concatenate([none, w[0]], axis=1))
    w_field[1] = merge_phases(jnp.concatenate([w[2], none], axis=1), jnp.concatenate([w[1], w[2]], axis=1))


def decoder_kernel(
    nb, first_ref, second_ref, w_edge, w_field, up_part, field_part, join_ref, turn_ref, part_ref,
    out_ref, l_ref, u_ref, g_ref,
):
    odd_row = lax.rem(lax.axis_index("row"), 2) == 1
    keeps = is_row(0), is_row(lax.axis_size("row") - 1)
    wide = l_ref.shape[2]
    first, second = first_ref[...].astype(F32), second_ref[...].astype(F32)
    put_latent(l_ref, 0, first * keeps[0])
    put_latent(l_ref, 1, second * keeps[1])
    keep_even, keep_odd = column_keeps(nb, wide)
    for side in range(2):
        v = silu_of_half(dot(w_edge[side], l_ref[side]) + up_part[side])
        for line in range(2):
            even = v[line * 64 : line * 64 + 32] * keep_even
            odd = v[line * 64 + 32 : line * 64 + 64] * keep_odd
            if line == side:
                even, odd = even * keeps[side], odd * keeps[side]
            at = line * 128
            u_ref[side, at : at + 32, :] = pltpu.roll(odd, 1, 1)[:, 0:nb].astype(BF)
            u_ref[side, at + 32 : at + 64, :] = even[:, 0:nb].astype(BF)
            u_ref[side, at + 64 : at + 96, :] = odd[:, 0:nb].astype(BF)
            u_ref[side, at + 96 : at + 128, :] = pltpu.roll(even, wide - 1, 1)[:, 0:nb].astype(BF)
        v = (dot(w_field[side], u_ref[side]) + field_part[side]).astype(BF)
        for ph in range(4):
            g_ref[side * 64 : side * 64 + 64, ph * nb : (ph + 1) * nb] = v[ph * 64 : ph * 64 + 64]
    g = dot(g_ref[...], join_ref[...]).astype(BF)
    out_ref[...] = (dot(turn_ref[...], g) + part_ref[...]).astype(BF).reshape(out_ref.shape)


def shifted(value, by):
    peers = lax.axis_size("row")
    return lax.ppermute(value, "row", [(i, (i + by) % peers) for i in range(peers)])


def swapped(value, by):
    return lax.ppermute(value, "mem", [(i, i ^ by) for i in range(lax.axis_size("mem"))])


VMEM = pl.BlockSpec(memory_space=pltpu.VMEM)


def call(kernel, outs, scratch, *operands, mb=8, us=1):
    return pl.pallas_call(
        kernel,
        out_shape=[jax.ShapeDtypeStruct(*o) for o in outs],
        in_specs=[VMEM] * len(operands),
        out_specs=[VMEM] * len(outs),
        scratch_shapes=[pltpu.VMEM(*s) for s in scratch],
        compiler_params=pltpu.CompilerParams(vmem_limit_bytes=mb * 2**20),
        cost_estimate=pl.CostEstimate(flops=us * 10**9, bytes_accessed=us * 3 * 10**6, transcendentals=0),
    )(*operands)


def per_device(members, enc_first, enc_second, enc_third, mix_weight, dec_first, dec_second):
    count, channels, rows, wide = members.shape
    half, quarter = rows // 2, rows // 4
    cols = wide // 4
    peers, lines = lax.axis_size("mem"), lax.axis_size("row")
    nb = cols // peers
    lanes = 512
    chunks = wide // lanes
    x = members.reshape(count * channels * rows, wide)
    nd, nu = count * channels * UP, count * channels * DOWN
    per = padded(nd, 8), padded(nu, 8)
    total = padded(5 * per[0], 16), padded(5 * per[1], 16)
    pack = functools.partial(pack_kernel, count, channels, rows)
    sizes = [(nd * chunks, lanes), (nu * chunks, lanes)]
    spreads, own, above, below = call(
        functools.partial(prepare_kernel, count, channels, per),
        [
            ((2, 256, 256), BF),
            ((5, 2, 48, 5 * channels * 8), BF),
            ((count, 2, 2, 48, total[0]), BF),
            ((count, 2, 48, total[1]), BF),
        ],
        [],
        us=20,
    )
    down, up = call(pack, [(s, BF) for s in sizes], [(s, F32) for s in sizes], x, below, mb=16, us=20)
    up = shifted(up, -1)
    down = shifted(down, 1)

    w1 = enc_first.transpose(1, 2, 3, 0)
    w2 = enc_second.transpose(2, 3, 0, 1).reshape(9, 64, 64)
    w3 = enc_third.transpose(2, 3, 0, 1).reshape(9, 16, 64)
    wide_cols = count * cols
    row_f32 = ((128, wide_cols), F32)
    third_f32 = ((32, wide_cols), F32)
    (
        h1, h_first, h_last, a_last, v_second, v_third, h2_mid,
        w2_big, w3_big, w1_down, w1_up, mix,
    ) = call(
        functools.partial(inner_kernel, count, channels, rows),
        [((256 * (half - 1), wide_cols), BF)]
        + [row_f32] * 3
        + [third_f32] * 2
        + [
            ((128, wide_cols), BF),
            ((128, 768), BF),
            ((64, 256), BF),
            ((count * 256, total[0]), BF),
            ((count * 128, total[1]), BF),
            ((32, count * CH_BOT), BF),
        ],
        [
            ((48, 64), F32),
            ((640, 5 * channels * 8), BF),
            ((count, rows // 8, 5 * channels * 8, cols), F32),
            ((rows // 8, 640, cols), F32),
            ((256, wide_cols), BF),
        ],
        x, w1, w2, w3, mix_weight, spreads, own, above, below, mb=24,
    )
    h2_low, carry = call(
        functools.partial(low_kernel, count, channels, per[1]),
        [((128, wide_cols), BF), ((count * CH_BOT, cols), BF)],
        [((total[1], cols), F32), ((256, wide_cols), BF)],
        up, spreads, w1_up, h_last, w2_big, a_last, w3_big, mb=12,
    )
    carry = shifted(carry, 1)
    a_first, a_second, mid = call(
        functools.partial(middle_kernel, count, half),
        [row_f32, row_f32, ((quarter * 32 - 64, cols + 256), F32)],
        [((256, (half // 2 - 2) * wide_cols), BF)],
        h1, h2_mid, h2_low, w2_big, w3_big, v_third, mix, mb=12,
    )
    pre, second = call(
        functools.partial(top_kernel, count, channels, per[0]),
        [((count, CH_BOT, cols), F32), ((32, cols + 256), F32)],
        [((total[0], cols), F32), ((512, wide_cols), BF), ((256, wide_cols), BF)],
        down, spreads, w1_down, h_first, w2_big, a_first, a_second, w3_big, v_second, mix, mb=12,
    )
    slots = peers // 2
    chunk = (quarter * 32 + EDGES, 128)
    keep, send = call(
        functools.partial(chunk_kernel, nb),
        [((slots,) + chunk, BF)] * 2,
        [((32, cols + 256), F32)],
        pre, carry, mix, second, mid,
    )
    got = swapped(send, 1)
    mine, *others = call(pair_kernel, [(chunk, F32)] + [(chunk, BF)] * (slots - 1), [], keep, got)
    order = sorted(range(slots - 1), key=lambda k: (k == 0, k))
    moved = {k: swapped(others[k], 2 * (k + 1)) for k in order}
    ext = padded(nb + 2, 128)
    latent, first, second = call(
        functools.partial(latent_kernel, nb, quarter),
        [((quarter * 32, ext), BF), ((32, ext), BF), ((32, ext), BF)],
        [],
        mine, *[moved[k] for k in range(slots - 1)],
    )
    first = shifted(first, 1)
    second = shifted(second, -1)

    d1, d2, _ = lax.optimization_barrier((dec_first, dec_second, others[0]))
    d1 = d1.transpose(2, 3, 0, 1).reshape(16, 32, 32)
    d2 = d2.transpose(2, 3, 0, 1).reshape(16, 16, 32)
    inside, outside = split_rows(quarter)
    edge_parts = call(
        functools.partial(decoder_inner, nb),
        [
            ((2, 128, 96), BF),
            ((2, 256, 256), BF),
            ((2, 128, ext), F32),
            ((2, 256, nb), F32),
            ((4 * nb, 4 * nb), BF),
            ((16 * rows, 32 * len(outside)), BF),
            ((16 * rows, 4 * nb), F32),
        ],
        [
            ((128, 288), BF),
            ((128, 384), BF),
            ((quarter + 3, 96, ext), BF),
            ((128 * (half + 2), nb), BF),
            ((32 * len(inside), 4 * nb), BF),
        ],
        latent, d1, d2,
    )
    (out,) = call(
        functools.partial(decoder_kernel, nb),
        [((16, rows, 4 * nb), BF)],
        [((2, 96, ext), BF), ((2, 256, nb), BF), ((128, 4 * nb), BF)],
        first, second, *edge_parts,
    )
    return out


def solution(mesh):
    placed = (P("mem", None, "row", None), P(), P(), P(), P(), P(), P())
    return jax.shard_map(
        per_device, mesh=mesh, in_specs=placed, out_specs=P(None, "row", "mem"), check_vma=False
    )
```

```python
import functools

import jax
import jax.numpy as jnp
import numpy as np
from jax import lax
from jax.experimental import pallas as pl
from jax.experimental.pallas import tpu as pltpu
from jax.sharding import PartitionSpec as P

BF = jnp.bfloat16
F32 = jnp.float32
CH_BOT = 16
EDGES = 8
UP = 3
DOWN = 2
TRANSPOSED = [(p, i, 2 * i - p) for p in range(2) for i in range(3) if 0 <= 2 * i - p < 4]


def dot(a, b):
    return lax.dot_general(a, b, (((1,), (0,)), ((), ())), preferred_element_type=F32)


def dot_t(a, b):
    return lax.dot_general(a, b, (((0,), (0,)), ((), ())), preferred_element_type=F32)


def silu_of_half(y):
    return y + y * jnp.tanh(y)


def padded(n, to):
    return -(-n // to) * to


def spread(step, tile):
    one = np.zeros((step * tile, step * tile), np.float32)
    for q in range(step):
        for c in range(tile):
            one[step * c + q, q * tile + c] = 1
    return one


def shift_right(v):
    return jnp.concatenate([jnp.zeros_like(v[:, :1]), v[:, :-1]], axis=1)


def shift_left(v):
    return jnp.concatenate([v[:, 1:], jnp.zeros_like(v[:, :1])], axis=1)


def is_row(at):
    return jnp.where(lax.axis_index("row") == at, 0.0, 1.0).astype(F32)


def put_hidden(ref, at, lanes, value):
    v = value.astype(BF)
    even, odd = v[0:64], v[64:128]
    ref[at * 256 + 64 : at * 256 + 128, lanes] = even
    ref[at * 256 + 128 : at * 256 + 192, lanes] = odd
    ref[at * 256 : at * 256 + 64, lanes] = shift_right(odd)
    ref[at * 256 + 192 : at * 256 + 256, lanes] = shift_left(even)


def put_line(ref, at, line):
    rows, cols = slice(at, at + 32), line.shape[1]
    ref[rows, 0:128] = jnp.zeros((32, 128), F32)
    ref[rows, 128 : 128 + cols] = line
    ref[rows, 128 + cols : 256 + cols] = jnp.zeros((32, 128), F32)


def bottleneck(w):
    return silu_of_half(w[0:16] + shift_right(w[16:32])).astype(BF)


def apart(block, even_ref, odd_ref):
    first = dot(block[:, 0:256], even_ref)
    second = dot(block[:, 256:512], odd_ref)
    low = lax.broadcasted_iota(jnp.int32, (block.shape[0], 128), 1) < 64
    out = []
    for half in range(2):
        e, o = first[:, half * 128 : half * 128 + 128], second[:, half * 128 : half * 128 + 128]
        out.append(jnp.where(low, e, o))
        out.append(pltpu.roll(jnp.where(low, o, e), 64, 1))
    return out


def place_halo(source, spread_ref, y_ref, count, per):
    cols = y_ref.shape[1]
    if count % 8:
        for q in range(5):
            y_ref[q * per + count // 8 * 8 : (q + 1) * per, :] = jnp.zeros((8, cols), F32)
    if 5 * per < y_ref.shape[0]:
        y_ref[5 * per :, :] = jnp.zeros((y_ref.shape[0] - 5 * per, cols), F32)
    for q, z in enumerate(apart(source, spread_ref[0], spread_ref[1])):
        for t in range(cols // 128):
            y_ref[(q + 1) * per : (q + 1) * per + count, t * 128 : (t + 1) * 128] = z[t * count : (t + 1) * count]
    y_ref[0:per, :] = shift_right(y_ref[4 * per : 5 * per, :])
    return y_ref[...].astype(BF)


def prepare_kernel(members, channels, per, spread_ref, own_ref, above_ref, below_ref):
    row_of = lax.broadcasted_iota(jnp.int32, (256, 256), 0)
    lane_of = lax.broadcasted_iota(jnp.int32, (256, 256), 1)
    place = lane_of // 64
    for odd in range(2):
        spread_ref[odd] = jnp.where(row_of == 4 * (lane_of - 64 * place) + (place ^ odd), 1.0, 0.0).astype(BF)

    def tap_of(lanes):
        tap = lax.broadcasted_iota(jnp.int32, (48, lanes), 0)
        c = sum(((tap >= 9 * k).astype(jnp.int32) for k in range(1, channels)), jnp.zeros_like(tap))
        rest = tap - 9 * c
        dr = (rest >= 3).astype(jnp.int32) + (rest >= 6).astype(jnp.int32)
        return c, dr, rest - 3 * dr, lax.broadcasted_iota(jnp.int32, (48, lanes), 1)

    def one_hot(hit):
        return jnp.where(hit, 1.0, 0.0).astype(BF)

    c, dr, dc, lane = tap_of(own_ref.shape[3])
    for j in range(5):
        row = 2 * j + dr - 1
        for pc in range(2):
            at = ((2 * pc + dc) * channels + c) * 8 + row
            own_ref[j, pc] = one_hot((lane == at) & (row >= 0) & (row < 8))
    c, dr, dc, lane = tap_of(above_ref.shape[4])
    for m in range(members):
        for kind in range(2):
            slot = dr + 2 * kind
            for pc in range(2):
                at = (2 * pc + dc) * per[0] + (m * channels + c) * UP + slot
                above_ref[m, kind, pc] = one_hot((lane == at) & (slot < UP))
    c, dr, dc, lane = tap_of(below_ref.shape[3])
    for m in range(members):
        for pc in range(2):
            at = (2 * pc + dc) * per[1] + (m * channels + c) * DOWN + dr - 1
            below_ref[m, pc] = one_hot((lane == at) & (dr >= 1))


def pack_kernel(members, channels, rows, x_ref, _, down_ref, up_ref, d_scr, u_scr):
    wide = x_ref.shape[1]
    lanes = down_ref.shape[1]
    nd, nu = members * channels * UP, members * channels * DOWN
    for t in range(wide // lanes):
        for g in range(members * channels):
            block = x_ref[g * rows : (g + 1) * rows, t * lanes : (t + 1) * lanes].astype(F32)
            d_scr[t * nd + g * UP : t * nd + (g + 1) * UP, :] = block[rows - UP : rows]
            u_scr[t * nu + g * DOWN : t * nu + (g + 1) * DOWN, :] = block[0:DOWN]
    down_ref[...] = d_scr[...].astype(BF)
    up_ref[...] = u_scr[...].astype(BF)


def inner_kernel(
    members, channels, rows,
    x_ref, w1_ref, w2_ref, w3_ref, mix_ref, spread_ref, own_ref, above_ref, below_ref,
    h1_ref, h_first, h_last, a_last, a_first, a_second, v_second, v_third, h2_mid,
    w2_big, w3_big, w1_down, w1_up, mix_own,
    w1_flat, w1_own, y_ref, out1_ref, h2_ref,
):
    half, groups = rows // 2, rows // 8
    wide = x_ref.shape[1]
    cols = wide // 4

    w1_flat[...] = jnp.zeros_like(w1_flat)
    for c in range(channels):
        for dr in range(3):
            at = (c * 3 + dr) * 3
            w1_flat[at : at + 3, :] = 0.5 * w1_ref[c, dr].astype(F32)
    w1 = w1_flat[...].astype(BF)
    for pc in range(2):
        for j in range(5):
            at = j * 128 + pc * 64
            w1_own[at : at + 64, :] = dot_t(w1, own_ref[j, pc]).astype(BF)
        for m in range(members):
            for kind in range(2):
                at = m * 256 + kind * 128 + pc * 64
                w1_down[at : at + 64, :] = dot_t(w1, above_ref[m, kind, pc]).astype(BF)
            at = m * 128 + pc * 64
            w1_up[at : at + 64, :] = dot_t(w1, below_ref[m, pc]).astype(BF)
    w2_big[...] = jnp.zeros_like(w2_big)
    for ocol in range(2):
        for dr in range(3):
            for dc in range(3):
                at = dr * 256 + (ocol + dc) * 64
                w2_big[ocol * 64 : ocol * 64 + 64, at : at + 64] = (0.5 * w2_ref[dr * 3 + dc].astype(F32)).astype(BF)
    w3_big[...] = jnp.zeros_like(w3_big)
    for dr, to, base in ((1, 0, 0), (2, 0, 128), (0, 2, 128)):
        for dc, moved, at in ((1, 0, 0), (2, 0, 64), (0, 1, 64)):
            w3_big[(to + moved) * 16 : (to + moved + 1) * 16, base + at : base + at + 64] = (
                0.5 * w3_ref[dr * 3 + dc].astype(F32)
            ).astype(BF)
    own_lanes = members * CH_BOT
    total = mix_ref.shape[1]
    start = lax.axis_index("mem") * own_lanes
    mix = pltpu.roll(mix_ref[...].astype(F32), lax.rem(total - start, total), 1)[:, 0:own_lanes].astype(BF)
    mix_own[...] = mix

    for t in range(wide // 512):
        for q, z in enumerate(apart(x_ref[:, 512 * t : 512 * (t + 1)], spread_ref[0], spread_ref[1])):
            for m in range(members):
                for c in range(channels):
                    for g in range(groups):
                        at = ((q + 1) * channels + c) * 8
                        frm = (m * channels + c) * rows + g * 8
                        y_ref[m, g, at : at + 8, t * 128 : (t + 1) * 128] = z[frm : frm + 8]
    c8 = channels * 8
    for m in range(members):
        for g in range(groups):
            y_ref[m, g, 0:c8, :] = shift_right(y_ref[m, g, 4 * c8 : 5 * c8, :])

    for m in range(members):
        for g in range(groups):
            out1_ref[g] = dot(w1_own[...], y_ref[m, g].astype(BF))
        lanes = slice(m * cols, (m + 1) * cols)
        h_first[:, lanes] = out1_ref[0, 0:128]
        h_last[:, lanes] = out1_ref[groups - 1, 512:640]
        for h in range(1, half):
            g, j = h // 4, h % 4
            v = out1_ref[g, j * 128 : j * 128 + 128]
            if j == 0:
                v = v + out1_ref[g - 1, 512:640]
            put_hidden(h1_ref, h - 1, lanes, silu_of_half(v))
    a_last[...] = dot(w2_big[:, 0:512], h1_ref[(half - 3) * 256 : (half - 1) * 256, :])
    for o in range(2):
        h2_ref[o * 128 : o * 128 + 128, :] = silu_of_half(
            dot(w2_big[...], h1_ref[o * 256 : (o + 3) * 256, :])
        ).astype(BF)
    v = dot(w3_big[...], h2_ref[...])
    v_second[...] = v[0:32]
    v_third[...] = v[32:64]
    a_first[...] = dot(w2_big[:, 512:768], h1_ref[0:256, :])
    a_second[...] = dot(w2_big[:, 256:768], h1_ref[0:512, :])
    h2_mid[...] = silu_of_half(dot(w2_big[...], h1_ref[512:1280, :])).astype(BF)


def low_kernel(
    members, channels, per,
    got_ref, spread_ref, w1_ref, h_ref, w2_ref, a_ref, w3_ref,
    h2_ref, carry_ref, y_ref, h1_ref,
):
    below = is_row(lax.axis_size("row") - 1)
    y = place_halo(got_ref[...], spread_ref, y_ref, members * channels * DOWN, per)
    cols = y_ref.shape[1]
    fresh = dot(w1_ref[...], y)
    for m in range(members):
        lanes = slice(m * cols, (m + 1) * cols)
        put_hidden(h1_ref, 0, lanes, silu_of_half((fresh[m * 128 : m * 128 + 128] + h_ref[:, lanes]) * below))
    h2 = silu_of_half(dot(w2_ref[:, 512:768], h1_ref[...]) + a_ref[...]).astype(BF)
    h2_ref[...] = h2
    v = dot(w3_ref[32:64, 128:256], h2)
    for m in range(members):
        lanes = slice(m * cols, (m + 1) * cols)
        carry_ref[m * 16 : m * 16 + 16, :] = (v[0:16, lanes] + shift_right(v[16:32, lanes])).astype(BF)


def middle_kernel(
    members, half,
    h1_ref, h2_mid, h2_low, w2_ref, w3_ref, v_ref, mix_ref,
    mixed_ref, h2_ref,
):
    wide = h1_ref.shape[1]
    cols = wide // members
    pairs = range(4, half, 2)
    for n, a in enumerate(pairs):
        lanes = slice(n * wide, (n + 1) * wide)
        for o in (a, a + 1):
            at = slice((o - a) * 128, (o - a) * 128 + 128)
            if o == half - 1:
                h2_ref[at, lanes] = h2_low[...]
            elif o == 4:
                h2_ref[at, lanes] = h2_mid[...]
            else:
                h2_ref[at, lanes] = silu_of_half(
                    dot(w2_ref[...], h1_ref[(o - 2) * 256 : (o + 1) * 256, :])
                ).astype(BF)
    v = dot(w3_ref[...], h2_ref[...])
    carry = v_ref[...]
    for n in range(len(pairs)):
        w = v[0:32, n * wide : (n + 1) * wide] + carry
        carry = v[32:64, n * wide : (n + 1) * wide]
        parts = [bottleneck(w[:, m * cols : (m + 1) * cols]) for m in range(members)]
        put_line(mixed_ref, n * 32, dot(mix_ref[...], jnp.concatenate(parts, axis=0)))


def top_kernel(
    members, channels, per,
    got_ref, spread_ref, w1_ref, h_ref, w2_ref, a_first, a_second, w3_ref, v_ref, mix_ref,
    pre_ref, second_ref, y_ref, h1_ref, h2_ref,
):
    source = (got_ref[...].astype(F32) * is_row(0)).astype(BF)
    y = place_halo(source, spread_ref, y_ref, members * channels * UP, per)
    cols = y_ref.shape[1]
    fresh = dot(w1_ref[...], y)
    for m in range(members):
        lanes = slice(m * cols, (m + 1) * cols)
        put_hidden(h1_ref, 0, lanes, silu_of_half(fresh[m * 256 : m * 256 + 128]))
        put_hidden(h1_ref, 1, lanes, silu_of_half(fresh[m * 256 + 128 : m * 256 + 256] + h_ref[:, lanes]))
    h2_ref[0:128, :] = silu_of_half(dot(w2_ref[:, 0:512], h1_ref[...]) + a_first[...]).astype(BF)
    h2_ref[128:256, :] = silu_of_half(dot(w2_ref[:, 0:256], h1_ref[256:512, :]) + a_second[...]).astype(BF)
    v = dot(w3_ref[...], h2_ref[...])
    second = []
    for m in range(members):
        lanes = slice(m * cols, (m + 1) * cols)
        pre_ref[m] = v[0:16, lanes] + shift_right(v[16:32, lanes])
        second.append(bottleneck(v[32:64, lanes] + v_ref[:, lanes]))
    put_line(second_ref, 0, dot(mix_ref[...], jnp.concatenate(second, axis=0)))


def chunk_kernel(nb, pre_ref, carry_ref, mix_ref, second_ref, tail_ref, keep_ref, send_ref, head_ref):
    members = pre_ref.shape[0]
    carry = carry_ref[...].astype(F32) * is_row(0)
    first = [
        silu_of_half(pre_ref[m] + carry[m * 16 : m * 16 + 16]).astype(BF) for m in range(members)
    ]
    put_line(head_ref, 0, dot(mix_ref[...], jnp.concatenate(first, axis=0)))

    me = lax.axis_index("mem")
    slots = lax.axis_size("mem") // 2
    tall = 64 + tail_ref.shape[0]

    def tile_at(base):
        at = pl.ds(pl.multiple_of(base, 128), 128)
        return jnp.concatenate([head_ref[:, at], second_ref[:, at], tail_ref[:, at]], axis=0)

    def lanes_from(lane):
        v = tile_at(lane // 128 * 128)
        return v if nb % 128 == 0 else pltpu.roll(v, (128 - lane % 128) % 128, 1)

    lane_at = lax.broadcasted_iota(jnp.int32, (tall, 128), 1)
    edges = jnp.zeros((tall, 128), F32)
    for side, ref in enumerate((keep_ref, send_ref)):
        for k in range(slots):
            start = 128 + (me ^ (2 * k + side)) * nb
            ref[k, 0:tall, :] = lanes_from(start).astype(BF)
            if nb % 128 == 0:
                left = tile_at(start - 128)[:, 127:128]
            else:
                left = lanes_from(start - 1)[:, 0:1]
            right = lanes_from(start + nb)[:, 0:1]
            at = 2 * (side * slots + k)
            edges = jnp.where(lane_at == at, left, edges)
            edges = jnp.where(lane_at == at + 1, right, edges)
    turned = edges.T
    for side, ref in enumerate((keep_ref, send_ref)):
        for k in range(slots):
            at = 2 * (side * slots + k)
            ref[k, tall : tall + EDGES, :] = jnp.concatenate(
                [turned[at : at + 2], jnp.zeros((EDGES - 2, 128), F32)], axis=0
            ).astype(BF)


def pair_kernel(keep_ref, got_ref, own_ref, *out_refs):
    own_ref[...] = keep_ref[0].astype(F32) + got_ref[0].astype(F32)
    for k, ref in enumerate(out_refs):
        ref[...] = (keep_ref[k + 1].astype(F32) + got_ref[k + 1].astype(F32)).astype(BF)


def put_latent(ref, at, line):
    ext = line.shape[1]
    ref[at, 0:32, :] = pltpu.roll(line, 1, 1).astype(BF)
    ref[at, 32:64, :] = line.astype(BF)
    ref[at, 64:96, :] = pltpu.roll(line, ext - 1, 1).astype(BF)


def latent_kernel(nb, quarter, own_ref, *refs):
    line_ref, first_ref, second_ref = refs[-3:]
    total = own_ref[...]
    for ref in refs[:-3]:
        total = total + ref[...].astype(F32)
    latent = silu_of_half(0.5 * total)
    tall = quarter * 32
    turned = jnp.concatenate([latent[tall : tall + EDGES], jnp.zeros((128 - EDGES, 128), F32)], axis=0).T
    ext = line_ref.shape[1]
    lines = []
    for r in range(quarter):
        rows = slice(r * 32, (r + 1) * 32)
        line = [latent[rows, 0:nb], turned[rows, 1:2], jnp.zeros((32, ext - nb - 2), F32), turned[rows, 0:1]]
        lines.append(jnp.concatenate(line, axis=1))
        line_ref[rows, :] = lines[-1].astype(BF)
    first_ref[...] = lines[-1].astype(BF)
    second_ref[...] = lines[0].astype(BF)


def upsample_row(w1, l_ref, a, keep_even, keep_odd, rows, u_ref, wanted, keeps):
    wide = l_ref.shape[2]
    nb = u_ref.shape[1]
    v = silu_of_half(dot(w1, l_ref[a + 1 : a + 4].reshape(288, wide)))
    for pr in range(2):
        row = 2 * a + pr
        if row not in wanted:
            continue
        even = v[pr * 64 : pr * 64 + 32] * keep_even
        odd = v[pr * 64 + 32 : pr * 64 + 64] * keep_odd
        if row in keeps:
            even, odd = even * keeps[row], odd * keeps[row]
        at = (row + 1) * 128
        u_ref[at : at + 32, :] = pltpu.roll(odd, 1, 1)[:, 0:nb].astype(BF)
        u_ref[at + 32 : at + 64, :] = even[:, 0:nb].astype(BF)
        u_ref[at + 64 : at + 96, :] = odd[:, 0:nb].astype(BF)
        u_ref[at + 96 : at + 128, :] = pltpu.roll(even, wide - 1, 1)[:, 0:nb].astype(BF)


def column_keeps(nb, wide):
    mem_at, mem_last = lax.axis_index("mem"), lax.axis_size("mem") - 1
    lane = lax.broadcasted_iota(jnp.int32, (32, wide), 1)
    keep_odd = jnp.where((lane == wide - 1) & (mem_at == 0), 0.0, 1.0).astype(F32)
    keep_even = jnp.where((lane == nb) & (mem_at == mem_last), 0.0, 1.0).astype(F32)
    return keep_even, keep_odd


def field_rows(w2, u_ref, g_ref, which):
    nb = u_ref.shape[1]
    for n, a in enumerate(which):
        v = dot(w2, u_ref[a * 128 : (a + 3) * 128, :]).astype(BF)
        for pr in range(2):
            for ph in range(4):
                g_ref[(2 * n + pr) * 16 : (2 * n + pr + 1) * 16, ph * nb : (ph + 1) * nb] = v[
                    (pr * 4 + ph) * 16 : (pr * 4 + ph + 1) * 16
                ]


def level_first(rows, which):
    count = 32 * len(which)
    to = lax.broadcasted_iota(jnp.int32, (16 * rows, count), 0)
    frm = lax.broadcasted_iota(jnp.int32, (16 * rows, count), 1)
    level, row = to // rows, lax.rem(to, rows)
    hit = jnp.zeros(to.shape, jnp.bool_)
    for n, a in enumerate(which):
        for pr in range(2):
            hit = hit | ((row == 2 * a + pr) & (frm == (2 * n + pr) * 16 + level))
    return jnp.where(hit, 1.0, 0.0).astype(BF)


def split_rows(rows):
    inside = [a for a in range(2, 2 * rows - 2)]
    return inside, [a for a in range(2 * rows) if a not in inside]


def by_phase(v):
    return jnp.concatenate(
        [v[(pr * 4 + ph) * 16 : (pr * 4 + ph + 1) * 16] for ph in range(4) for pr in range(2)], axis=0
    )


def merge_phases(a, b):
    return jnp.concatenate([v[ph * 32 : ph * 32 + 32] for ph in range(4) for v in (a, b)], axis=0)


def decoder_inner(
    nb, line_ref, d1_ref, d2_ref,
    w_edge, w_field, up_part, field_part, join_ref, turn_ref, part_ref, wd1, wd2, l_ref, u_ref, g_ref,
):
    wd1[...] = jnp.zeros_like(wd1)
    wd2[...] = jnp.zeros_like(wd2)
    for pr, rr, tr in TRANSPOSED:
        for pc, cc, tc in TRANSPOSED:
            wd1[(pr * 2 + pc) * 32 : (pr * 2 + pc + 1) * 32, (rr * 3 + cc) * 32 : (rr * 3 + cc + 1) * 32] = (
                0.5 * d1_ref[tr * 4 + tc].astype(F32)
            ).astype(BF)
            for q in range(2):
                at = pr * 4 + 2 * q + pc
                to = rr * 4 + q + cc
                wd2[at * 16 : (at + 1) * 16, to * 32 : (to + 1) * 32] = d2_ref[tr * 4 + tc]
    rows, wide = line_ref.shape[0] // 32, line_ref.shape[1]
    frm = lax.broadcasted_iota(jnp.int32, join_ref.shape, 0)
    to = lax.broadcasted_iota(jnp.int32, join_ref.shape, 1)
    place = frm // nb
    join_ref[...] = jnp.where(to == 4 * (frm - nb * place) + place, 1.0, 0.0).astype(BF)
    inside, outside = split_rows(rows)
    turn_ref[...] = level_first(4 * rows, outside)

    l_ref[0] = jnp.zeros_like(l_ref[0])
    l_ref[1] = jnp.zeros_like(l_ref[0])
    for r in range(rows):
        put_latent(l_ref, r + 2, line_ref[r * 32 : r * 32 + 32, :].astype(F32))
    l_ref[rows + 2] = jnp.zeros_like(l_ref[0])
    u_ref[...] = jnp.zeros_like(u_ref)
    keep_even, keep_odd = column_keeps(nb, wide)
    for a in range(rows):
        upsample_row(wd1[...], l_ref, a, keep_even, keep_odd, rows, u_ref, range(1, 2 * rows - 1), {})
    field_rows(wd2[...], u_ref, g_ref, inside)
    g = dot(level_first(4 * rows, inside), g_ref[...]).astype(BF)
    part_ref[...] = dot(g, join_ref[...])

    w_edge[0, 0:64, :] = wd1[64:128, 96:192]
    w_edge[0, 64:128, :] = wd1[0:64, 0:96]
    w_edge[1, 0:64, :] = wd1[64:128, 192:288]
    w_edge[1, 64:128, :] = wd1[0:64, 96:192]
    up_part[0] = dot(w_edge[1], l_ref[2])
    up_part[1] = dot(w_edge[0], l_ref[rows + 1])

    def known(taps, first, count):
        return by_phase(dot(wd2[:, taps : taps + 128 * count], u_ref[(first + 1) * 128 : (first + 1 + count) * 128, :]))

    last = 2 * rows - 1
    field_part[0] = merge_phases(known(256, 1, 1), known(128, 1, 2))
    field_part[1] = merge_phases(known(0, last - 2, 2), known(0, last - 1, 1))
    none = jnp.zeros((128, 128), BF)
    w = [by_phase(wd2[:, rr * 128 : rr * 128 + 128]) for rr in range(3)]
    w_field[0] = merge_phases(jnp.concatenate([w[0], w[1]], axis=1), jnp.concatenate([none, w[0]], axis=1))
    w_field[1] = merge_phases(jnp.concatenate([w[2], none], axis=1), jnp.concatenate([w[1], w[2]], axis=1))


def decoder_kernel(
    nb, first_ref, second_ref, w_edge, w_field, up_part, field_part, join_ref, turn_ref, part_ref,
    out_ref, l_ref, u_ref, g_ref,
):
    odd_row = lax.rem(lax.axis_index("row"), 2) == 1
    keeps = is_row(0), is_row(lax.axis_size("row") - 1)
    wide = l_ref.shape[2]
    first, second = first_ref[...].astype(F32), second_ref[...].astype(F32)
    put_latent(l_ref, 0, first * keeps[0])
    put_latent(l_ref, 1, second * keeps[1])
    keep_even, keep_odd = column_keeps(nb, wide)
    for side in range(2):
        v = silu_of_half(dot(w_edge[side], l_ref[side]) + up_part[side])
        for line in range(2):
            even = v[line * 64 : line * 64 + 32] * keep_even
            odd = v[line * 64 + 32 : line * 64 + 64] * keep_odd
            if line == side:
                even, odd = even * keeps[side], odd * keeps[side]
            at = line * 128
            u_ref[side, at : at + 32, :] = pltpu.roll(odd, 1, 1)[:, 0:nb].astype(BF)
            u_ref[side, at + 32 : at + 64, :] = even[:, 0:nb].astype(BF)
            u_ref[side, at + 64 : at + 96, :] = odd[:, 0:nb].astype(BF)
            u_ref[side, at + 96 : at + 128, :] = pltpu.roll(even, wide - 1, 1)[:, 0:nb].astype(BF)
        v = (dot(w_field[side], u_ref[side]) + field_part[side]).astype(BF)
        for ph in range(4):
            g_ref[side * 64 : side * 64 + 64, ph * nb : (ph + 1) * nb] = v[ph * 64 : ph * 64 + 64]
    g = dot(g_ref[...], join_ref[...]).astype(BF)
    out_ref[...] = (dot(turn_ref[...], g) + part_ref[...]).astype(BF).reshape(out_ref.shape)


def shifted(value, by):
    peers = lax.axis_size("row")
    return lax.ppermute(value, "row", [(i, (i + by) % peers) for i in range(peers)])


def swapped(value, by):
    return lax.ppermute(value, "mem", [(i, i ^ by) for i in range(lax.axis_size("mem"))])


VMEM = pl.BlockSpec(memory_space=pltpu.VMEM)


def call(kernel, outs, scratch, *operands, mb=8, us=1):
    return pl.pallas_call(
        kernel,
        out_shape=[jax.ShapeDtypeStruct(*o) for o in outs],
        in_specs=[VMEM] * len(operands),
        out_specs=[VMEM] * len(outs),
        scratch_shapes=[pltpu.VMEM(*s) for s in scratch],
        compiler_params=pltpu.CompilerParams(vmem_limit_bytes=mb * 2**20),
        cost_estimate=pl.CostEstimate(flops=us * 10**9, bytes_accessed=us * 3 * 10**6, transcendentals=0),
    )(*operands)


def per_device(members, enc_first, enc_second, enc_third, mix_weight, dec_first, dec_second):
    count, channels, rows, wide = members.shape
    half, quarter = rows // 2, rows // 4
    cols = wide // 4
    peers, lines = lax.axis_size("mem"), lax.axis_size("row")
    nb = cols // peers
    lanes = 512
    chunks = wide // lanes
    x = members.reshape(count * channels * rows, wide)
    nd, nu = count * channels * UP, count * channels * DOWN
    per = padded(nd, 8), padded(nu, 8)
    total = padded(5 * per[0], 16), padded(5 * per[1], 16)
    pack = functools.partial(pack_kernel, count, channels, rows)
    sizes = [(nd * chunks, lanes), (nu * chunks, lanes)]
    spreads, own, above, below = call(
        functools.partial(prepare_kernel, count, channels, per),
        [
            ((2, 256, 256), BF),
            ((5, 2, 48, 5 * channels * 8), BF),
            ((count, 2, 2, 48, total[0]), BF),
            ((count, 2, 48, total[1]), BF),
        ],
        [],
        us=20,
    )
    down, up = call(pack, [(s, BF) for s in sizes], [(s, F32) for s in sizes], x, below, mb=16, us=20)
    up = shifted(up, -1)
    down = shifted(down, 1)

    w1 = enc_first.transpose(1, 2, 3, 0)
    w2 = enc_second.transpose(2, 3, 0, 1).reshape(9, 64, 64)
    w3 = enc_third.transpose(2, 3, 0, 1).reshape(9, 16, 64)
    wide_cols = count * cols
    row_f32 = ((128, wide_cols), F32)
    third_f32 = ((32, wide_cols), F32)
    (
        h1, h_first, h_last, a_last, a_first, a_second, v_second, v_third, h2_mid,
        w2_big, w3_big, w1_down, w1_up, mix,
    ) = call(
        functools.partial(inner_kernel, count, channels, rows),
        [((256 * (half - 1), wide_cols), BF)]
        + [row_f32] * 5
        + [third_f32] * 2
        + [
            ((128, wide_cols), BF),
            ((128, 768), BF),
            ((64, 256), BF),
            ((count * 256, total[0]), BF),
            ((count * 128, total[1]), BF),
            ((32, count * CH_BOT), BF),
        ],
        [
            ((48, 64), F32),
            ((640, 5 * channels * 8), BF),
            ((count, rows // 8, 5 * channels * 8, cols), F32),
            ((rows // 8, 640, cols), F32),
            ((256, wide_cols), BF),
        ],
        x, w1, w2, w3, mix_weight, spreads, own, above, below, mb=24,
    )
    h2_low, carry = call(
        functools.partial(low_kernel, count, channels, per[1]),
        [((128, wide_cols), BF), ((count * CH_BOT, cols), BF)],
        [((total[1], cols), F32), ((256, wide_cols), BF)],
        up, spreads, w1_up, h_last, w2_big, a_last, w3_big, mb=12,
    )
    carry = shifted(carry, 1)
    (mid,) = call(
        functools.partial(middle_kernel, count, half),
        [((quarter * 32 - 64, cols + 256), F32)],
        [((256, (half // 2 - 2) * wide_cols), BF)],
        h1, h2_mid, h2_low, w2_big, w3_big, v_third, mix, mb=12,
    )
    pre, second = call(
        functools.partial(top_kernel, count, channels, per[0]),
        [((count, CH_BOT, cols), F32), ((32, cols + 256), F32)],
        [((total[0], cols), F32), ((512, wide_cols), BF), ((256, wide_cols), BF)],
        down, spreads, w1_down, h_first, w2_big, a_first, a_second, w3_big, v_second, mix, mb=12,
    )
    slots = peers // 2
    chunk = (quarter * 32 + EDGES, 128)
    keep, send = call(
        functools.partial(chunk_kernel, nb),
        [((slots,) + chunk, BF)] * 2,
        [((32, cols + 256), F32)],
        pre, carry, mix, second, mid,
    )
    got = swapped(send, 1)
    mine, *others = call(pair_kernel, [(chunk, F32)] + [(chunk, BF)] * (slots - 1), [], keep, got)
    order = sorted(range(slots - 1), key=lambda k: (k == 0, k))
    moved = {k: swapped(others[k], 2 * (k + 1)) for k in order}
    ext = padded(nb + 2, 128)
    latent, first, second = call(
        functools.partial(latent_kernel, nb, quarter),
        [((quarter * 32, ext), BF), ((32, ext), BF), ((32, ext), BF)],
        [],
        mine, *[moved[k] for k in range(slots - 1)],
    )
    first = shifted(first, 1)
    second = shifted(second, -1)

    d1, d2, _ = lax.optimization_barrier((dec_first, dec_second, others[0]))
    d1 = d1.transpose(2, 3, 0, 1).reshape(16, 32, 32)
    d2 = d2.transpose(2, 3, 0, 1).reshape(16, 16, 32)
    inside, outside = split_rows(quarter)
    edge_parts = call(
        functools.partial(decoder_inner, nb),
        [
            ((2, 128, 96), BF),
            ((2, 256, 256), BF),
            ((2, 128, ext), F32),
            ((2, 256, nb), F32),
            ((4 * nb, 4 * nb), BF),
            ((16 * rows, 32 * len(outside)), BF),
            ((16 * rows, 4 * nb), F32),
        ],
        [
            ((128, 288), BF),
            ((128, 384), BF),
            ((quarter + 3, 96, ext), BF),
            ((128 * (half + 2), nb), BF),
            ((32 * len(inside), 4 * nb), BF),
        ],
        latent, d1, d2,
    )
    (out,) = call(
        functools.partial(decoder_kernel, nb),
        [((16, rows, 4 * nb), BF)],
        [((2, 96, ext), BF), ((2, 256, nb), BF), ((128, 4 * nb), BF)],
        first, second, *edge_parts,
    )
    return out


def solution(mesh):
    placed = (P("mem", None, "row", None), P(), P(), P(), P(), P(), P())
    return jax.shard_map(
        per_device, mesh=mesh, in_specs=placed, out_specs=P(None, "row", "mem"), check_vma=False
    )
```

```python
import functools

import jax
import jax.numpy as jnp
import numpy as np
from jax import lax
from jax.experimental import pallas as pl
from jax.experimental.pallas import tpu as pltpu
from jax.sharding import PartitionSpec as P

BF = jnp.bfloat16
F32 = jnp.float32
CH_BOT = 16
EDGES = 8
UP = 3
DOWN = 2
TRANSPOSED = [(p, i, 2 * i - p) for p in range(2) for i in range(3) if 0 <= 2 * i - p < 4]


def dot(a, b):
    return lax.dot_general(a, b, (((1,), (0,)), ((), ())), preferred_element_type=F32)


def dot_t(a, b):
    return lax.dot_general(a, b, (((0,), (0,)), ((), ())), preferred_element_type=F32)


def silu_of_half(y):
    return y + y * jnp.tanh(y)


def padded(n, to):
    return -(-n // to) * to


def spread(step, tile):
    one = np.zeros((step * tile, step * tile), np.float32)
    for q in range(step):
        for c in range(tile):
            one[step * c + q, q * tile + c] = 1
    return one


def shift_right(v):
    return jnp.concatenate([jnp.zeros_like(v[:, :1]), v[:, :-1]], axis=1)


def shift_left(v):
    return jnp.concatenate([v[:, 1:], jnp.zeros_like(v[:, :1])], axis=1)


def is_row(at):
    return jnp.where(lax.axis_index("row") == at, 0.0, 1.0).astype(F32)


def put_hidden(ref, at, lanes, value):
    v = value.astype(BF)
    even, odd = v[0:64], v[64:128]
    ref[at * 256 + 64 : at * 256 + 128, lanes] = even
    ref[at * 256 + 128 : at * 256 + 192, lanes] = odd
    ref[at * 256 : at * 256 + 64, lanes] = shift_right(odd)
    ref[at * 256 + 192 : at * 256 + 256, lanes] = shift_left(even)


def put_line(ref, at, line):
    rows, cols = slice(at, at + 32), line.shape[1]
    ref[rows, 0:128] = jnp.zeros((32, 128), F32)
    ref[rows, 128 : 128 + cols] = line
    ref[rows, 128 + cols : 256 + cols] = jnp.zeros((32, 128), F32)


def bottleneck(w):
    return silu_of_half(w[0:16] + shift_right(w[16:32])).astype(BF)


def apart(block, even_ref, odd_ref):
    first = dot(block[:, 0:256], even_ref)
    second = dot(block[:, 256:512], odd_ref)
    low = lax.broadcasted_iota(jnp.int32, (block.shape[0], 128), 1) < 64
    out = []
    for half in range(2):
        e, o = first[:, half * 128 : half * 128 + 128], second[:, half * 128 : half * 128 + 128]
        out.append(jnp.where(low, e, o))
        out.append(pltpu.roll(jnp.where(low, o, e), 64, 1))
    return out


def place_halo(source, spread_ref, y_ref, count, per):
    cols = y_ref.shape[1]
    if count % 8:
        for q in range(5):
            y_ref[q * per + count // 8 * 8 : (q + 1) * per, :] = jnp.zeros((8, cols), F32)
    if 5 * per < y_ref.shape[0]:
        y_ref[5 * per :, :] = jnp.zeros((y_ref.shape[0] - 5 * per, cols), F32)
    for q, z in enumerate(apart(source, spread_ref[0], spread_ref[1])):
        for t in range(cols // 128):
            y_ref[(q + 1) * per : (q + 1) * per + count, t * 128 : (t + 1) * 128] = z[t * count : (t + 1) * count]
    y_ref[0:per, :] = shift_right(y_ref[4 * per : 5 * per, :])
    return y_ref[...].astype(BF)


def prepare_kernel(members, channels, per, spread_ref, own_ref, above_ref, below_ref):
    row_of = lax.broadcasted_iota(jnp.int32, (256, 256), 0)
    lane_of = lax.broadcasted_iota(jnp.int32, (256, 256), 1)
    place = lane_of // 64
    for odd in range(2):
        spread_ref[odd] = jnp.where(row_of == 4 * (lane_of - 64 * place) + (place ^ odd), 1.0, 0.0).astype(BF)

    def tap_of(lanes):
        tap = lax.broadcasted_iota(jnp.int32, (48, lanes), 0)
        c = sum(((tap >= 9 * k).astype(jnp.int32) for k in range(1, channels)), jnp.zeros_like(tap))
        rest = tap - 9 * c
        dr = (rest >= 3).astype(jnp.int32) + (rest >= 6).astype(jnp.int32)
        return c, dr, rest - 3 * dr, lax.broadcasted_iota(jnp.int32, (48, lanes), 1)

    def one_hot(hit):
        return jnp.where(hit, 1.0, 0.0).astype(BF)

    c, dr, dc, lane = tap_of(own_ref.shape[3])
    for j in range(5):
        row = 2 * j + dr - 1
        for pc in range(2):
            at = ((2 * pc + dc) * channels + c) * 8 + row
            own_ref[j, pc] = one_hot((lane == at) & (row >= 0) & (row < 8))
    c, dr, dc, lane = tap_of(above_ref.shape[4])
    for m in range(members):
        for kind in range(2):
            slot = dr + 2 * kind
            for pc in range(2):
                at = (2 * pc + dc) * per[0] + (m * channels + c) * UP + slot
                above_ref[m, kind, pc] = one_hot((lane == at) & (slot < UP))
    c, dr, dc, lane = tap_of(below_ref.shape[3])
    for m in range(members):
        for pc in range(2):
            at = (2 * pc + dc) * per[1] + (m * channels + c) * DOWN + dr - 1
            below_ref[m, pc] = one_hot((lane == at) & (dr >= 1))


def pack_kernel(members, channels, rows, x_ref, _, down_ref, up_ref, d_scr, u_scr):
    wide = x_ref.shape[1]
    lanes = down_ref.shape[1]
    nd, nu = members * channels * UP, members * channels * DOWN
    for t in range(wide // lanes):
        for g in range(members * channels):
            block = x_ref[g * rows : (g + 1) * rows, t * lanes : (t + 1) * lanes].astype(F32)
            d_scr[t * nd + g * UP : t * nd + (g + 1) * UP, :] = block[rows - UP : rows]
            u_scr[t * nu + g * DOWN : t * nu + (g + 1) * DOWN, :] = block[0:DOWN]
    down_ref[...] = d_scr[...].astype(BF)
    up_ref[...] = u_scr[...].astype(BF)


def inner_kernel(
    members, channels, rows,
    x_ref, w1_ref, w2_ref, w3_ref, mix_ref, spread_ref, own_ref, above_ref, below_ref,
    h1_ref, h_first, h_last, a_last, a_first, a_second, v_second, v_third, h2_mid,
    w2_big, w3_big, w1_down, w1_up, mix_own,
    w1_flat, w1_own, y_ref, out1_ref, h2_ref,
):
    half, groups = rows // 2, rows // 8
    wide = x_ref.shape[1]
    cols = wide // 4

    w1_flat[...] = jnp.zeros_like(w1_flat)
    for c in range(channels):
        for dr in range(3):
            at = (c * 3 + dr) * 3
            w1_flat[at : at + 3, :] = 0.5 * w1_ref[c, dr].astype(F32)
    w1 = w1_flat[...].astype(BF)
    for pc in range(2):
        for j in range(5):
            at = j * 128 + pc * 64
            w1_own[at : at + 64, :] = dot_t(w1, own_ref[j, pc]).astype(BF)
        for m in range(members):
            for kind in range(2):
                at = m * 256 + kind * 128 + pc * 64
                w1_down[at : at + 64, :] = dot_t(w1, above_ref[m, kind, pc]).astype(BF)
            at = m * 128 + pc * 64
            w1_up[at : at + 64, :] = dot_t(w1, below_ref[m, pc]).astype(BF)
    w2_big[...] = jnp.zeros_like(w2_big)
    for ocol in range(2):
        for dr in range(3):
            for dc in range(3):
                at = dr * 256 + (ocol + dc) * 64
                w2_big[ocol * 64 : ocol * 64 + 64, at : at + 64] = (0.5 * w2_ref[dr * 3 + dc].astype(F32)).astype(BF)
    w3_big[...] = jnp.zeros_like(w3_big)
    for dr, to, base in ((1, 0, 0), (2, 0, 128), (0, 2, 128)):
        for dc, moved, at in ((1, 0, 0), (2, 0, 64), (0, 1, 64)):
            w3_big[(to + moved) * 16 : (to + moved + 1) * 16, base + at : base + at + 64] = (
                0.5 * w3_ref[dr * 3 + dc].astype(F32)
            ).astype(BF)
    own_lanes = members * CH_BOT
    total = mix_ref.shape[1]
    start = lax.axis_index("mem") * own_lanes
    mix = pltpu.roll(mix_ref[...].astype(F32), lax.rem(total - start, total), 1)[:, 0:own_lanes].astype(BF)
    mix_own[...] = mix

    for t in range(wide // 512):
        for q, z in enumerate(apart(x_ref[:, 512 * t : 512 * (t + 1)], spread_ref[0], spread_ref[1])):
            for m in range(members):
                for c in range(channels):
                    for g in range(groups):
                        at = ((q + 1) * channels + c) * 8
                        frm = (m * channels + c) * rows + g * 8
                        y_ref[m, g, at : at + 8, t * 128 : (t + 1) * 128] = z[frm : frm + 8]
    c8 = channels * 8
    for m in range(members):
        for g in range(groups):
            y_ref[m, g, 0:c8, :] = shift_right(y_ref[m, g, 4 * c8 : 5 * c8, :])

    for m in range(members):
        for g in range(groups):
            out1_ref[g] = dot(w1_own[...], y_ref[m, g].astype(BF))
        lanes = slice(m * cols, (m + 1) * cols)
        h_first[:, lanes] = out1_ref[0, 0:128]
        h_last[:, lanes] = out1_ref[groups - 1, 512:640]
        for h in range(1, half):
            g, j = h // 4, h % 4
            v = out1_ref[g, j * 128 : j * 128 + 128]
            if j == 0:
                v = v + out1_ref[g - 1, 512:640]
            put_hidden(h1_ref, h - 1, lanes, silu_of_half(v))
    a_last[...] = dot(w2_big[:, 0:512], h1_ref[(half - 3) * 256 : (half - 1) * 256, :])
    for o in range(2):
        h2_ref[o * 128 : o * 128 + 128, :] = silu_of_half(
            dot(w2_big[...], h1_ref[o * 256 : (o + 3) * 256, :])
        ).astype(BF)
    v = dot(w3_big[...], h2_ref[...])
    v_second[...] = v[0:32]
    v_third[...] = v[32:64]
    a_first[...] = dot(w2_big[:, 512:768], h1_ref[0:256, :])
    a_second[...] = dot(w2_big[:, 256:768], h1_ref[0:512, :])
    h2_mid[...] = silu_of_half(dot(w2_big[...], h1_ref[512:1280, :])).astype(BF)


def low_kernel(
    members, channels, per,
    got_ref, spread_ref, w1_ref, h_ref, w2_ref, a_ref, w3_ref,
    h2_ref, carry_ref, y_ref, h1_ref,
):
    below = is_row(lax.axis_size("row") - 1)
    y = place_halo(got_ref[...], spread_ref, y_ref, members * channels * DOWN, per)
    cols = y_ref.shape[1]
    fresh = dot(w1_ref[...], y)
    for m in range(members):
        lanes = slice(m * cols, (m + 1) * cols)
        put_hidden(h1_ref, 0, lanes, silu_of_half((fresh[m * 128 : m * 128 + 128] + h_ref[:, lanes]) * below))
    h2 = silu_of_half(dot(w2_ref[:, 512:768], h1_ref[...]) + a_ref[...]).astype(BF)
    h2_ref[...] = h2
    v = dot(w3_ref[32:64, 128:256], h2)
    for m in range(members):
        lanes = slice(m * cols, (m + 1) * cols)
        carry_ref[m * 16 : m * 16 + 16, :] = (v[0:16, lanes] + shift_right(v[16:32, lanes])).astype(BF)


def middle_kernel(
    members, half,
    h1_ref, h2_mid, h2_low, w2_ref, w3_ref, v_ref, mix_ref,
    mixed_ref, h2_ref,
):
    wide = h1_ref.shape[1]
    cols = wide // members
    pairs = range(4, half, 2)
    for n, a in enumerate(pairs):
        lanes = slice(n * wide, (n + 1) * wide)
        for o in (a, a + 1):
            at = slice((o - a) * 128, (o - a) * 128 + 128)
            if o == half - 1:
                h2_ref[at, lanes] = h2_low[...]
            elif o == 4:
                h2_ref[at, lanes] = h2_mid[...]
            else:
                h2_ref[at, lanes] = silu_of_half(
                    dot(w2_ref[...], h1_ref[(o - 2) * 256 : (o + 1) * 256, :])
                ).astype(BF)
    v = dot(w3_ref[...], h2_ref[...])
    carry = v_ref[...]
    for n in range(len(pairs)):
        w = v[0:32, n * wide : (n + 1) * wide] + carry
        carry = v[32:64, n * wide : (n + 1) * wide]
        parts = [bottleneck(w[:, m * cols : (m + 1) * cols]) for m in range(members)]
        put_line(mixed_ref, n * 32, dot(mix_ref[...], jnp.concatenate(parts, axis=0)))


def top_kernel(
    members, channels, per,
    got_ref, spread_ref, w1_ref, h_ref, w2_ref, a_first, a_second, w3_ref, v_ref, mix_ref,
    pre_ref, second_ref, y_ref, h1_ref, h2_ref,
):
    source = (got_ref[...].astype(F32) * is_row(0)).astype(BF)
    y = place_halo(source, spread_ref, y_ref, members * channels * UP, per)
    cols = y_ref.shape[1]
    fresh = dot(w1_ref[...], y)
    for m in range(members):
        lanes = slice(m * cols, (m + 1) * cols)
        put_hidden(h1_ref, 0, lanes, silu_of_half(fresh[m * 256 : m * 256 + 128]))
        put_hidden(h1_ref, 1, lanes, silu_of_half(fresh[m * 256 + 128 : m * 256 + 256] + h_ref[:, lanes]))
    h2_ref[0:128, :] = silu_of_half(dot(w2_ref[:, 0:512], h1_ref[...]) + a_first[...]).astype(BF)
    h2_ref[128:256, :] = silu_of_half(dot(w2_ref[:, 0:256], h1_ref[256:512, :]) + a_second[...]).astype(BF)
    v = dot(w3_ref[...], h2_ref[...])
    second = []
    for m in range(members):
        lanes = slice(m * cols, (m + 1) * cols)
        pre_ref[m] = v[0:16, lanes] + shift_right(v[16:32, lanes])
        second.append(bottleneck(v[32:64, lanes] + v_ref[:, lanes]))
    put_line(second_ref, 0, dot(mix_ref[...], jnp.concatenate(second, axis=0)))


def chunk_kernel(nb, pre_ref, carry_ref, mix_ref, second_ref, tail_ref, keep_ref, send_ref, head_ref):
    members, _, cols = pre_ref.shape
    carry = carry_ref[...].astype(F32) * is_row(0)
    first = [
        silu_of_half(pre_ref[m] + carry[m * 16 : m * 16 + 16]).astype(BF) for m in range(members)
    ]
    put_line(head_ref, 0, dot(mix_ref[...], jnp.concatenate(first, axis=0)))

    me = lax.axis_index("mem")
    slots = lax.axis_size("mem") // 2
    tall = 64 + tail_ref.shape[0]

    def tile_at(base):
        at = pl.ds(pl.multiple_of(base, 128), 128)
        return jnp.concatenate([head_ref[:, at], second_ref[:, at], tail_ref[:, at]], axis=0)

    def lanes_from(lane):
        v = tile_at(lane // 128 * 128)
        return v if nb % 128 == 0 else pltpu.roll(v, (128 - lane % 128) % 128, 1)

    count = 4 * slots
    which = lax.broadcasted_iota(jnp.int32, (count, cols + 256), 0)
    lane = lax.broadcasted_iota(jnp.int32, (count, cols + 256), 1)
    block = me ^ (2 * (lax.rem(which, 2 * slots) // 2) + which // (2 * slots))
    edge = 128 + block * nb + jnp.where(lax.rem(which, 2) == 0, -1, nb)
    pick = jnp.where(lane == edge, 1.0, 0.0).astype(BF)
    whole = jnp.concatenate([head_ref[...], second_ref[...], tail_ref[...]], axis=0).astype(BF)
    turned = lax.dot_general(pick, whole, (((1,), (1,)), ((), ())), preferred_element_type=F32)
    for side, ref in enumerate((keep_ref, send_ref)):
        for k in range(slots):
            ref[k, 0:tall, :] = lanes_from(128 + (me ^ (2 * k + side)) * nb).astype(BF)
            at = 2 * (side * slots + k)
            ref[k, tall : tall + EDGES, :] = jnp.concatenate(
                [turned[at : at + 2], jnp.zeros((EDGES - 2, 128), F32)], axis=0
            ).astype(BF)


def pair_kernel(keep_ref, got_ref, own_ref, *out_refs):
    own_ref[...] = keep_ref[0].astype(F32) + got_ref[0].astype(F32)
    for k, ref in enumerate(out_refs):
        ref[...] = (keep_ref[k + 1].astype(F32) + got_ref[k + 1].astype(F32)).astype(BF)


def put_latent(ref, at, line):
    ext = line.shape[1]
    ref[at, 0:32, :] = pltpu.roll(line, 1, 1).astype(BF)
    ref[at, 32:64, :] = line.astype(BF)
    ref[at, 64:96, :] = pltpu.roll(line, ext - 1, 1).astype(BF)


def latent_kernel(nb, quarter, own_ref, *refs):
    line_ref, first_ref, second_ref = refs[-3:]
    total = own_ref[...]
    for ref in refs[:-3]:
        total = total + ref[...].astype(F32)
    latent = silu_of_half(0.5 * total)
    tall = quarter * 32
    turned = jnp.concatenate([latent[tall : tall + EDGES], jnp.zeros((128 - EDGES, 128), F32)], axis=0).T
    ext = line_ref.shape[1]
    lines = []
    for r in range(quarter):
        rows = slice(r * 32, (r + 1) * 32)
        line = [latent[rows, 0:nb], turned[rows, 1:2], jnp.zeros((32, ext - nb - 2), F32), turned[rows, 0:1]]
        lines.append(jnp.concatenate(line, axis=1))
        line_ref[rows, :] = lines[-1].astype(BF)
    first_ref[...] = lines[-1].astype(BF)
    second_ref[...] = lines[0].astype(BF)


def upsample_row(w1, l_ref, a, keep_even, keep_odd, rows, u_ref, wanted, keeps):
    wide = l_ref.shape[2]
    nb = u_ref.shape[1]
    v = silu_of_half(dot(w1, l_ref[a + 1 : a + 4].reshape(288, wide)))
    for pr in range(2):
        row = 2 * a + pr
        if row not in wanted:
            continue
        even = v[pr * 64 : pr * 64 + 32] * keep_even
        odd = v[pr * 64 + 32 : pr * 64 + 64] * keep_odd
        if row in keeps:
            even, odd = even * keeps[row], odd * keeps[row]
        at = (row + 1) * 128
        u_ref[at : at + 32, :] = pltpu.roll(odd, 1, 1)[:, 0:nb].astype(BF)
        u_ref[at + 32 : at + 64, :] = even[:, 0:nb].astype(BF)
        u_ref[at + 64 : at + 96, :] = odd[:, 0:nb].astype(BF)
        u_ref[at + 96 : at + 128, :] = pltpu.roll(even, wide - 1, 1)[:, 0:nb].astype(BF)


def column_keeps(nb, wide):
    mem_at, mem_last = lax.axis_index("mem"), lax.axis_size("mem") - 1
    lane = lax.broadcasted_iota(jnp.int32, (32, wide), 1)
    keep_odd = jnp.where((lane == wide - 1) & (mem_at == 0), 0.0, 1.0).astype(F32)
    keep_even = jnp.where((lane == nb) & (mem_at == mem_last), 0.0, 1.0).astype(F32)
    return keep_even, keep_odd


def field_rows(w2, u_ref, g_ref, which):
    nb = u_ref.shape[1]
    for n, a in enumerate(which):
        v = dot(w2, u_ref[a * 128 : (a + 3) * 128, :]).astype(BF)
        for pr in range(2):
            for ph in range(4):
                g_ref[(2 * n + pr) * 16 : (2 * n + pr + 1) * 16, ph * nb : (ph + 1) * nb] = v[
                    (pr * 4 + ph) * 16 : (pr * 4 + ph + 1) * 16
                ]


def level_first(rows, which):
    count = 32 * len(which)
    to = lax.broadcasted_iota(jnp.int32, (16 * rows, count), 0)
    frm = lax.broadcasted_iota(jnp.int32, (16 * rows, count), 1)
    level, row = to // rows, lax.rem(to, rows)
    hit = jnp.zeros(to.shape, jnp.bool_)
    for n, a in enumerate(which):
        for pr in range(2):
            hit = hit | ((row == 2 * a + pr) & (frm == (2 * n + pr) * 16 + level))
    return jnp.where(hit, 1.0, 0.0).astype(BF)


def split_rows(rows):
    inside = [a for a in range(2, 2 * rows - 2)]
    return inside, [a for a in range(2 * rows) if a not in inside]


def by_phase(v):
    return jnp.concatenate(
        [v[(pr * 4 + ph) * 16 : (pr * 4 + ph + 1) * 16] for ph in range(4) for pr in range(2)], axis=0
    )


def merge_phases(a, b):
    return jnp.concatenate([v[ph * 32 : ph * 32 + 32] for ph in range(4) for v in (a, b)], axis=0)


def decoder_inner(
    nb, line_ref, d1_ref, d2_ref,
    w_edge, w_field, up_part, field_part, join_ref, turn_ref, part_ref, wd1, wd2, l_ref, u_ref, g_ref,
):
    wd1[...] = jnp.zeros_like(wd1)
    wd2[...] = jnp.zeros_like(wd2)
    for pr, rr, tr in TRANSPOSED:
        for pc, cc, tc in TRANSPOSED:
            wd1[(pr * 2 + pc) * 32 : (pr * 2 + pc + 1) * 32, (rr * 3 + cc) * 32 : (rr * 3 + cc + 1) * 32] = (
                0.5 * d1_ref[tr * 4 + tc].astype(F32)
            ).astype(BF)
            for q in range(2):
                at = pr * 4 + 2 * q + pc
                to = rr * 4 + q + cc
                wd2[at * 16 : (at + 1) * 16, to * 32 : (to + 1) * 32] = d2_ref[tr * 4 + tc]
    rows, wide = line_ref.shape[0] // 32, line_ref.shape[1]
    frm = lax.broadcasted_iota(jnp.int32, join_ref.shape, 0)
    to = lax.broadcasted_iota(jnp.int32, join_ref.shape, 1)
    place = frm // nb
    join_ref[...] = jnp.where(to == 4 * (frm - nb * place) + place, 1.0, 0.0).astype(BF)
    inside, outside = split_rows(rows)
    turn_ref[...] = level_first(4 * rows, outside)

    l_ref[0] = jnp.zeros_like(l_ref[0])
    l_ref[1] = jnp.zeros_like(l_ref[0])
    for r in range(rows):
        put_latent(l_ref, r + 2, line_ref[r * 32 : r * 32 + 32, :].astype(F32))
    l_ref[rows + 2] = jnp.zeros_like(l_ref[0])
    u_ref[...] = jnp.zeros_like(u_ref)
    keep_even, keep_odd = column_keeps(nb, wide)
    for a in range(rows):
        upsample_row(wd1[...], l_ref, a, keep_even, keep_odd, rows, u_ref, range(1, 2 * rows - 1), {})
    field_rows(wd2[...], u_ref, g_ref, inside)
    g = dot(level_first(4 * rows, inside), g_ref[...]).astype(BF)
    part_ref[...] = dot(g, join_ref[...])

    w_edge[0, 0:64, :] = wd1[64:128, 96:192]
    w_edge[0, 64:128, :] = wd1[0:64, 0:96]
    w_edge[1, 0:64, :] = wd1[64:128, 192:288]
    w_edge[1, 64:128, :] = wd1[0:64, 96:192]
    up_part[0] = dot(w_edge[1], l_ref[2])
    up_part[1] = dot(w_edge[0], l_ref[rows + 1])

    def known(taps, first, count):
        return by_phase(dot(wd2[:, taps : taps + 128 * count], u_ref[(first + 1) * 128 : (first + 1 + count) * 128, :]))

    last = 2 * rows - 1
    field_part[0] = merge_phases(known(256, 1, 1), known(128, 1, 2))
    field_part[1] = merge_phases(known(0, last - 2, 2), known(0, last - 1, 1))
    none = jnp.zeros((128, 128), BF)
    w = [by_phase(wd2[:, rr * 128 : rr * 128 + 128]) for rr in range(3)]
    w_field[0] = merge_phases(jnp.concatenate([w[0], w[1]], axis=1), jnp.concatenate([none, w[0]], axis=1))
    w_field[1] = merge_phases(jnp.concatenate([w[2], none], axis=1), jnp.concatenate([w[1], w[2]], axis=1))


def decoder_kernel(
    nb, first_ref, second_ref, w_edge, w_field, up_part, field_part, join_ref, turn_ref, part_ref,
    out_ref, l_ref, u_ref, g_ref,
):
    odd_row = lax.rem(lax.axis_index("row"), 2) == 1
    keeps = is_row(0), is_row(lax.axis_size("row") - 1)
    wide = l_ref.shape[2]
    first, second = first_ref[...].astype(F32), second_ref[...].astype(F32)
    put_latent(l_ref, 0, first * keeps[0])
    put_latent(l_ref, 1, second * keeps[1])
    keep_even, keep_odd = column_keeps(nb, wide)
    for side in range(2):
        v = silu_of_half(dot(w_edge[side], l_ref[side]) + up_part[side])
        for line in range(2):
            even = v[line * 64 : line * 64 + 32] * keep_even
            odd = v[line * 64 + 32 : line * 64 + 64] * keep_odd
            if line == side:
                even, odd = even * keeps[side], odd * keeps[side]
            at = line * 128
            u_ref[side, at : at + 32, :] = pltpu.roll(odd, 1, 1)[:, 0:nb].astype(BF)
            u_ref[side, at + 32 : at + 64, :] = even[:, 0:nb].astype(BF)
            u_ref[side, at + 64 : at + 96, :] = odd[:, 0:nb].astype(BF)
            u_ref[side, at + 96 : at + 128, :] = pltpu.roll(even, wide - 1, 1)[:, 0:nb].astype(BF)
        v = (dot(w_field[side], u_ref[side]) + field_part[side]).astype(BF)
        for ph in range(4):
            g_ref[side * 64 : side * 64 + 64, ph * nb : (ph + 1) * nb] = v[ph * 64 : ph * 64 + 64]
    g = dot(g_ref[...], join_ref[...]).astype(BF)
    out_ref[...] = (dot(turn_ref[...], g) + part_ref[...]).astype(BF).reshape(out_ref.shape)


def shifted(value, by):
    peers = lax.axis_size("row")
    return lax.ppermute(value, "row", [(i, (i + by) % peers) for i in range(peers)])


def swapped(value, by):
    return lax.ppermute(value, "mem", [(i, i ^ by) for i in range(lax.axis_size("mem"))])


VMEM = pl.BlockSpec(memory_space=pltpu.VMEM)


def call(kernel, outs, scratch, *operands, mb=8, us=1):
    return pl.pallas_call(
        kernel,
        out_shape=[jax.ShapeDtypeStruct(*o) for o in outs],
        in_specs=[VMEM] * len(operands),
        out_specs=[VMEM] * len(outs),
        scratch_shapes=[pltpu.VMEM(*s) for s in scratch],
        compiler_params=pltpu.CompilerParams(vmem_limit_bytes=mb * 2**20),
        cost_estimate=pl.CostEstimate(flops=us * 10**9, bytes_accessed=us * 3 * 10**6, transcendentals=0),
    )(*operands)


def per_device(members, enc_first, enc_second, enc_third, mix_weight, dec_first, dec_second):
    count, channels, rows, wide = members.shape
    half, quarter = rows // 2, rows // 4
    cols = wide // 4
    peers, lines = lax.axis_size("mem"), lax.axis_size("row")
    nb = cols // peers
    lanes = 512
    chunks = wide // lanes
    x = members.reshape(count * channels * rows, wide)
    nd, nu = count * channels * UP, count * channels * DOWN
    per = padded(nd, 8), padded(nu, 8)
    total = padded(5 * per[0], 16), padded(5 * per[1], 16)
    pack = functools.partial(pack_kernel, count, channels, rows)
    sizes = [(nd * chunks, lanes), (nu * chunks, lanes)]
    spreads, own, above, below = call(
        functools.partial(prepare_kernel, count, channels, per),
        [
            ((2, 256, 256), BF),
            ((5, 2, 48, 5 * channels * 8), BF),
            ((count, 2, 2, 48, total[0]), BF),
            ((count, 2, 48, total[1]), BF),
        ],
        [],
        us=20,
    )
    down, up = call(pack, [(s, BF) for s in sizes], [(s, F32) for s in sizes], x, below, mb=16, us=20)
    up = shifted(up, -1)
    down = shifted(down, 1)

    w1 = enc_first.transpose(1, 2, 3, 0)
    w2 = enc_second.transpose(2, 3, 0, 1).reshape(9, 64, 64)
    w3 = enc_third.transpose(2, 3, 0, 1).reshape(9, 16, 64)
    wide_cols = count * cols
    row_f32 = ((128, wide_cols), F32)
    third_f32 = ((32, wide_cols), F32)
    (
        h1, h_first, h_last, a_last, a_first, a_second, v_second, v_third, h2_mid,
        w2_big, w3_big, w1_down, w1_up, mix,
    ) = call(
        functools.partial(inner_kernel, count, channels, rows),
        [((256 * (half - 1), wide_cols), BF)]
        + [row_f32] * 5
        + [third_f32] * 2
        + [
            ((128, wide_cols), BF),
            ((128, 768), BF),
            ((64, 256), BF),
            ((count * 256, total[0]), BF),
            ((count * 128, total[1]), BF),
            ((32, count * CH_BOT), BF),
        ],
        [
            ((48, 64), F32),
            ((640, 5 * channels * 8), BF),
            ((count, rows // 8, 5 * channels * 8, cols), F32),
            ((rows // 8, 640, cols), F32),
            ((256, wide_cols), BF),
        ],
        x, w1, w2, w3, mix_weight, spreads, own, above, below, mb=24,
    )
    h2_low, carry = call(
        functools.partial(low_kernel, count, channels, per[1]),
        [((128, wide_cols), BF), ((count * CH_BOT, cols), BF)],
        [((total[1], cols), F32), ((256, wide_cols), BF)],
        up, spreads, w1_up, h_last, w2_big, a_last, w3_big, mb=12,
    )
    carry = shifted(carry, 1)
    (mid,) = call(
        functools.partial(middle_kernel, count, half),
        [((quarter * 32 - 64, cols + 256), F32)],
        [((256, (half // 2 - 2) * wide_cols), BF)],
        h1, h2_mid, h2_low, w2_big, w3_big, v_third, mix, mb=12,
    )
    pre, second = call(
        functools.partial(top_kernel, count, channels, per[0]),
        [((count, CH_BOT, cols), F32), ((32, cols + 256), F32)],
        [((total[0], cols), F32), ((512, wide_cols), BF), ((256, wide_cols), BF)],
        down, spreads, w1_down, h_first, w2_big, a_first, a_second, w3_big, v_second, mix, mb=12,
    )
    slots = peers // 2
    chunk = (quarter * 32 + EDGES, 128)
    keep, send = call(
        functools.partial(chunk_kernel, nb),
        [((slots,) + chunk, BF)] * 2,
        [((32, cols + 256), F32)],
        pre, carry, mix, second, mid,
    )
    got = swapped(send, 1)
    mine, *others = call(pair_kernel, [(chunk, F32)] + [(chunk, BF)] * (slots - 1), [], keep, got)
    order = sorted(range(slots - 1), key=lambda k: (k == 0, k))
    moved = {k: swapped(others[k], 2 * (k + 1)) for k in order}
    ext = padded(nb + 2, 128)
    latent, first, second = call(
        functools.partial(latent_kernel, nb, quarter),
        [((quarter * 32, ext), BF), ((32, ext), BF), ((32, ext), BF)],
        [],
        mine, *[moved[k] for k in range(slots - 1)],
    )
    first = shifted(first, 1)
    second = shifted(second, -1)

    d1, d2, _ = lax.optimization_barrier((dec_first, dec_second, others[0]))
    d1 = d1.transpose(2, 3, 0, 1).reshape(16, 32, 32)
    d2 = d2.transpose(2, 3, 0, 1).reshape(16, 16, 32)
    inside, outside = split_rows(quarter)
    edge_parts = call(
        functools.partial(decoder_inner, nb),
        [
            ((2, 128, 96), BF),
            ((2, 256, 256), BF),
            ((2, 128, ext), F32),
            ((2, 256, nb), F32),
            ((4 * nb, 4 * nb), BF),
            ((16 * rows, 32 * len(outside)), BF),
            ((16 * rows, 4 * nb), F32),
        ],
        [
            ((128, 288), BF),
            ((128, 384), BF),
            ((quarter + 3, 96, ext), BF),
            ((128 * (half + 2), nb), BF),
            ((32 * len(inside), 4 * nb), BF),
        ],
        latent, d1, d2,
    )
    (out,) = call(
        functools.partial(decoder_kernel, nb),
        [((16, rows, 4 * nb), BF)],
        [((2, 96, ext), BF), ((2, 256, nb), BF), ((128, 4 * nb), BF)],
        first, second, *edge_parts,
    )
    return out


def solution(mesh):
    placed = (P("mem", None, "row", None), P(), P(), P(), P(), P(), P())
    return jax.shard_map(
        per_device, mesh=mesh, in_specs=placed, out_specs=P(None, "row", "mem"), check_vma=False
    )
```
